32 devices in a mesh: parts: 2 (over x), cell: 16 (over z, y, core).
Axes of the slice: x: 2, y: 2, z: 4, core: 2. Of those that a mesh axis runs over, the one named last changes fastest.
Arguments:
- vectors: bfloat16 [49152, 768], P(('parts', 'cell')), parts along dimension 0, may hold values from -12 to 12
- row_slot: int32 [2, 49152], P(None, ('parts', 'cell')), parts along dimension 1, may hold values from 0 to 31, as said below
- fine_codes: int32 [2, 49152], P(None, ('parts', 'cell')), parts along dimension 1, may hold values from 0 to 2047
- cell_list: int32 [2, 1024], P(None, ('parts', 'cell')), parts along dimension 1, may hold values from 0 to 511, as said below
- coarse_in: float32 [8192, 768], P('cell'), may hold values from -6 to 6
- fine_in: float32 [2048, 768], replicated, may hold values from -6 to 6
Outputs:
- coarse_out: float32 [16384, 768], P(('parts', 'cell')), parts along dimension 0
- fine_out: float32 [4096, 768], P(('parts', 'cell')), parts along dimension 0
The draws below stay inside these ranges and needn't reach their ends.
There are 2 independent parts, one for each index of `parts`. The reference program is written for one: setup_inputs(seed, part) draws one part's arguments, and reference() takes and returns one part's arrays. A program takes and returns all parts, laid end to end along the dimension named above; an argument that names none is the same for every part. Nothing has to cross between parts.
Inputs may be any that keep to these rules, and one draw needn't show every extreme that they name: In sweep 0, row_slot is nondecreasing over each device's 1536 vectors. `cell_list`: each run of 2 consecutive entries of a device's list is nondecreasing.
All inputs are finite; a program needn't handle non-finite values.
Results may differ from the reference program's by a relative error of at most 0.0028.
Values sent between devices are 32-bit elements; how exact they have to be, the bound alone decides.
No kernel may reach another device: no remote copies, remote signals or barrier semaphores. Data moves between devices by JAX's collectives and lax.ppermute only.
A program may use at most 128 MiB of HBM per device.

```python
import jax
import jax.numpy as jnp
from jax import lax

D = 768
M = 2048
KDEV = 512
SLOTS = 2
ROWS_DEV = 1536
K = 8192
LIST = 32
ROWS = 24576
ENTRIES = 512
N_CELL = 16


def shared_codes(key):
    keys = jax.random.split(key, 6)
    relabel = jax.random.permutation(keys[0], M).astype(jnp.int32)
    first_factor = jax.random.randint(keys[1], (ROWS,), 0, M)
    second_factor = jax.random.randint(keys[2], (ROWS,), 0, M)
    first_sweep = relabel[first_factor * second_factor // (M - 1)]
    third_factor = jax.random.randint(keys[3], (ROWS,), 0, M)
    fourth_factor = jax.random.randint(keys[4], (ROWS,), 0, M)
    redrawn = relabel[third_factor * fourth_factor // (M - 1)]
    change = jax.random.randint(keys[5], (ROWS,), 0, 4) == 0
    second = jnp.where(change, redrawn, first_sweep)
    both = jnp.stack([first_sweep, second]).astype(jnp.int32)
    both = both.at[:, 0].set(M - 1)
    both = both.at[:, 1].set(0)
    return both


def draw_fine_codes(key, part):
    return shared_codes(key)


def draw_vectors(key, part):
    code_rows = shared_codes(key)[0]
    key = jax.random.fold_in(key, 5)
    keys = jax.random.split(key, 2)
    centers = jax.random.normal(keys[0], (M, D), jnp.float32)
    noise_part = jax.random.normal(keys[1], (ROWS, D), jnp.float32)
    values = jnp.clip(centers[code_rows] + noise_part, -12.0, 12.0)
    return values.astype(jnp.bfloat16)


def draw_row_slot(key, part):
    key = jax.random.fold_in(key, 7)
    keys = jax.random.split(key, 3)
    groups = ROWS // ROWS_DEV
    sorted_slots = jnp.sort(jax.random.randint(keys[0], (groups, ROWS_DEV), 0, LIST), axis=-1)
    sorted_slots = sorted_slots.at[:, 0].set(0)
    sorted_slots = sorted_slots.at[:, -1].set(LIST - 1)
    first_sweep = sorted_slots.reshape(ROWS)
    redrawn = jax.random.randint(keys[1], (ROWS,), 0, LIST)
    change = jax.random.randint(keys[2], (ROWS,), 0, 4) == 0
    second = jnp.where(change, redrawn, first_sweep)
    return jnp.stack([first_sweep, second]).astype(jnp.int32)


def draw_cell_list(key, part):
    key = jax.random.fold_in(key, 11)
    keys = jax.random.split(key, 3)
    runs = ENTRIES // SLOTS
    first_sweep = jnp.sort(jax.random.randint(keys[0], (runs, SLOTS), 0, KDEV), axis=-1)
    redrawn = jax.random.randint(keys[1], (runs, SLOTS), 0, KDEV)
    change = jax.random.randint(keys[2], (runs, SLOTS), 0, 4) == 0
    second = jnp.sort(jnp.where(change, redrawn, first_sweep), axis=-1)
    both = jnp.stack([first_sweep, second])
    both = both.at[:, 0, 0].set(0)
    both = both.at[:, -1, -1].set(KDEV - 1)
    return both.reshape(2, ENTRIES).astype(jnp.int32)


def levels(key, shape, cuts, smallest, largest):
    gain, own = 1.0, jax.random.fold_in(key, 6)
    for axis_at, shards_of in cuts:
        heights = jnp.exp(jax.random.uniform(jax.random.fold_in(own, axis_at), (shards_of,), jnp.float32, smallest / len(cuts), largest / len(cuts)))
        gain = gain * jnp.repeat(heights, shape[axis_at] // shards_of).reshape([-1 if axis == axis_at else 1 for axis in range(len(shape))])
    return gain


def noise(own_key, dims, scale, bound, cuts=(), held_as=jnp.bfloat16):
    entries = jax.random.normal(own_key, dims, jnp.float32) * scale
    if len(cuts) > 0:
        entries = levels(own_key, dims, cuts, -0.22, 0.18) * entries
    return jnp.clip(entries, min=-bound, max=bound).astype(held_as)


def setup_inputs(seed: int = 0, part: int = 0) -> dict:
    key_list = jax.random.split(jax.random.key(seed), 7)
    own_keys = jax.random.split(jax.random.fold_in(key_list[6], part), 7)
    vectors = draw_vectors(jax.random.fold_in(jax.random.fold_in(key_list[6], part), 71), part)
    row_slot = draw_row_slot(jax.random.fold_in(jax.random.fold_in(key_list[6], part), 71), part)
    fine_codes = draw_fine_codes(jax.random.fold_in(jax.random.fold_in(key_list[6], part), 71), part)
    cell_list = draw_cell_list(jax.random.fold_in(jax.random.fold_in(key_list[6], part), 71), part)
    coarse_in = noise(key_list[4], (K, D), 1.0, 6.0, ((0, 16),), jnp.float32)
    fine_in = noise(key_list[5], (M, D), 1.0, 6.0, (), jnp.float32)
    return {"vectors": vectors, "row_slot": row_slot, "fine_codes": fine_codes, "cell_list": cell_list, "coarse_in": coarse_in, "fine_in": fine_in}


def rounded(values):
    return lax.optimization_barrier(values.astype(jnp.bfloat16)).astype(jnp.float32)


def reference(vectors, row_slot, fine_codes, cell_list, coarse_in, fine_in):
    owner_base = (jnp.arange(LIST, dtype=jnp.int32) // SLOTS) * KDEV
    device_of = jnp.arange(ROWS, dtype=jnp.int32) // ROWS_DEV
    as_float = vectors.astype(jnp.float32)
    coarse = coarse_in
    fine_book = fine_in
    for sweep in range(2):
        cell_table = cell_list[sweep].reshape(N_CELL, LIST) + owner_base[None, :]
        coarse_code = cell_table[device_of, row_slot[sweep]].astype(jnp.int32)
        residual = rounded(as_float - fine_book[fine_codes[sweep]])
        coarse_sums = jax.ops.segment_sum(residual, coarse_code, num_segments=K)
        coarse_counts = jax.ops.segment_sum(jnp.ones((ROWS,), jnp.float32), coarse_code, num_segments=K)
        coarse = jnp.where(coarse_counts[:, None] > 0, coarse_sums / jnp.maximum(coarse_counts, 1.0)[:, None], coarse)
        fine_residual = rounded(as_float - coarse[coarse_code])
        fine_sums = jax.ops.segment_sum(fine_residual, fine_codes[sweep], num_segments=M)
        fine_counts = jax.ops.segment_sum(jnp.ones((ROWS,), jnp.float32), fine_codes[sweep], num_segments=M)
        fine_book = jnp.where(fine_counts[:, None] > 0, fine_sums / jnp.maximum(fine_counts, 1.0)[:, None], fine_book)
    return coarse, fine_book
```

```python
import jax
import jax.numpy as jnp
from jax import lax
from jax.sharding import PartitionSpec as P


def code_tally(code_rows, codewords):
    return jax.ops.segment_sum(
        jnp.ones(code_rows.shape, jnp.float32), code_rows, num_segments=codewords
    )


def fine_update(code_term, totals_share, old_share, share_rows):
    part_sums = lax.psum_scatter(
        code_term(jnp.int32(0), lax.axis_size("cell") * share_rows),
        "cell",
        scatter_dimension=0,
        tiled=True,
    )
    return jnp.where(
        totals_share[:, None] > 0, part_sums / jnp.maximum(totals_share, 1.0)[:, None], old_share
    )


def routed_plan(vectors, row_slot, fine_codes, cell_list, coarse_in, fine_in):
    groups = lax.axis_size("cell")
    rows_here, feature = vectors.shape
    listed = cell_list.shape[1]
    slot_count = listed // groups
    owner_cells = coarse_in.shape[0]
    codewords = fine_in.shape[0]
    share_rows = codewords // groups
    share_start = lax.axis_index("cell") * share_rows
    fine_book = fine_in
    fine_share = lax.dynamic_slice_in_dim(fine_in, share_start, share_rows, 0)
    coarse = coarse_in
    list_iota = lax.iota(jnp.int32, listed)
    for sweep in range(2):
        code_totals = lax.psum(code_tally(fine_codes[sweep], codewords), "cell")
        slot_rows = row_slot[sweep]
        code_rows = fine_codes[sweep]
        picked = jnp.take(fine_book, code_rows, axis=0)
        residual = (vectors.astype(jnp.float32) - picked).astype(jnp.bfloat16)
        slot_hot = (slot_rows[None, :] == list_iota[:, None]).astype(jnp.bfloat16)
        slot_sums = jnp.dot(slot_hot, residual, preferred_element_type=jnp.float32)
        slot_counts = jnp.sum(slot_hot, axis=1, dtype=jnp.float32)
        slot_cells = cell_list[sweep].astype(jnp.float32)
        got_sums, got_counts, got_cells = (
            lax.all_to_all(
                slot_sums.reshape(groups, slot_count, feature),
                "cell",
                split_axis=0,
                concat_axis=0,
                tiled=True,
            ),
            lax.all_to_all(
                slot_counts.reshape(groups, slot_count),
                "cell",
                split_axis=0,
                concat_axis=0,
                tiled=True,
            ),
            lax.all_to_all(
                slot_cells.reshape(groups, slot_count),
                "cell",
                split_axis=0,
                concat_axis=0,
                tiled=True,
            ),
        )
        flat_cells = got_cells.reshape(groups * slot_count).astype(jnp.int32)
        cell_sums = jax.ops.segment_sum(
            got_sums.reshape(groups * slot_count, feature), flat_cells, num_segments=owner_cells
        )
        cell_counts = jax.ops.segment_sum(
            got_counts.reshape(groups * slot_count), flat_cells, num_segments=owner_cells
        )
        coarse = jnp.where(
            cell_counts[:, None] > 0, cell_sums / jnp.maximum(cell_counts, 1.0)[:, None], coarse
        )
        returned_rows = jnp.take(coarse, flat_cells, axis=0).reshape(groups, slot_count, feature)
        arrived = lax.all_to_all(returned_rows, "cell", split_axis=0, concat_axis=0, tiled=True)
        entry_centers = arrived.reshape(listed, feature)
        row_centers = jnp.take(entry_centers, slot_rows, axis=0)
        fine_residual = (vectors.astype(jnp.float32) - row_centers).astype(jnp.bfloat16)

        def code_term(start, count, code_rows=code_rows, fine_residual=fine_residual):
            wanted = start + lax.iota(jnp.int32, count)
            code_hot = (code_rows[None, :] == wanted[:, None]).astype(jnp.bfloat16)
            return jnp.dot(code_hot, fine_residual, preferred_element_type=jnp.float32)

        totals_share = lax.dynamic_slice_in_dim(code_totals, share_start, share_rows, 0)
        if sweep == 0:
            full_sums = lax.psum(code_term(0, codewords), "cell")
            fine_book = jnp.where(
                code_totals[:, None] > 0,
                full_sums / jnp.maximum(code_totals, 1.0)[:, None],
                fine_book,
            )
            fine_share = lax.dynamic_slice_in_dim(fine_book, share_start, share_rows, 0)
        else:
            fine_share = fine_update(code_term, totals_share, fine_share, share_rows)
    return (coarse, fine_share)

HIGH = lax.Precision.HIGHEST


def exact_dot(left, right):
    return jnp.dot(left, right, precision=HIGH, preferred_element_type=jnp.float32)


def hot(codes, count):
    return (codes[..., None, :] == lax.iota(jnp.int32, count)[:, None]).astype(jnp.bfloat16)


def pair_counts(codes, slots, codewords, listed):
    groups = codes.shape[0]
    low = 256
    high = codewords // low
    left = hot((codes // low) * listed + slots, high * listed)
    right = hot(codes % low, low)
    tables = lax.dot_general(
        left, right, (((2,), (2,)), ((0,), (0,))), preferred_element_type=jnp.float32
    )
    tables = tables.reshape(groups, high, listed, low)
    return tables.transpose(0, 2, 1, 3).reshape(groups * listed, codewords)


def dense_plan(vectors, row_slot, fine_codes, cell_list, coarse_in, fine_in):
    groups = lax.axis_size("cell")
    me = lax.axis_index("cell")
    rows_here, feature = vectors.shape
    listed = cell_list.shape[1]
    slot_count = listed // groups
    owner_cells = coarse_in.shape[0]
    codewords = fine_in.shape[0]
    share_rows = codewords // groups
    share_start = me * share_rows
    entries = groups * listed

    codes = jnp.concatenate([fine_codes, row_slot], axis=1)
    codes = jnp.concatenate([codes, cell_list], axis=1)
    gathered = lax.all_gather(codes.reshape(-1), "cell").reshape(groups, 2, -1)
    all_fine = gathered[:, :, :rows_here]
    all_slot = gathered[:, :, rows_here : 2 * rows_here]
    all_cell = gathered[:, :, 2 * rows_here :]

    own_hot = [hot(row_slot[t], listed) for t in range(2)]
    code_hot = [hot(fine_codes[t], codewords) for t in range(2)]
    own_sums = [
        jnp.dot(own_hot[t], vectors, preferred_element_type=jnp.float32) for t in range(2)
    ]
    fine_sums = [
        jnp.dot(code_hot[t], vectors, preferred_element_type=jnp.float32) for t in range(2)
    ]
    own_pairs = pair_counts(fine_codes[0][None], row_slot[0][None], codewords, listed)
    first_sums = lax.all_gather(
        own_sums[0] - exact_dot(own_pairs, fine_in), "cell", tiled=True
    )

    pairs = [
        pair_counts(all_fine[:, t], all_slot[:, t], codewords, listed) for t in range(2)
    ]
    code_totals = [jnp.sum(pairs[t], axis=0) for t in range(2)]
    entry_totals = [jnp.sum(pairs[t], axis=1) for t in range(2)]
    owner_of = (lax.iota(jnp.int32, entries) % listed) // slot_count
    cell_of = [
        all_cell[:, t].reshape(entries) + owner_of * owner_cells for t in range(2)
    ]
    same = [(cell_of[t][:, None] == cell_of[t][None, :]).astype(jnp.float32) for t in range(2)]
    cell_totals = [exact_dot(same[t], entry_totals[t][:, None]) for t in range(2)]

    kept_sums = jnp.where(code_totals[1][:, None] > 0, fine_sums[1], fine_sums[0])
    share_sums = lax.psum_scatter(kept_sums, "cell", scatter_dimension=0, tiled=True)

    fine_here = jnp.where(
        (lax.iota(jnp.int32, codewords) // share_rows == me) & (code_totals[0] == 0), 1.0, 0.0
    )
    fine_terms = jnp.where(fine_here[:, None] > 0, fine_in, fine_sums[0])
    weights = pairs[1] / jnp.maximum(code_totals[0], 1.0)[None, :]
    bracket = -exact_dot(weights, fine_terms)
    bracket = bracket + jnp.where(
        (lax.iota(jnp.int32, entries) // listed == me)[:, None],
        jnp.tile(own_sums[1], (groups, 1)),
        0.0,
    )
    bracket = bracket.reshape(groups, groups, slot_count, feature).transpose(1, 0, 2, 3)
    bracket = lax.psum_scatter(
        bracket.reshape(entries, feature), "cell", scatter_dimension=0, tiled=True
    )

    first_centers = exact_dot(same[0], first_sums) / jnp.maximum(cell_totals[0], 1.0)

    def owned(table):
        parts = table.reshape(groups, groups, slot_count, *table.shape[1:])
        return lax.dynamic_index_in_dim(parts, me, 1, keepdims=False).reshape(
            listed, *table.shape[1:]
        )

    mixing = exact_dot(owned(weights), pairs[0].T)
    second_sums = bracket + exact_dot(mixing, first_centers)
    own_cells = [owned(all_cell[:, t].reshape(entries)) for t in range(2)]
    own_totals = [owned(entry_totals[t]) for t in range(2)]
    own_same = (own_cells[1][:, None] == own_cells[1][None, :]).astype(jnp.float32)
    own_centers = exact_dot(own_same, second_sums) / jnp.maximum(
        exact_dot(own_same, own_totals[1][:, None]), 1.0
    )
    second_centers = lax.all_gather(own_centers, "cell")
    second_centers = (
        second_centers.reshape(groups, groups, slot_count, feature)
        .transpose(1, 0, 2, 3)
        .reshape(entries, feature)
    )

    coarse = coarse_in
    for t, sums in enumerate((owned(first_sums), second_sums)):
        picks = hot(own_cells[t], owner_cells).astype(jnp.float32)
        counts = exact_dot(picks, own_totals[t][:, None])
        coarse = jnp.where(counts > 0, exact_dot(picks, sums) / jnp.maximum(counts, 1.0), coarse)

    def share(table, axis):
        return lax.dynamic_slice_in_dim(table, share_start, share_rows, axis)

    counts = [share(code_totals[t], 0)[:, None] for t in range(2)]
    away = [
        exact_dot(share(pairs[t], 1).T, centers)
        for t, centers in enumerate((first_centers, second_centers))
    ]
    fine = jnp.where(counts[0] > 0, (share_sums - away[0]) / jnp.maximum(counts[0], 1.0), share(fine_in, 0))
    fine = jnp.where(counts[1] > 0, (share_sums - away[1]) / jnp.maximum(counts[1], 1.0), fine)
    return (coarse, fine)


def per_device(vectors, row_slot, fine_codes, cell_list, coarse_in, fine_in):
    entries = lax.axis_size("cell") * cell_list.shape[1]
    plan = dense_plan if entries <= fine_in.shape[1] else routed_plan
    return plan(vectors, row_slot, fine_codes, cell_list, coarse_in, fine_in)


def solution(mesh):
    return jax.shard_map(
        per_device,
        mesh=mesh,
        in_specs=(
            P(("parts", "cell"), None),
            P(None, ("parts", "cell")),
            P(None, ("parts", "cell")),
            P(None, ("parts", "cell")),
            P("cell", None),
            P(),
        ),
        out_specs=(P(("parts", "cell"), None), P(("parts", "cell"), None)),
        check_vma=False,
    )
```

```python
import jax
import jax.numpy as jnp
from jax import lax
from jax.experimental import pallas as pl
from jax.experimental.pallas import tpu as pltpu
from jax.sharding import PartitionSpec as P


def code_tally(code_rows, codewords):
    return jax.ops.segment_sum(
        jnp.ones(code_rows.shape, jnp.float32), code_rows, num_segments=codewords
    )


def fine_update(code_term, totals_share, old_share, share_rows):
    part_sums = lax.psum_scatter(
        code_term(jnp.int32(0), lax.axis_size("cell") * share_rows),
        "cell",
        scatter_dimension=0,
        tiled=True,
    )
    return jnp.where(
        totals_share[:, None] > 0, part_sums / jnp.maximum(totals_share, 1.0)[:, None], old_share
    )


def routed_plan(vectors, row_slot, fine_codes, cell_list, coarse_in, fine_in):
    groups = lax.axis_size("cell")
    rows_here, feature = vectors.shape
    listed = cell_list.shape[1]
    slot_count = listed // groups
    owner_cells = coarse_in.shape[0]
    codewords = fine_in.shape[0]
    share_rows = codewords // groups
    share_start = lax.axis_index("cell") * share_rows
    fine_book = fine_in
    fine_share = lax.dynamic_slice_in_dim(fine_in, share_start, share_rows, 0)
    coarse = coarse_in
    list_iota = lax.iota(jnp.int32, listed)
    for sweep in range(2):
        code_totals = lax.psum(code_tally(fine_codes[sweep], codewords), "cell")
        slot_rows = row_slot[sweep]
        code_rows = fine_codes[sweep]
        picked = jnp.take(fine_book, code_rows, axis=0)
        residual = (vectors.astype(jnp.float32) - picked).astype(jnp.bfloat16)
        slot_hot = (slot_rows[None, :] == list_iota[:, None]).astype(jnp.bfloat16)
        slot_sums = jnp.dot(slot_hot, residual, preferred_element_type=jnp.float32)
        slot_counts = jnp.sum(slot_hot, axis=1, dtype=jnp.float32)
        slot_cells = cell_list[sweep].astype(jnp.float32)
        got_sums, got_counts, got_cells = (
            lax.all_to_all(
                slot_sums.reshape(groups, slot_count, feature),
                "cell",
                split_axis=0,
                concat_axis=0,
                tiled=True,
            ),
            lax.all_to_all(
                slot_counts.reshape(groups, slot_count),
                "cell",
                split_axis=0,
                concat_axis=0,
                tiled=True,
            ),
            lax.all_to_all(
                slot_cells.reshape(groups, slot_count),
                "cell",
                split_axis=0,
                concat_axis=0,
                tiled=True,
            ),
        )
        flat_cells = got_cells.reshape(groups * slot_count).astype(jnp.int32)
        cell_sums = jax.ops.segment_sum(
            got_sums.reshape(groups * slot_count, feature), flat_cells, num_segments=owner_cells
        )
        cell_counts = jax.ops.segment_sum(
            got_counts.reshape(groups * slot_count), flat_cells, num_segments=owner_cells
        )
        coarse = jnp.where(
            cell_counts[:, None] > 0, cell_sums / jnp.maximum(cell_counts, 1.0)[:, None], coarse
        )
        returned_rows = jnp.take(coarse, flat_cells, axis=0).reshape(groups, slot_count, feature)
        arrived = lax.all_to_all(returned_rows, "cell", split_axis=0, concat_axis=0, tiled=True)
        entry_centers = arrived.reshape(listed, feature)
        row_centers = jnp.take(entry_centers, slot_rows, axis=0)
        fine_residual = (vectors.astype(jnp.float32) - row_centers).astype(jnp.bfloat16)

        def code_term(start, count, code_rows=code_rows, fine_residual=fine_residual):
            wanted = start + lax.iota(jnp.int32, count)
            code_hot = (code_rows[None, :] == wanted[:, None]).astype(jnp.bfloat16)
            return jnp.dot(code_hot, fine_residual, preferred_element_type=jnp.float32)

        totals_share = lax.dynamic_slice_in_dim(code_totals, share_start, share_rows, 0)
        if sweep == 0:
            full_sums = lax.psum(code_term(0, codewords), "cell")
            fine_book = jnp.where(
                code_totals[:, None] > 0,
                full_sums / jnp.maximum(code_totals, 1.0)[:, None],
                fine_book,
            )
            fine_share = lax.dynamic_slice_in_dim(fine_book, share_start, share_rows, 0)
        else:
            fine_share = fine_update(code_term, totals_share, fine_share, share_rows)
    return (coarse, fine_share)


F32 = jnp.float32
BF16 = jnp.bfloat16
LOW = 256
LANES = 128
PARAMS = pltpu.CompilerParams(vmem_limit_bytes=56 * 2**20)
VMEM = pl.BlockSpec(memory_space=pltpu.VMEM)
SMEM = pl.BlockSpec(memory_space=pltpu.SMEM)


def iota(shape, axis):
    return lax.broadcasted_iota(jnp.int32, shape, axis)


def matmul(left, right):
    return jnp.dot(left, right, preferred_element_type=F32)


def matmul_nt(left, right):
    return lax.dot_general(left, right, (((1,), (1,)), ((), ())), preferred_element_type=F32)


def split(values):
    high = values.astype(BF16)
    return high, (values - high.astype(F32)).astype(BF16)


def hot_rows(codes, rows=LOW):
    inside = jnp.where((codes >= 0) & (codes < rows), codes, -1)
    inside = inside.astype(F32).astype(BF16)
    row = iota((rows, codes.shape[1]), 0).astype(F32).astype(BF16)
    return jnp.where(row == inside, jnp.ones((), BF16), jnp.zeros((), BF16))


def pair_block(codes, slots, listed, high):
    left = hot_rows((codes >> 8) * listed + slots, high * listed)
    return matmul_nt(left, hot_rows(codes & (LOW - 1)))


def own_kernel(listed, vectors, fine_codes, row_slot, fine_in, first_ref, second_ref, sums_ref):
    codewords = fine_in.shape[0]
    high = codewords // LOW
    first = matmul(hot_rows(row_slot[0:1, :], listed), vectors[...])
    second_ref[...] = matmul(hot_rows(row_slot[1:2, :], listed), vectors[...])
    codes = fine_codes[0:1, :]
    pairs = pair_block(codes, row_slot[0:1, :], listed, high)
    for digit in range(high):
        pairs_high, pairs_low = split(pairs[digit * listed : (digit + 1) * listed])
        both = jnp.concatenate([pairs_high, pairs_low], axis=0)
        book = fine_in[digit * LOW : (digit + 1) * LOW, :]
        book_high, book_low = split(book)
        taken = matmul(both, book_high) + matmul(both, book_low)
        first = first - taken[:listed] - taken[listed:]
    first_ref[...] = first

    def block(at, carry):
        start = pl.multiple_of(at * 2 * LOW, 2 * LOW)
        hot = jnp.concatenate(
            [hot_rows(codes - start), hot_rows(codes - start - LOW)], axis=0
        )
        sums_ref[pl.ds(start, 2 * LOW), :] = matmul(hot, vectors[...])
        return carry

    lax.fori_loop(0, codewords // (2 * LOW), block, 0)


def tables_kernel(
    groups,
    slot_count,
    me_ref,
    codes_ref,
    sums_ref,
    first_ref,
    second_ref,
    share_ref,
    fine_ref,
    bracket_ref,
    pairs_ref,
    centers_ref,
    code_info_ref,
    entry_info_ref,
    passes_ref,
    table0,
    table1,
    cell0,
    cell1,
    wide,
    terms,
    permuted,
):
    me = me_ref[0]
    codewords, feature = sums_ref.shape
    listed = groups * slot_count
    entries = groups * listed
    high = codewords // LOW
    half = codes_ref.shape[2] - LANES
    share_rows = share_ref.shape[0]

    def device_tables(device, carry):
        at = device ^ me
        for sweep, table in enumerate((table0, table1)):
            block = jnp.zeros((high * listed, LOW), F32)
            for part in range(2):
                row = 2 * sweep + part
                block = block + pair_block(
                    codes_ref[at, row : row + 1, :half],
                    codes_ref[at, row + 4 : row + 5, :half],
                    listed,
                    high,
                )
            rows = pl.ds(pl.multiple_of(device * listed, listed), listed)
            for digit in range(high):
                table[rows, digit * LOW : (digit + 1) * LOW] = block[
                    digit * listed : (digit + 1) * listed
                ]
        return carry

    lax.fori_loop(0, groups, device_tables, 0)
    for device in range(groups):
        at = device ^ me
        for sweep, cell in enumerate((cell0, cell1)):
            row = codes_ref[at, sweep : sweep + 1, half : half + listed]
            cell[device * slot_count : (device + 1) * slot_count, :] = jnp.broadcast_to(
                row, (slot_count, listed)
            )

    row_at = iota((entries, listed), 0)
    owner_of = row_at // listed
    slot_of = owner_of * slot_count + row_at % slot_count
    is_slot = slot_of == iota((entries, listed), 1)
    device_of = (row_at // slot_count) % groups

    def entry_cells(cell):
        tiled = jnp.concatenate([cell[...]] * groups, axis=0)
        picked = jnp.sum(jnp.where(is_slot, tiled, 0), axis=1, keepdims=True)
        return picked.astype(F32)

    owner_col = owner_of[:, :1].astype(F32)
    cells = [entry_cells(cell0), entry_cells(cell1)]
    names = [cell + owner_col * 4096.0 for cell in cells]

    entry_row = iota((entries, entries), 0)
    natural = (
        ((entry_row // slot_count) % groups) * listed
        + (entry_row // listed) * slot_count
        + entry_row % slot_count
    )
    order = (natural == iota((entries, entries), 1)).astype(BF16)
    passes = jnp.where(
        jnp.maximum(jnp.max(table0[...]), jnp.max(table1[...])) > LOW, 2, 1
    ).astype(jnp.int32)
    passes_ref[0] = passes
    code_counts = [jnp.sum(table[...], axis=0, keepdims=True) for table in (table0, table1)]
    entry_counts = []
    for table in (table0, table1):
        count_high, count_low = split(
            jnp.broadcast_to(jnp.sum(table[...], axis=1, keepdims=True), (entries, LANES))
        )
        entry_counts.append(matmul(order, count_high) + matmul(order, count_low))
    for digit in range(high):
        columns = slice(digit * LOW, (digit + 1) * LOW)
        table_high, table_low = split(table1[:, columns])
        permuted[0, :, columns] = matmul(order, table_high).astype(BF16)
        permuted[1, :, columns] = matmul(order, table_low).astype(BF16)

    own_row = codes_ref[0, 0:1, half : half + listed].astype(F32)
    own_row = own_row + (iota((1, listed), 1) // slot_count).astype(F32) * 4096.0
    match = (names[0] == own_row).astype(BF16)
    match = lax.dot_general(match, order, (((0,), (0,)), ((), ())), preferred_element_type=F32)
    match = match.astype(BF16)
    for digit in range(high):
        columns = slice(digit * LOW, (digit + 1) * LOW)
        table_high, table_low = split(table0[:, columns])
        used = matmul(match, table_high) + matmul(match, table_low)
        used_high, used_low = split(used)
        wide[0:listed, columns] = used_high.astype(F32)
        wide[listed : 2 * listed, columns] = used_low.astype(F32)
    held = wide[0:listed, :] + wide[listed : 2 * listed, :]
    held = jnp.sum(held, axis=1, keepdims=True)
    wide[2 * listed : 2 * listed + 8, :] = jnp.broadcast_to(code_counts[0], (8, codewords))
    wide[2 * listed + 8 : 2 * listed + 16, :] = jnp.broadcast_to(code_counts[1], (8, codewords))
    wide[2 * listed + 16 :, :] = jnp.zeros((LANES - 2 * listed - 16, codewords), F32)
    center_high, center_low = split(first_ref[...] / jnp.maximum(held, 1.0))
    center_high = jnp.concatenate(
        [center_high, center_high, jnp.zeros((LANES - 2 * listed, feature), BF16)], axis=0
    )
    center_low = jnp.concatenate(
        [center_low, center_low, jnp.zeros((LANES - 2 * listed, feature), BF16)], axis=0
    )
    for digit in range(high):
        rows = slice(digit * LOW, (digit + 1) * LOW)
        columns = wide[:, rows].T
        code_info_ref[rows, :] = columns
        columns_high = columns.astype(BF16)
        columns_high = jnp.where(
            iota((LOW, LANES), 1) < 2 * listed, columns_high.astype(F32), 0.0
        ).astype(BF16)
        fine = sums_ref[rows, :] - (
            matmul(columns_high, center_high) + matmul(columns_high, center_low)
        )
        fine_ref[rows, :] = fine
        scaled = fine / jnp.maximum(columns[:, 2 * listed : 2 * listed + 1], 1.0)
        terms[0, rows, :], terms[1, rows, :] = split(scaled)
    mine = pl.ds(pl.multiple_of(me * share_rows, share_rows), share_rows)
    empty = code_info_ref[mine, 2 * listed : 2 * listed + 1] == 0
    share_high, share_low = split(share_ref[...])
    terms[0, mine, :] = jnp.where(
        empty, share_high.astype(F32), terms[0, mine, :].astype(F32)
    ).astype(BF16)
    terms[1, mine, :] = jnp.where(
        empty, share_low.astype(F32), terms[1, mine, :].astype(F32)
    ).astype(BF16)

    own_entry = (is_slot & (device_of == me)).astype(BF16)
    second_high, second_low = split(second_ref[...])
    bracket_ref[...] = (
        matmul(own_entry, second_high)
        + matmul(own_entry, second_low)
        - matmul(permuted[0], terms[0])
        - matmul(permuted[0], terms[1])
    )

    @pl.when(passes > 1)
    def _():
        bracket_ref[...] -= matmul(permuted[1], terms[0])

    same = (
        jnp.broadcast_to(names[1], (entries, entries))
        == jnp.broadcast_to(names[1], (entries, LANES)).T[0:1, :]
    ).astype(BF16)
    total_high, total_low = split(entry_counts[1])
    totals = matmul(same, total_high) + matmul(same, total_low)
    bracket_high, bracket_low = split(bracket_ref[...])
    centers = matmul(same, bracket_high) + matmul(same, bracket_low)
    centers = centers / jnp.maximum(totals[:, :1], 1.0)
    centers_ref[0], centers_ref[1] = split(centers)

    eye = (iota((LOW, LOW), 0) == iota((LOW, LOW), 1)).astype(BF16)
    for digit in range(high):
        rows = slice(digit * LOW, (digit + 1) * LOW)
        for part in range(2):
            pairs_ref[part, rows, :] = matmul_nt(eye, permuted[part, :, rows]).astype(BF16)
    lane = iota((entries, LANES), 1)
    info = jnp.where(lane == 0, entry_counts[0], entry_counts[1])
    info = jnp.where(lane == 2, cells[0], info)
    entry_info_ref[...] = jnp.where(lane == 3, cells[1], info)


def last_kernel(
    blocks,
    cuts,
    listed,
    me_ref,
    passes_ref,
    vectors,
    fine_codes,
    pairs_ref,
    centers_ref,
    fine_ref,
    code_info_ref,
    bracket_ref,
    *refs,
):
    outs, left = refs[:-1], refs[-1]
    me = me_ref[0]
    rows_here = vectors.shape[0]
    entries = centers_ref.shape[1]
    cell_rows = listed
    share_rows = outs[0].shape[1] - cell_rows
    codes = fine_codes[1:2, :]
    for at, block in enumerate(blocks):
        owner = me ^ block
        rows = pl.ds(pl.multiple_of(owner * share_rows, share_rows), share_rows)
        to = slice(at * share_rows, (at + 1) * share_rows)
        left[to, :rows_here] = hot_rows(codes - owner * share_rows, share_rows)
        left[to, rows_here : rows_here + entries] = -pairs_ref[0, rows, :]
    start = 0
    for cut, out in zip(cuts, outs):
        columns = slice(start, start + cut)
        start += cut
        sums = (
            matmul(left[:, :rows_here], vectors[:, columns])
            + matmul(left[:, rows_here:], centers_ref[0, :, columns])
            + matmul(left[:, rows_here:], centers_ref[1, :, columns])
        )
        for at, block in enumerate(blocks):
            owner = me ^ block
            rows = pl.ds(pl.multiple_of(owner * share_rows, share_rows), share_rows)
            used = code_info_ref[rows, 2 * listed + 8 : 2 * listed + 9] > 0
            out[at, :share_rows, :] = jnp.where(
                used, sums[at * share_rows : (at + 1) * share_rows], fine_ref[rows, columns]
            )
            cells = pl.ds(pl.multiple_of(owner * cell_rows, cell_rows), cell_rows)
            out[at, share_rows:, :] = bracket_ref[cells, columns]

            @pl.when(passes_ref[0] > 1)
            def _():
                more = matmul(pairs_ref[1, rows, :], centers_ref[0, :, columns])
                out[at, :share_rows, :] = jnp.where(
                    used, out[at, :share_rows, :] - more, out[at, :share_rows, :]
                )


def final_kernel(
    share_rows,
    coarse_in,
    fine_share,
    first_sums,
    last_sums,
    code_info,
    entry_info,
    coarse_out,
    fine_out,
):
    listed = first_sums.shape[0]
    owner_cells, feature = coarse_in.shape
    by_lane = entry_info[...].T
    info = [by_lane[at : at + 1, :] for at in range(4)]
    coarse = coarse_in[...]
    for sweep, sums in enumerate((first_sums[...], last_sums[share_rows:, :])):
        cell = info[2 + sweep].astype(jnp.int32)
        hit = iota((owner_cells, listed), 0) == cell
        counts = jnp.sum(jnp.where(hit, info[sweep], 0.0), axis=1, keepdims=True)
        picks = hit.astype(BF16)
        sums_high, sums_low = split(sums)
        found = matmul(picks, sums_high) + matmul(picks, sums_low)
        coarse = jnp.where(counts > 0, found / jnp.maximum(counts, 1.0), coarse)
    coarse_out[...] = coarse
    first_count = code_info[:, 2 * listed : 2 * listed + 1]
    last_count = code_info[:, 2 * listed + 8 : 2 * listed + 9]
    count = jnp.where(last_count > 0, last_count, first_count)
    fine_out[...] = jnp.where(
        count > 0, last_sums[:share_rows, :] / jnp.maximum(count, 1.0), fine_share[...]
    )


def exchange(values, step):
    groups = lax.axis_size("cell")
    return lax.ppermute(values, "cell", [(at, at ^ step) for at in range(groups)])


def gather_relative(values):
    groups = lax.axis_size("cell")
    far = groups // 4
    blocks = [values] + [exchange(values, 4 * step) for step in range(1, far)]
    near = jnp.stack(blocks)
    near = jnp.stack([near, exchange(near, 2)])
    both = jnp.stack([near, exchange(near, 1)])
    return both


def dense_plan(vectors, row_slot, fine_codes, cell_list, coarse_in, fine_in):
    groups = lax.axis_size("cell")
    me = lax.axis_index("cell")
    rows_here, feature = vectors.shape
    listed = cell_list.shape[1]
    slot_count = listed // groups
    codewords = fine_in.shape[0]
    share_rows = codewords // groups
    entries = groups * listed
    half = rows_here // 2
    me_arr = me.reshape(1).astype(jnp.int32)

    codes = jnp.concatenate([fine_codes.reshape(4, half), row_slot.reshape(4, half)], axis=0)
    cells = jnp.pad(cell_list, ((0, 6), (0, LANES - listed)))
    packed = jnp.concatenate([codes, cells], axis=1)
    gathered = gather_relative(packed)
    gathered = gathered.reshape(2, 2, groups // 4, 8, half + LANES)
    gathered = gathered.transpose(2, 1, 0, 3, 4).reshape(groups, 8, half + LANES)

    first, second, sums = pl.pallas_call(
        lambda *refs: own_kernel(listed, *refs),
        out_shape=(
            jax.ShapeDtypeStruct((listed, feature), F32),
            jax.ShapeDtypeStruct((listed, feature), F32),
            jax.ShapeDtypeStruct((codewords, feature), F32),
        ),
        in_specs=[VMEM] * 4,
        out_specs=[VMEM] * 3,
        compiler_params=PARAMS,
        cost_estimate=pl.CostEstimate(flops=6 * 10**9, bytes_accessed=15 * 10**6, transcendentals=0),
        name="own_sums",
    )(vectors, fine_codes, row_slot, fine_in)
    first_own = lax.all_to_all(
        first.reshape(groups, slot_count, feature), "cell", split_axis=0, concat_axis=0, tiled=True
    ).reshape(listed, feature)

    fine_share = lax.dynamic_slice_in_dim(fine_in, me * share_rows, share_rows, 0)
    fine, bracket, pairs, centers, code_info, entry_info, passes = pl.pallas_call(
        lambda *refs: tables_kernel(groups, slot_count, *refs),
        out_shape=(
            jax.ShapeDtypeStruct((codewords, feature), F32),
            jax.ShapeDtypeStruct((entries, feature), F32),
            jax.ShapeDtypeStruct((2, codewords, entries), BF16),
            jax.ShapeDtypeStruct((2, entries, feature), BF16),
            jax.ShapeDtypeStruct((codewords, LANES), F32),
            jax.ShapeDtypeStruct((entries, LANES), F32),
            jax.ShapeDtypeStruct((1,), jnp.int32),
        ),
        in_specs=[SMEM] + [VMEM] * 5,
        out_specs=[VMEM] * 6 + [SMEM],
        scratch_shapes=[
            pltpu.VMEM((entries, codewords), F32),
            pltpu.VMEM((entries, codewords), F32),
            pltpu.VMEM((listed, listed), jnp.int32),
            pltpu.VMEM((listed, listed), jnp.int32),
            pltpu.VMEM((LANES, codewords), F32),
            pltpu.VMEM((2, codewords, feature), BF16),
            pltpu.VMEM((2, entries, codewords), BF16),
        ],
        compiler_params=PARAMS,
        cost_estimate=pl.CostEstimate(flops=20 * 10**9, bytes_accessed=20 * 10**6, transcendentals=0),
        name="tables",
    )(me_arr, gathered, sums, first, second, fine_share)

    cuts = (2 * feature // 3, feature // 3)

    def last_terms(blocks):
        return pl.pallas_call(
            lambda *refs: last_kernel(blocks, cuts, listed, *refs),
            out_shape=tuple(
                jax.ShapeDtypeStruct((len(blocks), share_rows + listed, cut), F32) for cut in cuts
            ),
            in_specs=[SMEM] * 2 + [VMEM] * 7,
            out_specs=[VMEM] * len(cuts),
            scratch_shapes=[pltpu.VMEM((len(blocks) * share_rows, rows_here + entries), BF16)],
            compiler_params=PARAMS,
            cost_estimate=pl.CostEstimate(
                flops=4 * 10**8 * len(blocks), bytes_accessed=20 * 10**6, transcendentals=0
            ),
            name="last_sums",
        )(me_arr, passes, vectors, fine_codes, pairs, centers, fine, code_info, bracket)

    far = groups // 4
    away = last_terms([4 * z + 2 * y + 1 for y in (1, 0) for z in range(far)])
    near = last_terms([4 * z + 2 * y for y in (1, 0) for z in range(far)])
    total = []
    for column in range(2):
        got = exchange(away[column], 1)
        sums_here = near[column] + got
        other, kept = sums_here[:far], sums_here[far:]
        if column == 0:
            kept = kept + exchange(other, 2)
            pieces = [kept[0]] + [exchange(kept[z], 4 * z) for z in range(1, far)]
            total.append(sum(pieces[1:], pieces[0]))
        else:
            pairs_z = jnp.stack([other, kept], axis=1)
            pieces = [pairs_z[0]] + [exchange(pairs_z[z], 4 * z) for z in range(1, far)]
            summed = sum(pieces[1:], pieces[0])
            total.append(summed[1] + exchange(summed[0], 2))
    last_sums = jnp.concatenate(total, axis=1)

    own_code = lax.dynamic_slice_in_dim(code_info, me * share_rows, share_rows, 0)
    own_entry = lax.dynamic_slice_in_dim(entry_info, me * listed, listed, 0)
    return pl.pallas_call(
        lambda *refs: final_kernel(share_rows, *refs),
        out_shape=(
            jax.ShapeDtypeStruct(coarse_in.shape, F32),
            jax.ShapeDtypeStruct((share_rows, feature), F32),
        ),
        in_specs=[VMEM] * 6,
        out_specs=[VMEM] * 2,
        compiler_params=PARAMS,
        name="outputs",
    )(coarse_in, fine_share, first_own, last_sums, own_code, own_entry)


def fits_dense(mesh_groups, listed, codewords, rows_here):
    entries = mesh_groups * listed
    power = mesh_groups & (mesh_groups - 1) == 0 and mesh_groups >= 4
    digits = codewords % (2 * LOW) == 0 and (codewords // LOW) * listed <= LOW
    return power and digits and entries * codewords <= 2**20 and rows_here % (2 * LANES) == 0


def per_device(vectors, row_slot, fine_codes, cell_list, coarse_in, fine_in):
    groups = lax.axis_size("cell")
    dense = fits_dense(groups, cell_list.shape[1], fine_in.shape[0], vectors.shape[0])
    plan = dense_plan if dense else routed_plan
    return plan(vectors, row_slot, fine_codes, cell_list, coarse_in, fine_in)


def solution(mesh):
    return jax.shard_map(
        per_device,
        mesh=mesh,
        in_specs=(
            P(("parts", "cell"), None),
            P(None, ("parts", "cell")),
            P(None, ("parts", "cell")),
            P(None, ("parts", "cell")),
            P("cell", None),
            P(),
        ),
        out_specs=(P(("parts", "cell"), None), P(("parts", "cell"), None)),
        check_vma=False,
    )
```

```python
import jax
import jax.numpy as jnp
from jax import lax
from jax.experimental import pallas as pl
from jax.experimental.pallas import tpu as pltpu
from jax.sharding import PartitionSpec as P


def code_tally(code_rows, codewords):
    return jax.ops.segment_sum(
        jnp.ones(code_rows.shape, jnp.float32), code_rows, num_segments=codewords
    )


def fine_update(code_term, totals_share, old_share, share_rows):
    part_sums = lax.psum_scatter(
        code_term(jnp.int32(0), lax.axis_size("cell") * share_rows),
        "cell",
        scatter_dimension=0,
        tiled=True,
    )
    return jnp.where(
        totals_share[:, None] > 0, part_sums / jnp.maximum(totals_share, 1.0)[:, None], old_share
    )


def routed_plan(vectors, row_slot, fine_codes, cell_list, coarse_in, fine_in):
    groups = lax.axis_size("cell")
    rows_here, feature = vectors.shape
    listed = cell_list.shape[1]
    slot_count = listed // groups
    owner_cells = coarse_in.shape[0]
    codewords = fine_in.shape[0]
    share_rows = codewords // groups
    share_start = lax.axis_index("cell") * share_rows
    fine_book = fine_in
    fine_share = lax.dynamic_slice_in_dim(fine_in, share_start, share_rows, 0)
    coarse = coarse_in
    list_iota = lax.iota(jnp.int32, listed)
    for sweep in range(2):
        code_totals = lax.psum(code_tally(fine_codes[sweep], codewords), "cell")
        slot_rows = row_slot[sweep]
        code_rows = fine_codes[sweep]
        picked = jnp.take(fine_book, code_rows, axis=0)
        residual = (vectors.astype(jnp.float32) - picked).astype(jnp.bfloat16)
        slot_hot = (slot_rows[None, :] == list_iota[:, None]).astype(jnp.bfloat16)
        slot_sums = jnp.dot(slot_hot, residual, preferred_element_type=jnp.float32)
        slot_counts = jnp.sum(slot_hot, axis=1, dtype=jnp.float32)
        slot_cells = cell_list[sweep].astype(jnp.float32)
        got_sums, got_counts, got_cells = (
            lax.all_to_all(
                slot_sums.reshape(groups, slot_count, feature),
                "cell",
                split_axis=0,
                concat_axis=0,
                tiled=True,
            ),
            lax.all_to_all(
                slot_counts.reshape(groups, slot_count),
                "cell",
                split_axis=0,
                concat_axis=0,
                tiled=True,
            ),
            lax.all_to_all(
                slot_cells.reshape(groups, slot_count),
                "cell",
                split_axis=0,
                concat_axis=0,
                tiled=True,
            ),
        )
        flat_cells = got_cells.reshape(groups * slot_count).astype(jnp.int32)
        cell_sums = jax.ops.segment_sum(
            got_sums.reshape(groups * slot_count, feature), flat_cells, num_segments=owner_cells
        )
        cell_counts = jax.ops.segment_sum(
            got_counts.reshape(groups * slot_count), flat_cells, num_segments=owner_cells
        )
        coarse = jnp.where(
            cell_counts[:, None] > 0, cell_sums / jnp.maximum(cell_counts, 1.0)[:, None], coarse
        )
        returned_rows = jnp.take(coarse, flat_cells, axis=0).reshape(groups, slot_count, feature)
        arrived = lax.all_to_all(returned_rows, "cell", split_axis=0, concat_axis=0, tiled=True)
        entry_centers = arrived.reshape(listed, feature)
        row_centers = jnp.take(entry_centers, slot_rows, axis=0)
        fine_residual = (vectors.astype(jnp.float32) - row_centers).astype(jnp.bfloat16)

        def code_term(start, count, code_rows=code_rows, fine_residual=fine_residual):
            wanted = start + lax.iota(jnp.int32, count)
            code_hot = (code_rows[None, :] == wanted[:, None]).astype(jnp.bfloat16)
            return jnp.dot(code_hot, fine_residual, preferred_element_type=jnp.float32)

        totals_share = lax.dynamic_slice_in_dim(code_totals, share_start, share_rows, 0)
        if sweep == 0:
            full_sums = lax.psum(code_term(0, codewords), "cell")
            fine_book = jnp.where(
                code_totals[:, None] > 0,
                full_sums / jnp.maximum(code_totals, 1.0)[:, None],
                fine_book,
            )
            fine_share = lax.dynamic_slice_in_dim(fine_book, share_start, share_rows, 0)
        else:
            fine_share = fine_update(code_term, totals_share, fine_share, share_rows)
    return (coarse, fine_share)


F32 = jnp.float32
BF16 = jnp.bfloat16
LOW = 256
LANES = 128
PARAMS = pltpu.CompilerParams(vmem_limit_bytes=56 * 2**20)
VMEM = pl.BlockSpec(memory_space=pltpu.VMEM)
SMEM = pl.BlockSpec(memory_space=pltpu.SMEM)


def iota(shape, axis):
    return lax.broadcasted_iota(jnp.int32, shape, axis)


def matmul(left, right):
    return jnp.dot(left, right, preferred_element_type=F32)


def matmul_nt(left, right):
    return lax.dot_general(left, right, (((1,), (1,)), ((), ())), preferred_element_type=F32)


def split(values):
    high = values.astype(BF16)
    return high, (values - high.astype(F32)).astype(BF16)


def hot_rows(codes, rows=LOW):
    inside = jnp.where((codes >= 0) & (codes < rows), codes, -1)
    inside = inside.astype(F32).astype(BF16)
    row = iota((rows, codes.shape[1]), 0).astype(F32).astype(BF16)
    return jnp.where(row == inside, jnp.ones((), BF16), jnp.zeros((), BF16))


def pair_block(codes, slots, listed, high):
    left = hot_rows((codes >> 8) * listed + slots, high * listed)
    return matmul_nt(left, hot_rows(codes & (LOW - 1)))


def own_kernel(listed, vectors, fine_codes, row_slot, fine_in, first_ref, second_ref, sums_ref):
    codewords = fine_in.shape[0]
    high = codewords // LOW
    first = matmul(hot_rows(row_slot[0:1, :], listed), vectors[...])
    second_ref[...] = matmul(hot_rows(row_slot[1:2, :], listed), vectors[...])
    codes = fine_codes[0:1, :]
    pairs = pair_block(codes, row_slot[0:1, :], listed, high)
    for digit in range(high):
        pairs_high, pairs_low = split(pairs[digit * listed : (digit + 1) * listed])
        both = jnp.concatenate([pairs_high, pairs_low], axis=0)
        book = fine_in[digit * LOW : (digit + 1) * LOW, :]
        book_high, book_low = split(book)
        taken = matmul(both, book_high) + matmul(both, book_low)
        first = first - taken[:listed] - taken[listed:]
    first_ref[...] = first

    def block(at, carry):
        start = pl.multiple_of(at * 2 * LOW, 2 * LOW)
        hot = jnp.concatenate(
            [hot_rows(codes - start), hot_rows(codes - start - LOW)], axis=0
        )
        sums_ref[pl.ds(start, 2 * LOW), :] = matmul(hot, vectors[...])
        return carry

    lax.fori_loop(0, codewords // (2 * LOW), block, 0)


def tables_kernel(
    groups,
    slot_count,
    owner_cells,
    me_ref,
    codes_ref,
    sums_ref,
    first_ref,
    second_ref,
    share_ref,
    fine_ref,
    bracket_ref,
    pairs_ref,
    rest_ref,
    centers_ref,
    code_info_ref,
    entry_info_ref,
    passes_ref,
    table0,
    table1,
    cell0,
    cell1,
    wide,
    terms,
    permuted,
):
    me = me_ref[0]
    codewords, feature = sums_ref.shape
    listed = groups * slot_count
    entries = groups * listed
    high = codewords // LOW
    half = codes_ref.shape[2] - LANES
    share_rows = share_ref.shape[0]

    def device_tables(device, carry):
        at = device
        for sweep, table in enumerate((table0, table1)):
            block = jnp.zeros((high * listed, LOW), F32)
            for part in range(2):
                row = 2 * sweep + part
                block = block + pair_block(
                    codes_ref[at, row : row + 1, :half],
                    codes_ref[at, row + 4 : row + 5, :half],
                    listed,
                    high,
                )
            rows = pl.ds(pl.multiple_of(device * listed, listed), listed)
            for digit in range(high):
                table[rows, digit * LOW : (digit + 1) * LOW] = block[
                    digit * listed : (digit + 1) * listed
                ]
        return carry

    lax.fori_loop(0, groups, device_tables, 0)
    for device in range(groups):
        at = device
        for sweep, cell in enumerate((cell0, cell1)):
            row = codes_ref[at, sweep : sweep + 1, half : half + listed]
            cell[device * slot_count : (device + 1) * slot_count, :] = jnp.broadcast_to(
                row, (slot_count, listed)
            )

    row_at = iota((entries, listed), 0)
    owner_of = row_at // listed
    slot_of = owner_of * slot_count + row_at % slot_count
    is_slot = slot_of == iota((entries, listed), 1)
    device_of = (row_at // slot_count) % groups

    def entry_cells(cell):
        tiled = jnp.concatenate([cell[...]] * groups, axis=0)
        picked = jnp.sum(jnp.where(is_slot, tiled, 0), axis=1, keepdims=True)
        return picked.astype(F32)

    owner_col = owner_of[:, :1].astype(F32)
    cells = [entry_cells(cell0), entry_cells(cell1)]
    names = [cell + owner_col * float(owner_cells) for cell in cells]

    entry_row = iota((entries, entries), 0)
    natural = (
        ((entry_row // slot_count) % groups) * listed
        + (entry_row // listed) * slot_count
        + entry_row % slot_count
    )
    order = (natural == iota((entries, entries), 1)).astype(BF16)
    passes = jnp.where(
        jnp.maximum(jnp.max(table0[...]), jnp.max(table1[...])) > LOW, 2, 1
    ).astype(jnp.int32)
    passes_ref[0] = passes
    code_counts = [jnp.sum(table[...], axis=0, keepdims=True) for table in (table0, table1)]
    entry_counts = []
    for table in (table0, table1):
        count_high, count_low = split(
            jnp.broadcast_to(jnp.sum(table[...], axis=1, keepdims=True), (entries, LANES))
        )
        entry_counts.append(matmul(order, count_high) + matmul(order, count_low))
    for digit in range(high):
        columns = slice(digit * LOW, (digit + 1) * LOW)
        table_high, table_low = split(table1[:, columns])
        permuted[0, :, columns] = matmul(order, table_high).astype(BF16)
        permuted[1, :, columns] = matmul(order, table_low).astype(BF16)

    own_row = codes_ref[me, 0:1, half : half + listed].astype(F32)
    own_row = own_row + (iota((1, listed), 1) // slot_count).astype(F32) * float(owner_cells)
    match = (names[0] == own_row).astype(BF16)
    match = lax.dot_general(match, order, (((0,), (0,)), ((), ())), preferred_element_type=F32)
    match = match.astype(BF16)
    for digit in range(high):
        columns = slice(digit * LOW, (digit + 1) * LOW)
        table_high, table_low = split(table0[:, columns])
        used = matmul(match, table_high) + matmul(match, table_low)
        used_high, used_low = split(used)
        wide[0:listed, columns] = used_high.astype(F32)
        wide[listed : 2 * listed, columns] = used_low.astype(F32)
    held = wide[0:listed, :] + wide[listed : 2 * listed, :]
    held = jnp.sum(held, axis=1, keepdims=True)
    wide[2 * listed : 2 * listed + 8, :] = jnp.broadcast_to(code_counts[0], (8, codewords))
    wide[2 * listed + 8 : 2 * listed + 16, :] = jnp.broadcast_to(code_counts[1], (8, codewords))
    wide[2 * listed + 16 :, :] = jnp.zeros((LANES - 2 * listed - 16, codewords), F32)
    center_high, center_low = split(first_ref[...] / jnp.maximum(held, 1.0))
    center_high = jnp.concatenate(
        [center_high, center_high, jnp.zeros((LANES - 2 * listed, feature), BF16)], axis=0
    )
    center_low = jnp.concatenate(
        [center_low, center_low, jnp.zeros((LANES - 2 * listed, feature), BF16)], axis=0
    )
    for digit in range(high):
        rows = slice(digit * LOW, (digit + 1) * LOW)
        columns = wide[:, rows].T
        code_info_ref[rows, :] = columns
        columns_high = columns.astype(BF16)
        columns_high = jnp.where(
            iota((LOW, LANES), 1) < 2 * listed, columns_high.astype(F32), 0.0
        ).astype(BF16)
        fine = sums_ref[rows, :] - (
            matmul(columns_high, center_high) + matmul(columns_high, center_low)
        )
        fine_ref[rows, :] = jnp.where(
            columns[:, 2 * listed + 8 : 2 * listed + 9] > 0, 0.0, fine
        )
        scaled = fine / jnp.maximum(columns[:, 2 * listed : 2 * listed + 1], 1.0)
        terms[0, rows, :], terms[1, rows, :] = split(scaled)
    mine = pl.ds(pl.multiple_of(me * share_rows, share_rows), share_rows)
    empty = code_info_ref[mine, 2 * listed : 2 * listed + 1] == 0
    share_high, share_low = split(share_ref[...])
    terms[0, mine, :] = jnp.where(
        empty, share_high.astype(F32), terms[0, mine, :].astype(F32)
    ).astype(BF16)
    terms[1, mine, :] = jnp.where(
        empty, share_low.astype(F32), terms[1, mine, :].astype(F32)
    ).astype(BF16)

    own_entry = (is_slot & (device_of == me)).astype(BF16)
    second_high, second_low = split(second_ref[...])
    bracket_ref[...] = (
        matmul(own_entry, second_high)
        + matmul(own_entry, second_low)
        - matmul(permuted[0], terms[0])
        - matmul(permuted[0], terms[1])
    )

    @pl.when(passes > 1)
    def _():
        bracket_ref[...] -= matmul(permuted[1], terms[0])

    same = (
        jnp.broadcast_to(names[1], (entries, entries))
        == jnp.broadcast_to(names[1], (entries, LANES)).T[0:1, :]
    ).astype(BF16)
    total_high, total_low = split(entry_counts[1])
    totals = matmul(same, total_high) + matmul(same, total_low)
    bracket_high, bracket_low = split(bracket_ref[...])
    centers = matmul(same, bracket_high) + matmul(same, bracket_low)
    centers = centers / jnp.maximum(totals[:, :1], 1.0)
    centers_ref[0], centers_ref[1] = split(centers)

    eye = (iota((LOW, LOW), 0) == iota((LOW, LOW), 1)).astype(BF16)
    for digit in range(high):
        rows = slice(digit * LOW, (digit + 1) * LOW)
        pairs_ref[rows, :] = matmul_nt(eye, permuted[0, :, rows]).astype(BF16)
        rest_ref[rows, :] = matmul_nt(eye, permuted[1, :, rows]).astype(BF16)
    lane = iota((entries, LANES), 1)
    info = jnp.where(lane == 0, entry_counts[0], entry_counts[1])
    info = jnp.where(lane == 2, cells[0], info)
    entry_info_ref[...] = jnp.where(lane == 3, cells[1], info)


def last_kernel(
    orders,
    listed,
    me_ref,
    passes_ref,
    vectors,
    fine_codes,
    pairs_ref,
    rest_ref,
    centers_ref,
    fine_ref,
    bracket_ref,
    _,
    *refs,
):
    outs, left, rest, sem = refs[:-3], refs[-3], refs[-2], refs[-1]
    me = me_ref[0]
    rows_here = vectors.shape[0]
    share_rows = outs[0].shape[1] - listed
    codes = fine_codes[1:2, :]
    for order, out in zip(orders, outs):
        for at, block in enumerate(order):
            owner = me ^ block
            rows = pl.ds(pl.multiple_of(owner * share_rows, share_rows), share_rows)
            to = slice(at * share_rows, (at + 1) * share_rows)
            left[to, :rows_here] = hot_rows(codes - owner * share_rows, share_rows)
            left[to, rows_here:] = -pairs_ref[rows, :]
        used = slice(0, len(order) * share_rows)
        sums = (
            matmul(left[used, :rows_here], vectors[...])
            + matmul(left[used, rows_here:], centers_ref[0])
            + matmul(left[used, rows_here:], centers_ref[1])
        )
        for at, block in enumerate(order):
            owner = me ^ block
            rows = pl.ds(pl.multiple_of(owner * share_rows, share_rows), share_rows)
            out[at, :share_rows, :] = (
                sums[at * share_rows : (at + 1) * share_rows] + fine_ref[rows, :]
            )
            cells = pl.ds(pl.multiple_of(owner * listed, listed), listed)
            out[at, share_rows:, :] = bracket_ref[cells, :]

    @pl.when(passes_ref[0] > 1)
    def _():
        copy = pltpu.make_async_copy(rest_ref, rest, sem)
        copy.start()
        copy.wait()
        for order, out in zip(orders, outs):
            for at, block in enumerate(order):
                owner = me ^ block
                rows = pl.ds(pl.multiple_of(owner * share_rows, share_rows), share_rows)
                out[at, :share_rows, :] -= matmul(rest[rows, :], centers_ref[0])


def final_kernel(
    share_rows,
    coarse_in,
    fine_share,
    first_sums,
    last_sums,
    code_info,
    entry_info,
    coarse_out,
    fine_out,
):
    listed = first_sums.shape[0]
    owner_cells, feature = coarse_in.shape
    by_lane = entry_info[...].T
    info = [by_lane[at : at + 1, :] for at in range(4)]
    coarse = coarse_in[...]
    for sweep, sums in enumerate((first_sums[...], last_sums[share_rows:, :])):
        cell = info[2 + sweep].astype(jnp.int32)
        hit = iota((owner_cells, listed), 0) == cell
        counts = jnp.sum(jnp.where(hit, info[sweep], 0.0), axis=1, keepdims=True)
        picks = hit.astype(BF16)
        sums_high, sums_low = split(sums)
        found = matmul(picks, sums_high) + matmul(picks, sums_low)
        coarse = jnp.where(counts > 0, found / jnp.maximum(counts, 1.0), coarse)
    coarse_out[...] = coarse
    first_count = code_info[:, 2 * listed : 2 * listed + 1]
    last_count = code_info[:, 2 * listed + 8 : 2 * listed + 9]
    count = jnp.where(last_count > 0, last_count, first_count)
    fine_out[...] = jnp.where(
        count > 0, last_sums[:share_rows, :] / jnp.maximum(count, 1.0), fine_share[...]
    )


def exchange(values, step):
    groups = lax.axis_size("cell")
    return lax.ppermute(values, "cell", [(at, at ^ step) for at in range(groups)])


def block_orders(bits):
    order = [0]
    for bit in bits[::-1]:
        order = [block + (1 << bit) for block in order] + order
    half = len(order) // 2
    return [block + 1 for block in order], order[:half], order[half:]


def scatter_sums(away, other, kept, bits):
    got = exchange(away, 1)
    other, kept = other + got[: other.shape[0]], kept + got[other.shape[0] :]
    for bit in bits[:-1]:
        got = exchange(other, 1 << bit)
        half = got.shape[0] // 2
        other, kept = kept[:half] + got[:half], kept[half:] + got[half:]
    return (kept + exchange(other, 1 << bits[-1]))[0]


def dense_plan(vectors, row_slot, fine_codes, cell_list, coarse_in, fine_in):
    groups = lax.axis_size("cell")
    me = lax.axis_index("cell")
    rows_here, feature = vectors.shape
    listed = cell_list.shape[1]
    slot_count = listed // groups
    codewords = fine_in.shape[0]
    share_rows = codewords // groups
    entries = groups * listed
    half = rows_here // 2
    me_arr = me.reshape(1).astype(jnp.int32)

    codes = jnp.concatenate([fine_codes.reshape(4, half), row_slot.reshape(4, half)], axis=0)
    cells = jnp.pad(cell_list, ((0, 6), (0, LANES - listed)))
    packed = jnp.concatenate([codes, cells], axis=1)
    gathered = lax.all_to_all(
        jnp.broadcast_to(packed[None], (groups, *packed.shape)),
        "cell",
        split_axis=0,
        concat_axis=0,
        tiled=True,
    )

    first, second, sums = pl.pallas_call(
        lambda *refs: own_kernel(listed, *refs),
        out_shape=(
            jax.ShapeDtypeStruct((listed, feature), F32),
            jax.ShapeDtypeStruct((listed, feature), F32),
            jax.ShapeDtypeStruct((codewords, feature), F32),
        ),
        in_specs=[VMEM] * 4,
        out_specs=[VMEM] * 3,
        compiler_params=PARAMS,
        cost_estimate=pl.CostEstimate(flops=6 * 10**9, bytes_accessed=15 * 10**6, transcendentals=0),
        name="own_sums",
    )(vectors, fine_codes, row_slot, fine_in)
    first_own = lax.all_to_all(
        first.reshape(groups, slot_count, feature), "cell", split_axis=0, concat_axis=0, tiled=True
    ).reshape(listed, feature)

    fine_share = lax.dynamic_slice_in_dim(fine_in, me * share_rows, share_rows, 0)
    fine, bracket, pairs, rest, centers, code_info, entry_info, passes = pl.pallas_call(
        lambda *refs: tables_kernel(groups, slot_count, coarse_in.shape[0], *refs),
        out_shape=(
            jax.ShapeDtypeStruct((codewords, feature), F32),
            jax.ShapeDtypeStruct((entries, feature), F32),
            jax.ShapeDtypeStruct((codewords, entries), BF16),
            jax.ShapeDtypeStruct((codewords, entries), BF16),
            jax.ShapeDtypeStruct((2, entries, feature), BF16),
            jax.ShapeDtypeStruct((codewords, LANES), F32),
            jax.ShapeDtypeStruct((entries, LANES), F32),
            jax.ShapeDtypeStruct((1,), jnp.int32),
        ),
        in_specs=[SMEM] + [VMEM] * 5,
        out_specs=[VMEM] * 7 + [SMEM],
        scratch_shapes=[
            pltpu.VMEM((entries, codewords), F32),
            pltpu.VMEM((entries, codewords), F32),
            pltpu.VMEM((listed, listed), jnp.int32),
            pltpu.VMEM((listed, listed), jnp.int32),
            pltpu.VMEM((LANES, codewords), F32),
            pltpu.VMEM((2, codewords, feature), BF16),
            pltpu.VMEM((2, entries, codewords), BF16),
        ],
        compiler_params=PARAMS,
        cost_estimate=pl.CostEstimate(flops=20 * 10**9, bytes_accessed=20 * 10**6, transcendentals=0),
        name="tables",
    )(me_arr, gathered, sums, first, second, fine_share)

    cut = feature // 3
    top = groups.bit_length() - 1
    near_first = list(range(1, top))
    far_first = near_first[1:] + near_first[:1]
    total = []
    for at, bits in enumerate((near_first, far_first, near_first)):
        orders = block_orders(bits)
        away, other, kept = pl.pallas_call(
            lambda *refs: last_kernel(orders, listed, *refs),
            grid=(1,),
            out_shape=tuple(
                jax.ShapeDtypeStruct((len(order), share_rows + listed, cut), F32)
                for order in orders
            ),
            in_specs=[
                SMEM,
                SMEM,
                pl.BlockSpec((rows_here, cut), lambda step, at=at: (0, at)),
                VMEM,
                VMEM,
                pl.BlockSpec(memory_space=pl.ANY),
                pl.BlockSpec((2, entries, cut), lambda step, at=at: (0, 0, at)),
                pl.BlockSpec((codewords, cut), lambda step, at=at: (0, at)),
                pl.BlockSpec((entries, cut), lambda step, at=at: (0, at)),
                pl.BlockSpec(memory_space=pl.ANY),
            ],
            out_specs=[VMEM] * len(orders),
            scratch_shapes=[
                pltpu.VMEM((len(orders[0]) * share_rows, rows_here + entries), BF16),
                pltpu.VMEM((codewords, entries), BF16),
                pltpu.SemaphoreType.DMA,
            ],
            compiler_params=PARAMS,
            cost_estimate=pl.CostEstimate(
                flops=27 * 10**8, bytes_accessed=8 * 10**6, transcendentals=0
            ),
            name="last_sums",
        )(me_arr, passes, vectors, fine_codes, pairs, rest, centers, fine, bracket, first_own)
        total.append(scatter_sums(away, other, kept, bits))
    last_sums = jnp.concatenate(total, axis=1)

    own_code = lax.dynamic_slice_in_dim(code_info, me * share_rows, share_rows, 0)
    own_entry = lax.dynamic_slice_in_dim(entry_info, me * listed, listed, 0)
    return pl.pallas_call(
        lambda *refs: final_kernel(share_rows, *refs),
        out_shape=(
            jax.ShapeDtypeStruct(coarse_in.shape, F32),
            jax.ShapeDtypeStruct((share_rows, feature), F32),
        ),
        in_specs=[VMEM] * 6,
        out_specs=[VMEM] * 2,
        compiler_params=PARAMS,
        name="outputs",
    )(coarse_in, fine_share, first_own, last_sums, own_code, own_entry)


def fits_dense(mesh_groups, listed, codewords, rows_here):
    entries = mesh_groups * listed
    power = mesh_groups & (mesh_groups - 1) == 0 and mesh_groups >= 4
    digits = codewords % (2 * LOW) == 0 and (codewords // LOW) * listed <= LOW
    return power and digits and entries * codewords <= 2**20 and rows_here % (2 * LANES) == 0


def per_device(vectors, row_slot, fine_codes, cell_list, coarse_in, fine_in):
    groups = lax.axis_size("cell")
    dense = fits_dense(groups, cell_list.shape[1], fine_in.shape[0], vectors.shape[0])
    plan = dense_plan if dense else routed_plan
    return plan(vectors, row_slot, fine_codes, cell_list, coarse_in, fine_in)


def solution(mesh):
    return jax.shard_map(
        per_device,
        mesh=mesh,
        in_specs=(
            P(("parts", "cell"), None),
            P(None, ("parts", "cell")),
            P(None, ("parts", "cell")),
            P(None, ("parts", "cell")),
            P("cell", None),
            P(),
        ),
        out_specs=(P(("parts", "cell"), None), P(("parts", "cell"), None)),
        check_vma=False,
    )
```

```python
import jax
import jax.numpy as jnp
from jax import lax
from jax.experimental import pallas as pl
from jax.experimental.pallas import tpu as pltpu
from jax.sharding import PartitionSpec as P


def code_tally(code_rows, codewords):
    return jax.ops.segment_sum(
        jnp.ones(code_rows.shape, jnp.float32), code_rows, num_segments=codewords
    )


def fine_update(code_term, totals_share, old_share, share_rows):
    part_sums = lax.psum_scatter(
        code_term(jnp.int32(0), lax.axis_size("cell") * share_rows),
        "cell",
        scatter_dimension=0,
        tiled=True,
    )
    return jnp.where(
        totals_share[:, None] > 0, part_sums / jnp.maximum(totals_share, 1.0)[:, None], old_share
    )


def routed_plan(vectors, row_slot, fine_codes, cell_list, coarse_in, fine_in):
    groups = lax.axis_size("cell")
    rows_here, feature = vectors.shape
    listed = cell_list.shape[1]
    slot_count = listed // groups
    owner_cells = coarse_in.shape[0]
    codewords = fine_in.shape[0]
    share_rows = codewords // groups
    share_start = lax.axis_index("cell") * share_rows
    fine_book = fine_in
    fine_share = lax.dynamic_slice_in_dim(fine_in, share_start, share_rows, 0)
    coarse = coarse_in
    list_iota = lax.iota(jnp.int32, listed)
    for sweep in range(2):
        code_totals = lax.psum(code_tally(fine_codes[sweep], codewords), "cell")
        slot_rows = row_slot[sweep]
        code_rows = fine_codes[sweep]
        picked = jnp.take(fine_book, code_rows, axis=0)
        residual = (vectors.astype(jnp.float32) - picked).astype(jnp.bfloat16)
        slot_hot = (slot_rows[None, :] == list_iota[:, None]).astype(jnp.bfloat16)
        slot_sums = jnp.dot(slot_hot, residual, preferred_element_type=jnp.float32)
        slot_counts = jnp.sum(slot_hot, axis=1, dtype=jnp.float32)
        slot_cells = cell_list[sweep].astype(jnp.float32)
        got_sums, got_counts, got_cells = (
            lax.all_to_all(
                slot_sums.reshape(groups, slot_count, feature),
                "cell",
                split_axis=0,
                concat_axis=0,
                tiled=True,
            ),
            lax.all_to_all(
                slot_counts.reshape(groups, slot_count),
                "cell",
                split_axis=0,
                concat_axis=0,
                tiled=True,
            ),
            lax.all_to_all(
                slot_cells.reshape(groups, slot_count),
                "cell",
                split_axis=0,
                concat_axis=0,
                tiled=True,
            ),
        )
        flat_cells = got_cells.reshape(groups * slot_count).astype(jnp.int32)
        cell_sums = jax.ops.segment_sum(
            got_sums.reshape(groups * slot_count, feature), flat_cells, num_segments=owner_cells
        )
        cell_counts = jax.ops.segment_sum(
            got_counts.reshape(groups * slot_count), flat_cells, num_segments=owner_cells
        )
        coarse = jnp.where(
            cell_counts[:, None] > 0, cell_sums / jnp.maximum(cell_counts, 1.0)[:, None], coarse
        )
        returned_rows = jnp.take(coarse, flat_cells, axis=0).reshape(groups, slot_count, feature)
        arrived = lax.all_to_all(returned_rows, "cell", split_axis=0, concat_axis=0, tiled=True)
        entry_centers = arrived.reshape(listed, feature)
        row_centers = jnp.take(entry_centers, slot_rows, axis=0)
        fine_residual = (vectors.astype(jnp.float32) - row_centers).astype(jnp.bfloat16)

        def code_term(start, count, code_rows=code_rows, fine_residual=fine_residual):
            wanted = start + lax.iota(jnp.int32, count)
            code_hot = (code_rows[None, :] == wanted[:, None]).astype(jnp.bfloat16)
            return jnp.dot(code_hot, fine_residual, preferred_element_type=jnp.float32)

        totals_share = lax.dynamic_slice_in_dim(code_totals, share_start, share_rows, 0)
        if sweep == 0:
            full_sums = lax.psum(code_term(0, codewords), "cell")
            fine_book = jnp.where(
                code_totals[:, None] > 0,
                full_sums / jnp.maximum(code_totals, 1.0)[:, None],
                fine_book,
            )
            fine_share = lax.dynamic_slice_in_dim(fine_book, share_start, share_rows, 0)
        else:
            fine_share = fine_update(code_term, totals_share, fine_share, share_rows)
    return (coarse, fine_share)


F32 = jnp.float32
BF16 = jnp.bfloat16
LOW = 256
LANES = 128
PARAMS = pltpu.CompilerParams(vmem_limit_bytes=56 * 2**20)
VMEM = pl.BlockSpec(memory_space=pltpu.VMEM)
SMEM = pl.BlockSpec(memory_space=pltpu.SMEM)
ANY = pl.BlockSpec(memory_space=pl.ANY)


def iota(shape, axis):
    return lax.broadcasted_iota(jnp.int32, shape, axis)


def matmul(left, right):
    return jnp.dot(left, right, preferred_element_type=F32)


def matmul_nt(left, right):
    return lax.dot_general(left, right, (((1,), (1,)), ((), ())), preferred_element_type=F32)


def split(values):
    high = values.astype(BF16)
    return high, (values - high.astype(F32)).astype(BF16)


def hot_rows(codes, rows=LOW):
    inside = jnp.where((codes >= 0) & (codes < rows), codes, -1)
    inside = inside.astype(F32).astype(BF16)
    row = iota((rows, codes.shape[1]), 0).astype(F32).astype(BF16)
    return jnp.where(row == inside, jnp.ones((), BF16), jnp.zeros((), BF16))


def pair_block(codes, slots, listed, high):
    left = hot_rows((codes >> 8) * listed + slots, high * listed)
    return matmul_nt(left, hot_rows(codes & (LOW - 1)))


def own_cells_kernel(listed, vectors, fine_codes, row_slot, fine_in, first_ref, second_ref):
    high = fine_in.shape[0] // LOW
    first = matmul(hot_rows(row_slot[0:1, :], listed), vectors[...])
    second_ref[...] = matmul(hot_rows(row_slot[1:2, :], listed), vectors[...])
    pairs = pair_block(fine_codes[0:1, :], row_slot[0:1, :], listed, high)
    for digit in range(high):
        pairs_high, pairs_low = split(pairs[digit * listed : (digit + 1) * listed])
        both = jnp.concatenate([pairs_high, pairs_low], axis=0)
        book = fine_in[digit * LOW : (digit + 1) * LOW, :]
        book_high, book_low = split(book)
        taken = matmul(both, book_high) + matmul(both, book_low)
        first = first - taken[:listed] - taken[listed:]
    first_ref[...] = first


def own_codes_kernel(base, vectors, fine_codes, _, sums_ref):
    codes = fine_codes[0:1, :] - base
    for start in range(0, sums_ref.shape[0], 2 * LOW):
        hot = jnp.concatenate(
            [hot_rows(codes - start), hot_rows(codes - start - LOW)], axis=0
        )
        sums_ref[start : start + 2 * LOW, :] = matmul(hot, vectors[...])


def position(block, groups):
    return (block & 1) * (groups // 2) + (block >> 1 & 1) * (groups // 4) + (block >> 2)


def tables_kernel(
    groups,
    slot_count,
    owner_cells,
    me_ref,
    codes_ref,
    low_sums_ref,
    high_sums_ref,
    first_ref,
    second_ref,
    share_ref,
    fine_ref,
    bracket_ref,
    pairs_ref,
    rest_ref,
    centers_ref,
    code_info_ref,
    entry_info_ref,
    passes_ref,
    table0,
    table1,
    cell0,
    cell1,
    wide,
    terms,
    permuted,
):
    me = me_ref[0]
    codewords, feature = fine_ref.shape
    listed = groups * slot_count
    entries = groups * listed
    high = codewords // LOW
    half = codes_ref.shape[2] - LANES
    share_rows = share_ref.shape[0]

    def device_tables(device, carry):
        at = position(device ^ me, groups)
        for sweep, table in enumerate((table0, table1)):
            block = jnp.zeros((high * listed, LOW), F32)
            for part in range(2):
                row = 2 * sweep + part
                block = block + pair_block(
                    codes_ref[at, row : row + 1, :half],
                    codes_ref[at, row + 4 : row + 5, :half],
                    listed,
                    high,
                )
            rows = pl.ds(pl.multiple_of(device * listed, listed), listed)
            for digit in range(high):
                table[rows, digit * LOW : (digit + 1) * LOW] = block[
                    digit * listed : (digit + 1) * listed
                ]
        return carry

    lax.fori_loop(0, groups, device_tables, 0)
    for device in range(groups):
        at = position(device ^ me, groups)
        for sweep, cell in enumerate((cell0, cell1)):
            row = codes_ref[at, sweep : sweep + 1, half : half + listed]
            cell[device * slot_count : (device + 1) * slot_count, :] = jnp.broadcast_to(
                row, (slot_count, listed)
            )

    row_at = iota((entries, listed), 0)
    owner_of = row_at // listed
    slot_of = owner_of * slot_count + row_at % slot_count
    is_slot = slot_of == iota((entries, listed), 1)
    device_of = (row_at // slot_count) % groups

    def entry_cells(cell):
        tiled = jnp.concatenate([cell[...]] * groups, axis=0)
        picked = jnp.sum(jnp.where(is_slot, tiled, 0), axis=1, keepdims=True)
        return picked.astype(F32)

    owner_col = owner_of[:, :1].astype(F32)
    cells = [entry_cells(cell0), entry_cells(cell1)]
    names = [cell + owner_col * float(owner_cells) for cell in cells]

    entry_row = iota((entries, entries), 0)
    natural = (
        ((entry_row // slot_count) % groups) * listed
        + (entry_row // listed) * slot_count
        + entry_row % slot_count
    )
    order = (natural == iota((entries, entries), 1)).astype(BF16)
    passes = jnp.where(
        jnp.maximum(jnp.max(table0[...]), jnp.max(table1[...])) > LOW, 2, 1
    ).astype(jnp.int32)
    passes_ref[0] = passes
    code_counts = [jnp.sum(table[...], axis=0, keepdims=True) for table in (table0, table1)]
    entry_counts = []
    for table in (table0, table1):
        count_high, count_low = split(
            jnp.broadcast_to(jnp.sum(table[...], axis=1, keepdims=True), (entries, LANES))
        )
        entry_counts.append(matmul(order, count_high) + matmul(order, count_low))
    for digit in range(high):
        columns = slice(digit * LOW, (digit + 1) * LOW)
        table_high, table_low = split(table1[:, columns])
        permuted[0, :, columns] = matmul(order, table_high).astype(BF16)
        permuted[1, :, columns] = matmul(order, table_low).astype(BF16)

    own_row = codes_ref[0, 0:1, half : half + listed].astype(F32)
    own_row = own_row + (iota((1, listed), 1) // slot_count).astype(F32) * float(owner_cells)
    match = (names[0] == own_row).astype(BF16)
    match = lax.dot_general(match, order, (((0,), (0,)), ((), ())), preferred_element_type=F32)
    match = match.astype(BF16)
    for digit in range(high):
        columns = slice(digit * LOW, (digit + 1) * LOW)
        table_high, table_low = split(table0[:, columns])
        used = matmul(match, table_high) + matmul(match, table_low)
        used_high, used_low = split(used)
        wide[0:listed, columns] = used_high.astype(F32)
        wide[listed : 2 * listed, columns] = used_low.astype(F32)
    held = wide[0:listed, :] + wide[listed : 2 * listed, :]
    held = jnp.sum(held, axis=1, keepdims=True)
    wide[2 * listed : 2 * listed + 8, :] = jnp.broadcast_to(code_counts[0], (8, codewords))
    wide[2 * listed + 8 : 2 * listed + 16, :] = jnp.broadcast_to(code_counts[1], (8, codewords))
    wide[2 * listed + 16 :, :] = jnp.zeros((LANES - 2 * listed - 16, codewords), F32)
    center_high, center_low = split(first_ref[...] / jnp.maximum(held, 1.0))
    center_high = jnp.concatenate(
        [center_high, center_high, jnp.zeros((LANES - 2 * listed, feature), BF16)], axis=0
    )
    center_low = jnp.concatenate(
        [center_low, center_low, jnp.zeros((LANES - 2 * listed, feature), BF16)], axis=0
    )
    for digit in range(high):
        rows = slice(digit * LOW, (digit + 1) * LOW)
        columns = wide[:, rows].T
        code_info_ref[rows, :] = columns
        columns_high = columns.astype(BF16)
        columns_high = jnp.where(
            iota((LOW, LANES), 1) < 2 * listed, columns_high.astype(F32), 0.0
        ).astype(BF16)
        at = digit % (high // 2) * LOW
        sums_ref = low_sums_ref if digit < high // 2 else high_sums_ref
        fine = sums_ref[at : at + LOW, :] - (
            matmul(columns_high, center_high) + matmul(columns_high, center_low)
        )
        fine_ref[rows, :] = jnp.where(
            columns[:, 2 * listed + 8 : 2 * listed + 9] > 0, 0.0, fine
        )
        scaled = fine / jnp.maximum(columns[:, 2 * listed : 2 * listed + 1], 1.0)
        terms[0, rows, :], terms[1, rows, :] = split(scaled)
    mine = pl.ds(pl.multiple_of(me * share_rows, share_rows), share_rows)
    empty = code_info_ref[mine, 2 * listed : 2 * listed + 1] == 0
    share_high, share_low = split(share_ref[...])
    terms[0, mine, :] = jnp.where(
        empty, share_high.astype(F32), terms[0, mine, :].astype(F32)
    ).astype(BF16)
    terms[1, mine, :] = jnp.where(
        empty, share_low.astype(F32), terms[1, mine, :].astype(F32)
    ).astype(BF16)

    own_entry = (is_slot & (device_of == me)).astype(BF16)
    second_high, second_low = split(second_ref[...])
    bracket_ref[...] = (
        matmul(own_entry, second_high)
        + matmul(own_entry, second_low)
        - matmul(permuted[0], terms[0])
        - matmul(permuted[0], terms[1])
    )

    @pl.when(passes > 1)
    def _():
        bracket_ref[...] -= matmul(permuted[1], terms[0])

    same = (
        jnp.broadcast_to(names[1], (entries, entries))
        == jnp.broadcast_to(names[1], (entries, LANES)).T[0:1, :]
    ).astype(BF16)
    total_high, total_low = split(entry_counts[1])
    totals = matmul(same, total_high) + matmul(same, total_low)
    bracket_high, bracket_low = split(bracket_ref[...])
    centers = matmul(same, bracket_high) + matmul(same, bracket_low)
    centers = centers / jnp.maximum(totals[:, :1], 1.0)
    centers_ref[0], centers_ref[1] = split(centers)

    eye = (iota((LOW, LOW), 0) == iota((LOW, LOW), 1)).astype(BF16)
    for digit in range(high):
        rows = slice(digit * LOW, (digit + 1) * LOW)
        pairs_ref[rows, :] = matmul_nt(eye, permuted[0, :, rows]).astype(BF16)
        rest_ref[rows, :] = matmul_nt(eye, permuted[1, :, rows]).astype(BF16)
    lane = iota((entries, LANES), 1)
    info = jnp.where(lane == 0, entry_counts[0], entry_counts[1])
    info = jnp.where(lane == 2, cells[0], info)
    entry_info_ref[...] = jnp.where(lane == 3, cells[1], info)


def last_kernel(
    orders,
    listed,
    me_ref,
    passes_ref,
    vectors,
    fine_codes,
    pairs_ref,
    rest_ref,
    centers_ref,
    fine_ref,
    bracket_ref,
    _,
    *refs,
):
    outs, left, rest, sem = refs[:-3], refs[-3], refs[-2], refs[-1]
    me = me_ref[0]
    rows_here = vectors.shape[0]
    share_rows = outs[0].shape[1] - listed
    codes = fine_codes[1:2, :]
    for order, out in zip(orders, outs):
        for at, block in enumerate(order):
            owner = me ^ block
            rows = pl.ds(pl.multiple_of(owner * share_rows, share_rows), share_rows)
            to = slice(at * share_rows, (at + 1) * share_rows)
            left[to, :rows_here] = hot_rows(codes - owner * share_rows, share_rows)
            left[to, rows_here:] = -pairs_ref[rows, :]
        used = slice(0, len(order) * share_rows)
        sums = (
            matmul(left[used, :rows_here], vectors[...])
            + matmul(left[used, rows_here:], centers_ref[0])
            + matmul(left[used, rows_here:], centers_ref[1])
        )
        for at, block in enumerate(order):
            owner = me ^ block
            rows = pl.ds(pl.multiple_of(owner * share_rows, share_rows), share_rows)
            out[at, :share_rows, :] = (
                sums[at * share_rows : (at + 1) * share_rows] + fine_ref[rows, :]
            )
            cells = pl.ds(pl.multiple_of(owner * listed, listed), listed)
            out[at, share_rows:, :] = bracket_ref[cells, :]

    @pl.when(passes_ref[0] > 1)
    def _():
        copy = pltpu.make_async_copy(rest_ref, rest, sem)
        copy.start()
        copy.wait()
        for order, out in zip(orders, outs):
            for at, block in enumerate(order):
                owner = me ^ block
                rows = pl.ds(pl.multiple_of(owner * share_rows, share_rows), share_rows)
                out[at, :share_rows, :] -= matmul(rest[rows, :], centers_ref[0])


def final_kernel(
    share_rows,
    coarse_in,
    fine_share,
    first_sums,
    last_sums,
    code_info,
    entry_info,
    coarse_out,
    fine_out,
):
    listed = entry_info.shape[0]
    owner_cells, cut = coarse_in.shape
    by_lane = entry_info[...].T
    info = [by_lane[at : at + 1, :] for at in range(4)]
    coarse = coarse_in[...]
    own_first = first_sums[...].reshape(listed, cut)
    for sweep, sums in enumerate((own_first, last_sums[share_rows:, :])):
        cell = info[2 + sweep].astype(jnp.int32)
        hit = iota((owner_cells, listed), 0) == cell
        counts = jnp.sum(jnp.where(hit, info[sweep], 0.0), axis=1, keepdims=True)
        picks = hit.astype(BF16)
        sums_high, sums_low = split(sums)
        found = matmul(picks, sums_high) + matmul(picks, sums_low)
        coarse = jnp.where(counts > 0, found / jnp.maximum(counts, 1.0), coarse)
    coarse_out[...] = coarse
    first_count = code_info[:, 2 * listed : 2 * listed + 1]
    last_count = code_info[:, 2 * listed + 8 : 2 * listed + 9]
    count = jnp.where(last_count > 0, last_count, first_count)
    fine_out[...] = jnp.where(
        count > 0, last_sums[:share_rows, :] / jnp.maximum(count, 1.0), fine_share[...]
    )


def exchange(values, step):
    groups = lax.axis_size("cell")
    return lax.ppermute(values, "cell", [(at, at ^ step) for at in range(groups)])


def block_orders(bits):
    order = [0]
    for bit in bits[::-1]:
        order = [block + (1 << bit) for block in order] + order
    half = len(order) // 2
    return [block + 1 for block in order], order[:half], order[half:]


def scatter_sums(other, kept, bits):
    for bit in bits[:-1]:
        got = exchange(other, 1 << bit)
        half = got.shape[0] // 2
        other, kept = kept[:half] + got[:half], kept[half:] + got[half:]
    return (kept + exchange(other, 1 << bits[-1]))[0]


def local(kernel, shapes, in_specs, out_specs, scratch, flops, name, aliases=None):
    return pl.pallas_call(
        kernel,
        out_shape=tuple(jax.ShapeDtypeStruct(shape, dtype) for shape, dtype in shapes),
        grid_spec=pltpu.PrefetchScalarGridSpec(
            num_scalar_prefetch=1,
            grid=(1,),
            in_specs=in_specs,
            out_specs=out_specs,
            scratch_shapes=scratch,
        ),
        input_output_aliases=aliases or {},
        compiler_params=PARAMS,
        cost_estimate=pl.CostEstimate(
            flops=int(flops), bytes_accessed=10**6, transcendentals=0
        ),
        name=name,
    )


def block(shape, *place):
    return pl.BlockSpec(
        shape, lambda step, me: tuple(me[0] if at is None else at for at in place)
    )


def dense_plan(vectors, row_slot, fine_codes, cell_list, coarse_in, fine_in):
    groups = lax.axis_size("cell")
    rows_here, feature = vectors.shape
    listed = cell_list.shape[1]
    slot_count = listed // groups
    owner_cells = coarse_in.shape[0]
    codewords = fine_in.shape[0]
    share_rows = codewords // groups
    entries = groups * listed
    half = rows_here // 2
    me = lax.axis_index("cell").reshape(1).astype(jnp.int32)

    codes = jnp.concatenate([fine_codes.reshape(4, half), row_slot.reshape(4, half)], axis=0)
    cells = jnp.pad(cell_list, ((0, 6), (0, LANES - listed)))
    packed = jnp.concatenate([codes, cells], axis=1)
    first, second = local(
        lambda me_ref, *refs: own_cells_kernel(listed, *refs),
        [((listed, feature), F32)] * 2,
        [VMEM] * 4,
        [VMEM] * 2,
        [],
        5e9,
        "own_cells",
    )(me, vectors, fine_codes, row_slot, fine_in)
    first_all = lax.all_gather(first.reshape(groups, slot_count, feature), "cell")
    far = groups // 4
    gathered = jnp.stack([packed] + [exchange(packed, 4 * step) for step in range(1, far)])
    sums = []
    for step, base in ((2, 0), (1, codewords // 2)):
        sums += local(
            lambda me_ref, *refs, base=base: own_codes_kernel(base, *refs),
            [((codewords // 2, feature), F32)],
            [VMEM, VMEM, ANY],
            [VMEM],
            [],
            6e9,
            "own_codes",
        )(me, vectors, fine_codes, gathered)
        gathered = jnp.concatenate([gathered, exchange(gathered, step)])

    fine, bracket, pairs, rest, centers, code_info, entry_info, passes = local(
        lambda *refs: tables_kernel(groups, slot_count, owner_cells, *refs),
        [
            ((codewords, feature), F32),
            ((entries, feature), F32),
            ((codewords, entries), BF16),
            ((codewords, entries), BF16),
            ((2, entries, feature), BF16),
            ((codewords, LANES), F32),
            ((entries, LANES), F32),
            ((1,), jnp.int32),
        ],
        [VMEM] * 5 + [block((share_rows, feature), None, 0)],
        [VMEM] * 7 + [SMEM],
        [
            pltpu.VMEM((entries, codewords), F32),
            pltpu.VMEM((entries, codewords), F32),
            pltpu.VMEM((listed, listed), jnp.int32),
            pltpu.VMEM((listed, listed), jnp.int32),
            pltpu.VMEM((LANES, codewords), F32),
            pltpu.VMEM((2, codewords, feature), BF16),
            pltpu.VMEM((2, entries, codewords), BF16),
        ],
        34e9,
        "tables",
    )(me, gathered, *sums, first, second, fine_in)

    cut = feature // 3
    top = groups.bit_length() - 1
    near_first = list(range(1, top))
    far_first = near_first[1:] + near_first[:1]
    begun = []
    for at, bits in enumerate((near_first, far_first, near_first)):
        orders = block_orders(bits)
        ahead = begun[-2][1] if len(begun) > 1 else first_all
        away, other, kept = local(
            lambda *refs: last_kernel(orders, listed, *refs),
            [((len(order), share_rows + listed, cut), F32) for order in orders],
            [
                SMEM,
                block((rows_here, cut), 0, at),
                VMEM,
                VMEM,
                ANY,
                block((2, entries, cut), 0, 0, at),
                block((codewords, cut), 0, at),
                block((entries, cut), 0, at),
                ANY,
            ],
            [VMEM] * len(orders),
            [
                pltpu.VMEM((len(orders[0]) * share_rows, rows_here + entries), BF16),
                pltpu.VMEM((codewords, entries), BF16),
                pltpu.SemaphoreType.DMA,
            ],
            9e9,
            "last_sums",
        )(me, passes, vectors, fine_codes, pairs, rest, centers, fine, bracket, ahead)
        got = exchange(away, 1)
        size = other.shape[0]
        begun.append((bits, other + got[:size], kept + got[size:]))

    outs = ()
    for at, (bits, other, kept) in enumerate(begun):
        last_sums = scatter_sums(other, kept, bits)
        outs = local(
            lambda me_ref, *refs: final_kernel(share_rows, *refs[:6], *refs[-2:]),
            [(coarse_in.shape, F32), ((share_rows, feature), F32)],
            [
                block((owner_cells, cut), 0, at),
                block((share_rows, cut), None, at),
                block((groups, 1, slot_count, cut), 0, None, 0, at),
                VMEM,
                block((share_rows, LANES), None, 0),
                block((listed, LANES), None, 0),
            ]
            + [ANY] * len(outs),
            [block((owner_cells, cut), 0, at), block((share_rows, cut), 0, at)],
            [],
            1e9,
            "outputs",
            {7 + number: number for number in range(len(outs))},
        )(me, coarse_in, fine_in, first_all, last_sums, code_info, entry_info, *outs)
    return tuple(outs)


def fits_dense(mesh_groups, listed, codewords, rows_here):
    entries = mesh_groups * listed
    power = mesh_groups & (mesh_groups - 1) == 0 and mesh_groups >= 4
    digits = codewords % (2 * LOW) == 0 and (codewords // LOW) * listed <= LOW
    return power and digits and entries * codewords <= 2**20 and rows_here % (2 * LANES) == 0


def per_device(vectors, row_slot, fine_codes, cell_list, coarse_in, fine_in):
    groups = lax.axis_size("cell")
    dense = fits_dense(groups, cell_list.shape[1], fine_in.shape[0], vectors.shape[0])
    plan = dense_plan if dense else routed_plan
    return plan(vectors, row_slot, fine_codes, cell_list, coarse_in, fine_in)


def solution(mesh):
    return jax.shard_map(
        per_device,
        mesh=mesh,
        in_specs=(
            P(("parts", "cell"), None),
            P(None, ("parts", "cell")),
            P(None, ("parts", "cell")),
            P(None, ("parts", "cell")),
            P("cell", None),
            P(),
        ),
        out_specs=(P(("parts", "cell"), None), P(("parts", "cell"), None)),
        check_vma=False,
    )
```

```python
import jax
import jax.numpy as jnp
from jax import lax
from jax.experimental import pallas as pl
from jax.experimental.pallas import tpu as pltpu
from jax.sharding import PartitionSpec as P


def code_tally(code_rows, codewords):
    return jax.ops.segment_sum(
        jnp.ones(code_rows.shape, jnp.float32), code_rows, num_segments=codewords
    )


def fine_update(code_term, totals_share, old_share, share_rows):
    part_sums = lax.psum_scatter(
        code_term(jnp.int32(0), lax.axis_size("cell") * share_rows),
        "cell",
        scatter_dimension=0,
        tiled=True,
    )
    return jnp.where(
        totals_share[:, None] > 0, part_sums / jnp.maximum(totals_share, 1.0)[:, None], old_share
    )


def routed_plan(vectors, row_slot, fine_codes, cell_list, coarse_in, fine_in):
    groups = lax.axis_size("cell")
    rows_here, feature = vectors.shape
    listed = cell_list.shape[1]
    slot_count = listed // groups
    owner_cells = coarse_in.shape[0]
    codewords = fine_in.shape[0]
    share_rows = codewords // groups
    share_start = lax.axis_index("cell") * share_rows
    fine_book = fine_in
    fine_share = lax.dynamic_slice_in_dim(fine_in, share_start, share_rows, 0)
    coarse = coarse_in
    list_iota = lax.iota(jnp.int32, listed)
    for sweep in range(2):
        code_totals = lax.psum(code_tally(fine_codes[sweep], codewords), "cell")
        slot_rows = row_slot[sweep]
        code_rows = fine_codes[sweep]
        picked = jnp.take(fine_book, code_rows, axis=0)
        residual = (vectors.astype(jnp.float32) - picked).astype(jnp.bfloat16)
        slot_hot = (slot_rows[None, :] == list_iota[:, None]).astype(jnp.bfloat16)
        slot_sums = jnp.dot(slot_hot, residual, preferred_element_type=jnp.float32)
        slot_counts = jnp.sum(slot_hot, axis=1, dtype=jnp.float32)
        slot_cells = cell_list[sweep].astype(jnp.float32)
        got_sums, got_counts, got_cells = (
            lax.all_to_all(
                slot_sums.reshape(groups, slot_count, feature),
                "cell",
                split_axis=0,
                concat_axis=0,
                tiled=True,
            ),
            lax.all_to_all(
                slot_counts.reshape(groups, slot_count),
                "cell",
                split_axis=0,
                concat_axis=0,
                tiled=True,
            ),
            lax.all_to_all(
                slot_cells.reshape(groups, slot_count),
                "cell",
                split_axis=0,
                concat_axis=0,
                tiled=True,
            ),
        )
        flat_cells = got_cells.reshape(groups * slot_count).astype(jnp.int32)
        cell_sums = jax.ops.segment_sum(
            got_sums.reshape(groups * slot_count, feature), flat_cells, num_segments=owner_cells
        )
        cell_counts = jax.ops.segment_sum(
            got_counts.reshape(groups * slot_count), flat_cells, num_segments=owner_cells
        )
        coarse = jnp.where(
            cell_counts[:, None] > 0, cell_sums / jnp.maximum(cell_counts, 1.0)[:, None], coarse
        )
        returned_rows = jnp.take(coarse, flat_cells, axis=0).reshape(groups, slot_count, feature)
        arrived = lax.all_to_all(returned_rows, "cell", split_axis=0, concat_axis=0, tiled=True)
        entry_centers = arrived.reshape(listed, feature)
        row_centers = jnp.take(entry_centers, slot_rows, axis=0)
        fine_residual = (vectors.astype(jnp.float32) - row_centers).astype(jnp.bfloat16)

        def code_term(start, count, code_rows=code_rows, fine_residual=fine_residual):
            wanted = start + lax.iota(jnp.int32, count)
            code_hot = (code_rows[None, :] == wanted[:, None]).astype(jnp.bfloat16)
            return jnp.dot(code_hot, fine_residual, preferred_element_type=jnp.float32)

        totals_share = lax.dynamic_slice_in_dim(code_totals, share_start, share_rows, 0)
        if sweep == 0:
            full_sums = lax.psum(code_term(0, codewords), "cell")
            fine_book = jnp.where(
                code_totals[:, None] > 0,
                full_sums / jnp.maximum(code_totals, 1.0)[:, None],
                fine_book,
            )
            fine_share = lax.dynamic_slice_in_dim(fine_book, share_start, share_rows, 0)
        else:
            fine_share = fine_update(code_term, totals_share, fine_share, share_rows)
    return (coarse, fine_share)


F32 = jnp.float32
BF16 = jnp.bfloat16
LOW = 256
LANES = 128
PARAMS = pltpu.CompilerParams(vmem_limit_bytes=60 * 2**20)
VMEM = pl.BlockSpec(memory_space=pltpu.VMEM)
SMEM = pl.BlockSpec(memory_space=pltpu.SMEM)
ANY = pl.BlockSpec(memory_space=pl.ANY)


def iota(shape, axis):
    return lax.broadcasted_iota(jnp.int32, shape, axis)


def matmul(left, right):
    return jnp.dot(left, right, preferred_element_type=F32)


def matmul_nt(left, right):
    return lax.dot_general(left, right, (((1,), (1,)), ((), ())), preferred_element_type=F32)


def split(values):
    high = values.astype(BF16)
    return high, (values - high.astype(F32)).astype(BF16)


def hot_rows(codes, rows=LOW):
    inside = jnp.where((codes >= 0) & (codes < rows), codes, -1)
    inside = inside.astype(F32).astype(BF16)
    row = iota((rows, codes.shape[1]), 0).astype(F32).astype(BF16)
    return jnp.where(row == inside, jnp.ones((), BF16), jnp.zeros((), BF16))


def pair_block(codes, slots, listed, high):
    left = hot_rows((codes >> 8) * listed + slots, high * listed)
    return matmul_nt(left, hot_rows(codes & (LOW - 1)))


def own_cells_kernel(listed, vectors, fine_codes, row_slot, fine_in, first_ref, second_ref):
    high = fine_in.shape[0] // LOW
    first = matmul(hot_rows(row_slot[0:1, :], listed), vectors[...])
    second_ref[...] = matmul(hot_rows(row_slot[1:2, :], listed), vectors[...])
    pairs = pair_block(fine_codes[0:1, :], row_slot[0:1, :], listed, high)
    for digit in range(high):
        pairs_high, pairs_low = split(pairs[digit * listed : (digit + 1) * listed])
        both = jnp.concatenate([pairs_high, pairs_low], axis=0)
        book = fine_in[digit * LOW : (digit + 1) * LOW, :]
        book_high, book_low = split(book)
        taken = matmul(both, book_high) + matmul(both, book_low)
        first = first - taken[:listed] - taken[listed:]
    first_ref[...] = first


def own_codes_kernel(base, vectors, fine_codes, _, sums_ref):
    codes = fine_codes[0:1, :] - base
    for start in range(0, sums_ref.shape[0], 2 * LOW):
        hot = jnp.concatenate(
            [hot_rows(codes - start), hot_rows(codes - start - LOW)], axis=0
        )
        sums_ref[start : start + 2 * LOW, :] = matmul(hot, vectors[...])


def position(block, groups):
    return (block & 1) * (groups // 2) + (block >> 1 & 1) * (groups // 4) + (block >> 2)


def sums_kernel(
    groups,
    slot_count,
    owner_cells,
    cuts,
    orders,
    me_ref,
    codes_ref,
    vectors,
    fine_codes,
    low_sums_ref,
    high_sums_ref,
    first_ref,
    second_ref,
    share_ref,
    _,
    *refs,
):
    out_refs, refs = refs[: 3 * len(cuts)], refs[3 * len(cuts) :]
    code_info_ref, entry_info_ref, refs = refs[0], refs[1], refs[2:]
    table0, table1, cell0, cell1, wide, terms, permuted, rows_hot = refs[:8]
    fine, bracket, centers_ref, pairs_ref, left = refs[8:13]
    in_sem, out_sem, stages = refs[13], refs[14], refs[15:]
    me = me_ref[0]
    codewords, feature = fine.shape
    listed = groups * slot_count
    entries = groups * listed
    high = codewords // LOW
    half = codes_ref.shape[2] - LANES
    share_rows = share_ref.shape[0]

    loads = [
        pltpu.make_async_copy(
            ref, fine.at[pl.ds(at * (codewords // 2), codewords // 2)], in_sem.at[at]
        )
        for at, ref in enumerate((low_sums_ref, high_sums_ref))
    ]
    for load in loads:
        load.start()

    rows_hot[...] = iota(rows_hot.shape, 0).astype(F32).astype(BF16)
    one, zero = jnp.ones((), BF16), jnp.zeros((), BF16)

    def hot(codes):
        return jnp.where(rows_hot[...] == codes.astype(F32).astype(BF16), one, zero)

    def device_tables(device, carry):
        at = position(device ^ me, groups)
        for sweep, table in enumerate((table0, table1)):
            block = jnp.zeros((high * listed, LOW), F32)
            for part in range(2):
                row = 2 * sweep + part
                codes = codes_ref[at, row : row + 1, :half]
                slots = codes_ref[at, row + 4 : row + 5, :half]
                block = block + matmul_nt(
                    hot((codes >> 8) * listed + slots)[: high * listed], hot(codes & (LOW - 1))
                )
            rows = pl.ds(pl.multiple_of(device * listed, listed), listed)
            for digit in range(high):
                table[rows, digit * LOW : (digit + 1) * LOW] = block[
                    digit * listed : (digit + 1) * listed
                ]
        return carry

    lax.fori_loop(0, groups, device_tables, 0)
    for device in range(groups):
        at = position(device ^ me, groups)
        for sweep, cell in enumerate((cell0, cell1)):
            row = codes_ref[at, sweep : sweep + 1, half : half + listed]
            cell[device * slot_count : (device + 1) * slot_count, :] = jnp.broadcast_to(
                row, (slot_count, listed)
            )

    row_at = iota((entries, listed), 0)
    owner_of = row_at // listed
    slot_of = owner_of * slot_count + row_at % slot_count
    is_slot = slot_of == iota((entries, listed), 1)
    device_of = (row_at // slot_count) % groups

    def entry_cells(cell):
        tiled = jnp.concatenate([cell[...]] * groups, axis=0)
        picked = jnp.sum(jnp.where(is_slot, tiled, 0), axis=1, keepdims=True)
        return picked.astype(F32)

    owner_col = owner_of[:, :1].astype(F32)
    cells = [entry_cells(cell0), entry_cells(cell1)]
    names = [cell + owner_col * float(owner_cells) for cell in cells]

    entry_row = iota((entries, entries), 0)
    natural = (
        ((entry_row // slot_count) % groups) * listed
        + (entry_row // listed) * slot_count
        + entry_row % slot_count
    )
    order = (natural == iota((entries, entries), 1)).astype(BF16)
    code_counts = [jnp.sum(table[...], axis=0, keepdims=True) for table in (table0, table1)]
    entry_counts = []
    for table in (table0, table1):
        count_high, count_low = split(
            jnp.broadcast_to(jnp.sum(table[...], axis=1, keepdims=True), (entries, LANES))
        )
        entry_counts.append(matmul(order, count_high) + matmul(order, count_low))
    most = jnp.maximum(jnp.max(table0[...]), jnp.max(table1[...]))
    large = most > LOW
    for digit in range(high):
        columns = slice(digit * LOW, (digit + 1) * LOW)
        permuted[0, :, columns] = matmul(order, table1[:, columns].astype(BF16)).astype(BF16)

    @pl.when(large)
    def _():
        for digit in range(high):
            columns = slice(digit * LOW, (digit + 1) * LOW)
            rest = split(table1[:, columns])[1]
            permuted[1, :, columns] = matmul(order, rest).astype(BF16)

    own_row = codes_ref[0, 0:1, half : half + listed].astype(F32)
    own_row = own_row + (iota((1, listed), 1) // slot_count).astype(F32) * float(owner_cells)
    match = (names[0] == own_row).astype(BF16)
    match = lax.dot_general(match, order, (((0,), (0,)), ((), ())), preferred_element_type=F32)
    match = match.astype(BF16)
    held = jnp.zeros((listed, 1), F32)
    for digit in range(high):
        columns = slice(digit * LOW, (digit + 1) * LOW)
        table_high, table_low = split(table0[:, columns])
        used = matmul(match, table_high) + matmul(match, table_low)
        held = held + jnp.sum(used, axis=1, keepdims=True)
        used_high, used_low = split(used)
        wide[0:listed, columns] = used_high.astype(F32)
        wide[listed : 2 * listed, columns] = used_low.astype(F32)
    wide[2 * listed : 2 * listed + 8, :] = jnp.broadcast_to(code_counts[0], (8, codewords))
    wide[2 * listed + 8 : 2 * listed + 16, :] = jnp.broadcast_to(code_counts[1], (8, codewords))
    wide[2 * listed + 16 :, :] = jnp.zeros((LANES - 2 * listed - 16, codewords), F32)
    center_high, center_low = split(first_ref[...] / jnp.maximum(held, 1.0))
    blank = jnp.zeros((LANES - 2 * listed, feature), BF16)
    center_high = jnp.concatenate([center_high, center_high, blank], axis=0)
    center_low = jnp.concatenate([center_low, center_low, blank], axis=0)
    for load in loads:
        load.wait()
    for digit in range(high):
        rows = slice(digit * LOW, (digit + 1) * LOW)
        columns = wide[:, rows].T
        code_info_ref[rows, :] = columns
        taken = jnp.where(iota((LOW, LANES), 1) < 2 * listed, columns, 0.0).astype(BF16)
        first_fine = fine[rows, :] - (matmul(taken, center_high) + matmul(taken, center_low))
        scaled = first_fine / jnp.maximum(columns[:, 2 * listed : 2 * listed + 1], 1.0)
        terms[0, rows, :], terms[1, rows, :] = split(scaled)
        fine[rows, :] = jnp.where(
            columns[:, 2 * listed + 8 : 2 * listed + 9] > 0, 0.0, first_fine
        )
    mine = pl.ds(pl.multiple_of(me * share_rows, share_rows), share_rows)
    empty = code_info_ref[mine, 2 * listed : 2 * listed + 1] == 0
    for part, share in enumerate(split(share_ref[...])):
        terms[part, mine, :] = jnp.where(
            empty, share.astype(F32), terms[part, mine, :].astype(F32)
        ).astype(BF16)

    own_entry = (is_slot & (device_of == me)).astype(BF16)
    second_high, second_low = split(second_ref[...])
    bracket[...] = (
        matmul(own_entry, second_high)
        + matmul(own_entry, second_low)
        - matmul(permuted[0], terms[0])
        - matmul(permuted[0], terms[1])
    )

    @pl.when(large)
    def _():
        bracket[...] -= matmul(permuted[1], terms[0])

    same = (
        jnp.broadcast_to(names[1], (entries, entries))
        == jnp.broadcast_to(names[1], (entries, LANES)).T[0:1, :]
    ).astype(BF16)
    total_high, total_low = split(entry_counts[1])
    totals = matmul(same, total_high) + matmul(same, total_low)
    bracket_high, bracket_low = split(bracket[...])
    centers = matmul(same, bracket_high) + matmul(same, bracket_low)
    centers = centers / jnp.maximum(totals[:, :1], 1.0)
    centers_ref[0], centers_ref[1] = split(centers)
    lane = iota((entries, LANES), 1)
    info = jnp.where(lane == 0, entry_counts[0], entry_counts[1])
    info = jnp.where(lane == 2, cells[0], info)
    entry_info_ref[...] = jnp.where(lane == 3, cells[1], info)

    eye = (iota((LOW, LOW), 0) == iota((LOW, LOW), 1)).astype(BF16)
    for digit in range(high):
        rows = slice(digit * LOW, (digit + 1) * LOW)
        pairs_ref[rows, :] = -matmul_nt(eye, permuted[0, :, rows]).astype(BF16)
    rows_here = vectors.shape[0]
    codes = fine_codes[1:2, :]
    copies = []
    for odd in (1, 0):
        blocks = [at for at in range(groups) if at % 2 == odd]
        for at, block in enumerate(blocks):
            owner = me ^ block
            rows = pl.ds(pl.multiple_of(owner * share_rows, share_rows), share_rows)
            to = slice(at * share_rows, (at + 1) * share_rows)
            left[to, :rows_here] = hot_rows(codes - owner * share_rows, share_rows)
            left[to, rows_here:] = pairs_ref[rows, :]
        start = 0
        for chunk, cut in enumerate(cuts):
            columns = slice(start, start + cut)
            start += cut
            sums = (
                matmul(left[:, :rows_here], vectors[:, columns])
                + matmul(left[:, rows_here:], centers_ref[0, :, columns])
                + matmul(left[:, rows_here:], centers_ref[1, :, columns])
            )
            for part, order_of in enumerate(orders[chunk]):
                if order_of[0] % 2 != odd:
                    continue
                number = 3 * chunk + part
                stage = stages[number]
                for to, block in enumerate(order_of):
                    owner = me ^ block
                    rows = pl.ds(pl.multiple_of(owner * share_rows, share_rows), share_rows)
                    cell_rows = pl.ds(pl.multiple_of(owner * listed, listed), listed)
                    at = blocks.index(block) * share_rows
                    stage[to, :share_rows, :] = sums[at : at + share_rows] + fine[rows, columns]
                    stage[to, share_rows:, :] = bracket[cell_rows, columns]

                @pl.when(large)
                def _():
                    for to, block in enumerate(order_of):
                        owner = me ^ block
                        rows = pl.ds(pl.multiple_of(owner * share_rows, share_rows), share_rows)
                        rest = lax.dot_general(
                            permuted[1, :, rows],
                            centers_ref[0, :, columns],
                            (((0,), (0,)), ((), ())),
                            preferred_element_type=F32,
                        )
                        stage[to, :share_rows, :] -= rest

                copy = pltpu.make_async_copy(stage, out_refs[number], out_sem.at[number])
                copy.start()
                copies.append(copy)
    for copy in copies:
        copy.wait()


def final_kernel(
    share_rows,
    coarse_in,
    fine_share,
    first_sums,
    last_sums,
    code_info,
    entry_info,
    coarse_out,
    fine_out,
):
    listed = entry_info.shape[0]
    owner_cells, cut = coarse_in.shape
    by_lane = entry_info[...].T
    info = [by_lane[at : at + 1, :] for at in range(4)]
    coarse = coarse_in[...]
    own_first = first_sums[...].reshape(listed, cut)
    for sweep, sums in enumerate((own_first, last_sums[share_rows:, :])):
        cell = info[2 + sweep].astype(jnp.int32)
        hit = iota((owner_cells, listed), 0) == cell
        counts = jnp.sum(jnp.where(hit, info[sweep], 0.0), axis=1, keepdims=True)
        picks = hit.astype(BF16)
        sums_high, sums_low = split(sums)
        found = matmul(picks, sums_high) + matmul(picks, sums_low)
        coarse = jnp.where(counts > 0, found / jnp.maximum(counts, 1.0), coarse)
    coarse_out[...] = coarse
    first_count = code_info[:, 2 * listed : 2 * listed + 1]
    last_count = code_info[:, 2 * listed + 8 : 2 * listed + 9]
    count = jnp.where(last_count > 0, last_count, first_count)
    fine_out[...] = jnp.where(
        count > 0, last_sums[:share_rows, :] / jnp.maximum(count, 1.0), fine_share[...]
    )


def exchange(values, step):
    groups = lax.axis_size("cell")
    return lax.ppermute(values, "cell", [(at, at ^ step) for at in range(groups)])


def block_orders(bits):
    order = [0]
    for bit in bits[::-1]:
        order = [block + (1 << bit) for block in order] + order
    half = len(order) // 2
    return [block + 1 for block in order], order[:half], order[half:]


def scatter_sums(other, kept, bits):
    for bit in bits[:-1]:
        got = exchange(other, 1 << bit)
        half = got.shape[0] // 2
        other, kept = kept[:half] + got[:half], kept[half:] + got[half:]
    return (kept + exchange(other, 1 << bits[-1]))[0]


def local(kernel, shapes, in_specs, out_specs, scratch, flops, name, aliases=None):
    return pl.pallas_call(
        kernel,
        out_shape=tuple(jax.ShapeDtypeStruct(shape, dtype) for shape, dtype in shapes),
        grid_spec=pltpu.PrefetchScalarGridSpec(
            num_scalar_prefetch=1,
            grid=(1,),
            in_specs=in_specs,
            out_specs=out_specs,
            scratch_shapes=scratch,
        ),
        input_output_aliases=aliases or {},
        compiler_params=PARAMS,
        cost_estimate=pl.CostEstimate(
            flops=int(flops), bytes_accessed=10**6, transcendentals=0
        ),
        name=name,
    )


def block(shape, *place):
    return pl.BlockSpec(
        shape, lambda step, me: tuple(me[0] if at is None else at for at in place)
    )


def dense_plan(vectors, row_slot, fine_codes, cell_list, coarse_in, fine_in):
    groups = lax.axis_size("cell")
    rows_here, feature = vectors.shape
    listed = cell_list.shape[1]
    slot_count = listed // groups
    owner_cells = coarse_in.shape[0]
    codewords = fine_in.shape[0]
    share_rows = codewords // groups
    entries = groups * listed
    half = rows_here // 2
    me = lax.axis_index("cell").reshape(1).astype(jnp.int32)

    codes = jnp.concatenate([fine_codes.reshape(4, half), row_slot.reshape(4, half)], axis=0)
    cells = jnp.pad(cell_list, ((0, 6), (0, LANES - listed)))
    packed = jnp.concatenate([codes, cells], axis=1)
    first, second = local(
        lambda me_ref, *refs: own_cells_kernel(listed, *refs),
        [((listed, feature), F32)] * 2,
        [VMEM] * 4,
        [VMEM] * 2,
        [],
        5e9,
        "own_cells",
    )(me, vectors, fine_codes, row_slot, fine_in)
    first_own = lax.all_to_all(
        first.reshape(groups, slot_count, feature), "cell", split_axis=0, concat_axis=0, tiled=True
    )
    far = groups // 4
    gathered = jnp.stack([packed] + [exchange(packed, 4 * step) for step in range(1, far)])
    sums = []
    for step, base in ((2, 0), (1, codewords // 2)):
        sums += local(
            lambda me_ref, *refs, base=base: own_codes_kernel(base, *refs),
            [((codewords // 2, feature), F32)],
            [VMEM, VMEM, ANY],
            [VMEM],
            [],
            6e9,
            "own_codes",
        )(me, vectors, fine_codes, gathered)
        gathered = jnp.concatenate([gathered, exchange(gathered, step)])

    top = groups.bit_length() - 1
    near_first = list(range(1, top))
    far_first = near_first[1:] + near_first[:1]
    cuts = [feature // 3, feature // 6, feature // 6, feature // 3]
    bits = [near_first, far_first, near_first, near_first]
    turns = [0, 1, 3, 2]
    orders = [block_orders(each) for each in bits]
    shapes = [
        (len(order), share_rows + listed, cut)
        for cut, three in zip(cuts, orders)
        for order in three
    ]
    *terms, code_info, entry_info = local(
        lambda *refs: sums_kernel(groups, slot_count, owner_cells, cuts, orders, *refs),
        [(shape, F32) for shape in shapes]
        + [((codewords, LANES), F32), ((entries, LANES), F32)],
        [VMEM] * 3 + [ANY] * 2 + [VMEM] * 2 + [block((share_rows, feature), None, 0), ANY],
        [ANY] * len(shapes) + [VMEM] * 2,
        [
            pltpu.VMEM((entries, codewords), F32),
            pltpu.VMEM((entries, codewords), F32),
            pltpu.VMEM((listed, listed), jnp.int32),
            pltpu.VMEM((listed, listed), jnp.int32),
            pltpu.VMEM((LANES, codewords), F32),
            pltpu.VMEM((2, codewords, feature), BF16),
            pltpu.VMEM((2, entries, codewords), BF16),
            pltpu.VMEM((LOW, half), BF16),
            pltpu.VMEM((codewords, feature), F32),
            pltpu.VMEM((entries, feature), F32),
            pltpu.VMEM((2, entries, feature), BF16),
            pltpu.VMEM((codewords, entries), BF16),
            pltpu.VMEM((codewords // 2, rows_here + entries), BF16),
            pltpu.SemaphoreType.DMA((2,)),
            pltpu.SemaphoreType.DMA((len(shapes),)),
        ]
        + [pltpu.VMEM(shape, F32) for shape in shapes],
        40e9,
        "sums",
    )(me, gathered, vectors, fine_codes, *sums, first, second, fine_in, first_own)

    begun = {}
    for at in turns:
        away, other, kept = terms[3 * at : 3 * at + 3]
        got = exchange(away, 1)
        size = other.shape[0]
        begun[at] = (other + got[:size], kept + got[size:])

    outs = ()
    for at in turns:
        last_sums = scatter_sums(*begun[at], bits[at])
        cut = cuts[at]
        place = sum(cuts[:at]) // cut
        outs = local(
            lambda me_ref, *refs: final_kernel(share_rows, *refs[:6], *refs[-2:]),
            [(coarse_in.shape, F32), ((share_rows, feature), F32)],
            [
                block((owner_cells, cut), 0, place),
                block((share_rows, cut), None, place),
                block((groups, slot_count, cut), 0, 0, place),
                VMEM,
                block((share_rows, LANES), None, 0),
                block((listed, LANES), None, 0),
            ]
            + [ANY] * len(outs),
            [block((owner_cells, cut), 0, place), block((share_rows, cut), 0, place)],
            [],
            1e9,
            "outputs",
            {7 + number: number for number in range(len(outs))},
        )(me, coarse_in, fine_in, first_own, last_sums, code_info, entry_info, *outs)
    return tuple(outs)


def fits_dense(mesh_groups, listed, codewords, rows_here, feature):
    entries = mesh_groups * listed
    power = mesh_groups & (mesh_groups - 1) == 0 and mesh_groups >= 4
    digits = codewords % (2 * LOW) == 0 and (codewords // LOW) * listed <= LOW
    shapes = rows_here % (2 * LANES) == 0 and feature % (6 * LANES) == 0
    return power and digits and shapes and entries * codewords <= 2**20


def per_device(vectors, row_slot, fine_codes, cell_list, coarse_in, fine_in):
    groups = lax.axis_size("cell")
    dense = fits_dense(groups, cell_list.shape[1], *fine_in.shape[:1], *vectors.shape)
    plan = dense_plan if dense else routed_plan
    return plan(vectors, row_slot, fine_codes, cell_list, coarse_in, fine_in)


def solution(mesh):
    return jax.shard_map(
        per_device,
        mesh=mesh,
        in_specs=(
            P(("parts", "cell"), None),
            P(None, ("parts", "cell")),
            P(None, ("parts", "cell")),
            P(None, ("parts", "cell")),
            P("cell", None),
            P(),
        ),
        out_specs=(P(("parts", "cell"), None), P(("parts", "cell"), None)),
        check_vma=False,
    )
```

```python
import jax
import jax.numpy as jnp
from jax import lax
from jax.experimental import pallas as pl
from jax.experimental.pallas import tpu as pltpu
from jax.sharding import PartitionSpec as P


def code_tally(code_rows, codewords):
    return jax.ops.segment_sum(
        jnp.ones(code_rows.shape, jnp.float32), code_rows, num_segments=codewords
    )


def fine_update(code_term, totals_share, old_share, share_rows):
    part_sums = lax.psum_scatter(
        code_term(jnp.int32(0), lax.axis_size("cell") * share_rows),
        "cell",
        scatter_dimension=0,
        tiled=True,
    )
    return jnp.where(
        totals_share[:, None] > 0, part_sums / jnp.maximum(totals_share, 1.0)[:, None], old_share
    )


def routed_plan(vectors, row_slot, fine_codes, cell_list, coarse_in, fine_in):
    groups = lax.axis_size("cell")
    rows_here, feature = vectors.shape
    listed = cell_list.shape[1]
    slot_count = listed // groups
    owner_cells = coarse_in.shape[0]
    codewords = fine_in.shape[0]
    share_rows = codewords // groups
    share_start = lax.axis_index("cell") * share_rows
    fine_book = fine_in
    fine_share = lax.dynamic_slice_in_dim(fine_in, share_start, share_rows, 0)
    coarse = coarse_in
    list_iota = lax.iota(jnp.int32, listed)
    for sweep in range(2):
        code_totals = lax.psum(code_tally(fine_codes[sweep], codewords), "cell")
        slot_rows = row_slot[sweep]
        code_rows = fine_codes[sweep]
        picked = jnp.take(fine_book, code_rows, axis=0)
        residual = (vectors.astype(jnp.float32) - picked).astype(jnp.bfloat16)
        slot_hot = (slot_rows[None, :] == list_iota[:, None]).astype(jnp.bfloat16)
        slot_sums = jnp.dot(slot_hot, residual, preferred_element_type=jnp.float32)
        slot_counts = jnp.sum(slot_hot, axis=1, dtype=jnp.float32)
        slot_cells = cell_list[sweep].astype(jnp.float32)
        got_sums, got_counts, got_cells = (
            lax.all_to_all(
                slot_sums.reshape(groups, slot_count, feature),
                "cell",
                split_axis=0,
                concat_axis=0,
                tiled=True,
            ),
            lax.all_to_all(
                slot_counts.reshape(groups, slot_count),
                "cell",
                split_axis=0,
                concat_axis=0,
                tiled=True,
            ),
            lax.all_to_all(
                slot_cells.reshape(groups, slot_count),
                "cell",
                split_axis=0,
                concat_axis=0,
                tiled=True,
            ),
        )
        flat_cells = got_cells.reshape(groups * slot_count).astype(jnp.int32)
        cell_sums = jax.ops.segment_sum(
            got_sums.reshape(groups * slot_count, feature), flat_cells, num_segments=owner_cells
        )
        cell_counts = jax.ops.segment_sum(
            got_counts.reshape(groups * slot_count), flat_cells, num_segments=owner_cells
        )
        coarse = jnp.where(
            cell_counts[:, None] > 0, cell_sums / jnp.maximum(cell_counts, 1.0)[:, None], coarse
        )
        returned_rows = jnp.take(coarse, flat_cells, axis=0).reshape(groups, slot_count, feature)
        arrived = lax.all_to_all(returned_rows, "cell", split_axis=0, concat_axis=0, tiled=True)
        entry_centers = arrived.reshape(listed, feature)
        row_centers = jnp.take(entry_centers, slot_rows, axis=0)
        fine_residual = (vectors.astype(jnp.float32) - row_centers).astype(jnp.bfloat16)

        def code_term(start, count, code_rows=code_rows, fine_residual=fine_residual):
            wanted = start + lax.iota(jnp.int32, count)
            code_hot = (code_rows[None, :] == wanted[:, None]).astype(jnp.bfloat16)
            return jnp.dot(code_hot, fine_residual, preferred_element_type=jnp.float32)

        totals_share = lax.dynamic_slice_in_dim(code_totals, share_start, share_rows, 0)
        if sweep == 0:
            full_sums = lax.psum(code_term(0, codewords), "cell")
            fine_book = jnp.where(
                code_totals[:, None] > 0,
                full_sums / jnp.maximum(code_totals, 1.0)[:, None],
                fine_book,
            )
            fine_share = lax.dynamic_slice_in_dim(fine_book, share_start, share_rows, 0)
        else:
            fine_share = fine_update(code_term, totals_share, fine_share, share_rows)
    return (coarse, fine_share)


F32 = jnp.float32
BF16 = jnp.bfloat16
LOW = 256
LANES = 128
PARAMS = pltpu.CompilerParams(vmem_limit_bytes=58 * 2**20)
VMEM = pl.BlockSpec(memory_space=pltpu.VMEM)
SMEM = pl.BlockSpec(memory_space=pltpu.SMEM)
ANY = pl.BlockSpec(memory_space=pl.ANY)


def iota(shape, axis):
    return lax.broadcasted_iota(jnp.int32, shape, axis)


def matmul(left, right):
    return jnp.dot(left, right, preferred_element_type=F32)


def matmul_nt(left, right):
    return lax.dot_general(left, right, (((1,), (1,)), ((), ())), preferred_element_type=F32)


def split(values):
    high = values.astype(BF16)
    return high, (values - high.astype(F32)).astype(BF16)


def hot_rows(codes, rows=LOW):
    inside = jnp.where((codes >= 0) & (codes < rows), codes, -1)
    inside = inside.astype(F32).astype(BF16)
    row = iota((rows, codes.shape[1]), 0).astype(F32).astype(BF16)
    return jnp.where(row == inside, jnp.ones((), BF16), jnp.zeros((), BF16))


def pair_block(codes, slots, listed, high):
    left = hot_rows((codes >> 8) * listed + slots, high * listed)
    return matmul_nt(left, hot_rows(codes & (LOW - 1)))


def pack_kernel(fine_codes, row_slot, cell_list, packed):
    half = fine_codes.shape[1] // 2
    listed = cell_list.shape[1]
    packed[:, half:] = jnp.zeros((8, LANES), jnp.int32)
    for number, ref in enumerate((fine_codes, row_slot)):
        for sweep in range(2):
            for part in range(2):
                row = 4 * number + 2 * sweep + part
                packed[row : row + 1, :half] = ref[
                    sweep : sweep + 1, part * half : (part + 1) * half
                ]
    packed[0:2, half : half + listed] = cell_list[...]


def own_cells_kernel(
    groups, listed, me_ref, vectors, fine_codes, row_slot, fine_in, first_ref, second_ref, to_ref
):
    high = fine_in.shape[0] // LOW
    first = matmul(hot_rows(row_slot[0:1, :], listed), vectors[...])
    second_ref[...] = matmul(hot_rows(row_slot[1:2, :], listed), vectors[...])
    pairs = pair_block(fine_codes[0:1, :], row_slot[0:1, :], listed, high)
    for digit in range(high):
        pairs_high, pairs_low = split(pairs[digit * listed : (digit + 1) * listed])
        both = jnp.concatenate([pairs_high, pairs_low], axis=0)
        book = fine_in[digit * LOW : (digit + 1) * LOW, :]
        book_high, book_low = split(book)
        taken = matmul(both, book_high) + matmul(both, book_low)
        first = first - taken[:listed] - taken[listed:]
    first_ref[...] = first
    slots = listed // groups
    top = groups.bit_length() - 1
    for owner in range(groups):
        block = owner ^ me_ref[0]
        at = sum((1 - (block >> bit & 1)) << (top - 1 - bit) for bit in range(top))
        to_ref[at, 0] = first[owner * slots : (owner + 1) * slots]


def own_codes_kernel(base, vectors, fine_codes, _, sums_ref):
    codes = fine_codes[0:1, :] - base
    for start in range(0, sums_ref.shape[0], 2 * LOW):
        hot = jnp.concatenate(
            [hot_rows(codes - start), hot_rows(codes - start - LOW)], axis=0
        )
        sums_ref[start : start + 2 * LOW, :] = matmul(hot, vectors[...])


def position(block, groups):
    return (block & 1) * (groups // 2) + (block >> 1 & 1) * (groups // 4) + (block >> 2)


def sums_kernel(
    groups,
    slot_count,
    owner_cells,
    cuts,
    orders,
    me_ref,
    codes_ref,
    vectors,
    fine_codes,
    low_sums_ref,
    high_sums_ref,
    first_ref,
    second_ref,
    share_ref,
    *refs,
):
    out_refs, refs = refs[: 3 * len(cuts)], refs[3 * len(cuts) :]
    code_info_ref, entry_info_ref, refs = refs[0], refs[1], refs[2:]
    table0, table1, cell0, cell1, wide, terms, permuted, rows_hot = refs[:8]
    fine, bracket, centers_ref, pairs_ref, left = refs[8:13]
    in_sem, out_sem, stages = refs[13], refs[14], refs[15:]
    me = me_ref[0]
    codewords, feature = fine.shape
    listed = groups * slot_count
    entries = groups * listed
    high = codewords // LOW
    half = codes_ref.shape[2] - LANES
    share_rows = share_ref.shape[0]

    loads = [
        pltpu.make_async_copy(
            ref, fine.at[pl.ds(at * (codewords // 2), codewords // 2)], in_sem.at[at]
        )
        for at, ref in enumerate((low_sums_ref, high_sums_ref))
    ]
    for load in loads:
        load.start()

    rows_hot[...] = iota(rows_hot.shape, 0).astype(F32).astype(BF16)
    one, zero = jnp.ones((), BF16), jnp.zeros((), BF16)

    def hot(codes):
        return jnp.where(rows_hot[...] == codes.astype(F32).astype(BF16), one, zero)

    def device_tables(device, carry):
        at = position(device ^ me, groups)
        for sweep, table in enumerate((table0, table1)):
            block = jnp.zeros((high * listed, LOW), F32)
            for part in range(2):
                row = 2 * sweep + part
                codes = codes_ref[at, row : row + 1, :half]
                slots = codes_ref[at, row + 4 : row + 5, :half]
                block = block + matmul_nt(
                    hot((codes >> 8) * listed + slots)[: high * listed], hot(codes & (LOW - 1))
                )
            rows = pl.ds(pl.multiple_of(device * listed, listed), listed)
            for digit in range(high):
                table[rows, digit * LOW : (digit + 1) * LOW] = block[
                    digit * listed : (digit + 1) * listed
                ]
        return carry

    lax.fori_loop(0, groups, device_tables, 0)
    for device in range(groups):
        at = position(device ^ me, groups)
        for sweep, cell in enumerate((cell0, cell1)):
            row = codes_ref[at, sweep : sweep + 1, half : half + listed]
            cell[device * slot_count : (device + 1) * slot_count, :] = jnp.broadcast_to(
                row, (slot_count, listed)
            )

    row_at = iota((entries, listed), 0)
    owner_of = row_at // listed
    slot_of = owner_of * slot_count + row_at % slot_count
    is_slot = slot_of == iota((entries, listed), 1)
    device_of = (row_at // slot_count) % groups

    def entry_cells(cell):
        tiled = jnp.concatenate([cell[...]] * groups, axis=0)
        picked = jnp.sum(jnp.where(is_slot, tiled, 0), axis=1, keepdims=True)
        return picked.astype(F32)

    owner_col = owner_of[:, :1].astype(F32)
    cells = [entry_cells(cell0), entry_cells(cell1)]
    names = [cell + owner_col * float(owner_cells) for cell in cells]

    entry_row = iota((entries, entries), 0)
    natural = (
        ((entry_row // slot_count) % groups) * listed
        + (entry_row // listed) * slot_count
        + entry_row % slot_count
    )
    order = (natural == iota((entries, entries), 1)).astype(BF16)
    code_counts = [jnp.sum(table[...], axis=0, keepdims=True) for table in (table0, table1)]
    entry_counts = []
    for table in (table0, table1):
        count_high, count_low = split(
            jnp.broadcast_to(jnp.sum(table[...], axis=1, keepdims=True), (entries, LANES))
        )
        entry_counts.append(matmul(order, count_high) + matmul(order, count_low))
    most = jnp.maximum(jnp.max(table0[...]), jnp.max(table1[...]))
    large = most > LOW
    for digit in range(high):
        columns = slice(digit * LOW, (digit + 1) * LOW)
        permuted[0, :, columns] = matmul(order, table1[:, columns].astype(BF16)).astype(BF16)

    @pl.when(large)
    def _():
        for digit in range(high):
            columns = slice(digit * LOW, (digit + 1) * LOW)
            rest = split(table1[:, columns])[1]
            permuted[1, :, columns] = matmul(order, rest).astype(BF16)

    own_row = codes_ref[0, 0:1, half : half + listed].astype(F32)
    own_row = own_row + (iota((1, listed), 1) // slot_count).astype(F32) * float(owner_cells)
    match = (names[0] == own_row).astype(BF16)
    match = lax.dot_general(match, order, (((0,), (0,)), ((), ())), preferred_element_type=F32)
    match = match.astype(BF16)
    held = jnp.zeros((listed, 1), F32)
    for digit in range(high):
        columns = slice(digit * LOW, (digit + 1) * LOW)
        table_high, table_low = split(table0[:, columns])
        used = matmul(match, table_high) + matmul(match, table_low)
        held = held + jnp.sum(used, axis=1, keepdims=True)
        used_high, used_low = split(used)
        wide[0:listed, columns] = used_high.astype(F32)
        wide[listed : 2 * listed, columns] = used_low.astype(F32)
    wide[2 * listed : 2 * listed + 8, :] = jnp.broadcast_to(code_counts[0], (8, codewords))
    wide[2 * listed + 8 : 2 * listed + 16, :] = jnp.broadcast_to(code_counts[1], (8, codewords))
    wide[2 * listed + 16 :, :] = jnp.zeros((LANES - 2 * listed - 16, codewords), F32)
    center_high, center_low = split(first_ref[...] / jnp.maximum(held, 1.0))
    blank = jnp.zeros((LANES - 2 * listed, feature), BF16)
    center_high = jnp.concatenate([center_high, center_high, blank], axis=0)
    center_low = jnp.concatenate([center_low, center_low, blank], axis=0)
    for load in loads:
        load.wait()
    for digit in range(high):
        rows = slice(digit * LOW, (digit + 1) * LOW)
        columns = wide[:, rows].T
        code_info_ref[rows, :] = columns
        taken = jnp.where(iota((LOW, LANES), 1) < 2 * listed, columns, 0.0).astype(BF16)
        first_fine = fine[rows, :] - (matmul(taken, center_high) + matmul(taken, center_low))
        scaled = first_fine / jnp.maximum(columns[:, 2 * listed : 2 * listed + 1], 1.0)
        terms[0, rows, :], terms[1, rows, :] = split(scaled)
        fine[rows, :] = jnp.where(
            columns[:, 2 * listed + 8 : 2 * listed + 9] > 0, 0.0, first_fine
        )
    mine = pl.ds(pl.multiple_of(me * share_rows, share_rows), share_rows)
    empty = code_info_ref[mine, 2 * listed : 2 * listed + 1] == 0
    for part, share in enumerate(split(share_ref[...])):
        terms[part, mine, :] = jnp.where(
            empty, share.astype(F32), terms[part, mine, :].astype(F32)
        ).astype(BF16)

    own_entry = (is_slot & (device_of == me)).astype(BF16)
    second_high, second_low = split(second_ref[...])
    bracket[...] = (
        matmul(own_entry, second_high)
        + matmul(own_entry, second_low)
        - matmul(permuted[0], terms[0])
        - matmul(permuted[0], terms[1])
    )

    @pl.when(large)
    def _():
        bracket[...] -= matmul(permuted[1], terms[0])

    same = (
        jnp.broadcast_to(names[1], (entries, entries))
        == jnp.broadcast_to(names[1], (entries, LANES)).T[0:1, :]
    ).astype(BF16)
    total_high, total_low = split(entry_counts[1])
    totals = matmul(same, total_high) + matmul(same, total_low)
    bracket_high, bracket_low = split(bracket[...])
    centers = matmul(same, bracket_high) + matmul(same, bracket_low)
    centers = centers / jnp.maximum(totals[:, :1], 1.0)
    centers_ref[0], centers_ref[1] = split(centers)
    lane = iota((entries, LANES), 1)
    info = jnp.where(lane == 0, entry_counts[0], entry_counts[1])
    info = jnp.where(lane == 2, cells[0], info)
    entry_info_ref[...] = jnp.where(lane == 3, cells[1], info)

    eye = (iota((LOW, LOW), 0) == iota((LOW, LOW), 1)).astype(BF16)
    for digit in range(high):
        rows = slice(digit * LOW, (digit + 1) * LOW)
        pairs_ref[rows, :] = -matmul_nt(eye, permuted[0, :, rows]).astype(BF16)
    rows_here = vectors.shape[0]
    codes = fine_codes[1:2, :]
    copies = []
    for odd in (1, 0):
        blocks = [at for at in range(groups) if at % 2 == odd]
        for at, block in enumerate(blocks):
            owner = me ^ block
            rows = pl.ds(pl.multiple_of(owner * share_rows, share_rows), share_rows)
            to = slice(at * share_rows, (at + 1) * share_rows)
            left[to, :rows_here] = hot_rows(codes - owner * share_rows, share_rows)
            left[to, rows_here:] = pairs_ref[rows, :]
        start = 0
        for chunk, cut in enumerate(cuts):
            columns = slice(start, start + cut)
            start += cut
            sums = (
                matmul(left[:, :rows_here], vectors[:, columns])
                + matmul(left[:, rows_here:], centers_ref[0, :, columns])
                + matmul(left[:, rows_here:], centers_ref[1, :, columns])
            )
            for part, order_of in enumerate(orders[chunk]):
                if order_of[0] % 2 != odd:
                    continue
                number = 3 * chunk + part
                stage = stages[number]
                for to, block in enumerate(order_of):
                    owner = me ^ block
                    rows = pl.ds(pl.multiple_of(owner * share_rows, share_rows), share_rows)
                    cell_rows = pl.ds(pl.multiple_of(owner * listed, listed), listed)
                    at = blocks.index(block) * share_rows
                    stage[to, :share_rows, :] = sums[at : at + share_rows] + fine[rows, columns]
                    stage[to, share_rows:, :] = bracket[cell_rows, columns]

                @pl.when(large)
                def _():
                    for to, block in enumerate(order_of):
                        owner = me ^ block
                        rows = pl.ds(pl.multiple_of(owner * share_rows, share_rows), share_rows)
                        rest = lax.dot_general(
                            permuted[1, :, rows],
                            centers_ref[0, :, columns],
                            (((0,), (0,)), ((), ())),
                            preferred_element_type=F32,
                        )
                        stage[to, :share_rows, :] -= rest

                copy = pltpu.make_async_copy(stage, out_refs[number], out_sem.at[number])
                copy.start()
                copies.append(copy)
    for copy in copies:
        copy.wait()


def final_kernel(
    groups,
    slot_count,
    share_rows,
    me_ref,
    coarse_in,
    fine_share,
    first_sums,
    last_sums,
    code_info,
    entry_info,
    coarse_out,
    fine_out,
    own_first,
):
    listed = entry_info.shape[0]
    owner_cells, cut = coarse_in.shape
    by_lane = entry_info[...].T
    info = [by_lane[at : at + 1, :] for at in range(4)]
    coarse = coarse_in[...]
    for device in range(groups):
        rows = slice(device * slot_count, (device + 1) * slot_count)
        own_first[rows, :] = first_sums[device ^ me_ref[0]]
    for sweep, sums in enumerate((own_first[...], last_sums[share_rows:, :])):
        cell = info[2 + sweep].astype(jnp.int32)
        hit = iota((owner_cells, listed), 0) == cell
        counts = jnp.sum(jnp.where(hit, info[sweep], 0.0), axis=1, keepdims=True)
        picks = hit.astype(BF16)
        sums_high, sums_low = split(sums)
        found = matmul(picks, sums_high) + matmul(picks, sums_low)
        coarse = jnp.where(counts > 0, found / jnp.maximum(counts, 1.0), coarse)
    coarse_out[...] = coarse
    first_count = code_info[:, 2 * listed : 2 * listed + 1]
    last_count = code_info[:, 2 * listed + 8 : 2 * listed + 9]
    count = jnp.where(last_count > 0, last_count, first_count)
    fine_out[...] = jnp.where(
        count > 0, last_sums[:share_rows, :] / jnp.maximum(count, 1.0), fine_share[...]
    )


def exchange(values, step):
    groups = lax.axis_size("cell")
    return lax.ppermute(values, "cell", [(at, at ^ step) for at in range(groups)])


def block_order(bits):
    order = [0]
    for bit in list(bits)[::-1]:
        order = [block + (1 << bit) for block in order] + order
    return order


def block_orders(bits):
    order = block_order(bits)
    half = len(order) // 2
    return [block + 1 for block in order], order[:half], order[half:]


def after(values, *others):
    return lax.optimization_barrier((values, *others))[0]


def halved(got, other, kept):
    half = other.shape[0]
    return other + got[:half], kept + got[half:]


def swap(blocks, bit):
    half = blocks.shape[0] // 2
    got = exchange(blocks[:half], 1 << bit)
    return jnp.concatenate([blocks[half:], got], axis=1)


def local(kernel, shapes, in_specs, out_specs, scratch, flops, name, aliases=None):
    return pl.pallas_call(
        kernel,
        out_shape=tuple(jax.ShapeDtypeStruct(shape, dtype) for shape, dtype in shapes),
        grid_spec=pltpu.PrefetchScalarGridSpec(
            num_scalar_prefetch=1,
            grid=(1,),
            in_specs=in_specs,
            out_specs=out_specs,
            scratch_shapes=scratch,
        ),
        input_output_aliases=aliases or {},
        compiler_params=PARAMS,
        cost_estimate=pl.CostEstimate(
            flops=int(flops), bytes_accessed=10**6, transcendentals=0
        ),
        name=name,
    )


def block(shape, *place):
    return pl.BlockSpec(
        shape, lambda step, me: tuple(me[0] if at is None else at for at in place)
    )


def dense_plan(vectors, row_slot, fine_codes, cell_list, coarse_in, fine_in):
    groups = lax.axis_size("cell")
    rows_here, feature = vectors.shape
    listed = cell_list.shape[1]
    slot_count = listed // groups
    owner_cells = coarse_in.shape[0]
    codewords = fine_in.shape[0]
    share_rows = codewords // groups
    entries = groups * listed
    half = rows_here // 2
    me = lax.axis_index("cell").reshape(1).astype(jnp.int32)

    packed = local(
        lambda me_ref, *refs: pack_kernel(*refs),
        [((8, half + LANES), jnp.int32)],
        [VMEM] * 3,
        [VMEM],
        [],
        1e9,
        "pack",
    )(me, fine_codes, row_slot, cell_list)[0]
    first, second, first_to = local(
        lambda *refs: own_cells_kernel(groups, listed, *refs),
        [((listed, feature), F32)] * 2 + [((groups, 1, slot_count, feature), F32)],
        [VMEM] * 4,
        [VMEM] * 3,
        [],
        5e9,
        "own_cells",
    )(me, vectors, fine_codes, row_slot, fine_in)
    far = groups // 4
    gathered = jnp.stack([packed] + [exchange(packed, 4 * step) for step in range(1, far)])
    sums = []
    for step, base in ((2, 0), (1, codewords // 2)):
        sums += local(
            lambda me_ref, *refs, base=base: own_codes_kernel(base, *refs),
            [((codewords // 2, feature), F32)],
            [VMEM, VMEM, ANY],
            [VMEM],
            [],
            6e9,
            "own_codes",
        )(me, vectors, fine_codes, gathered)
        gathered = jnp.concatenate([gathered, exchange(gathered, step)])

    top = groups.bit_length() - 1
    near_first = list(range(1, top))
    far_first = near_first[1:] + near_first[:1]
    cuts = [feature // 3, feature // 6, feature // 6, feature // 3]
    bits = [near_first, far_first, near_first, near_first]
    turns = [0, 1, 3, 2]
    orders = [block_orders(each) for each in bits]
    shapes = [
        (len(order), share_rows + listed, cut)
        for cut, three in zip(cuts, orders)
        for order in three
    ]
    *terms, code_info, entry_info = local(
        lambda *refs: sums_kernel(groups, slot_count, owner_cells, cuts, orders, *refs),
        [(shape, F32) for shape in shapes]
        + [((codewords, LANES), F32), ((entries, LANES), F32)],
        [VMEM] * 3 + [ANY] * 2 + [VMEM] * 2 + [block((share_rows, feature), None, 0)],
        [ANY] * len(shapes) + [VMEM] * 2,
        [
            pltpu.VMEM((entries, codewords), F32),
            pltpu.VMEM((entries, codewords), F32),
            pltpu.VMEM((listed, listed), jnp.int32),
            pltpu.VMEM((listed, listed), jnp.int32),
            pltpu.VMEM((LANES, codewords), F32),
            pltpu.VMEM((2, codewords, feature), BF16),
            pltpu.VMEM((2, entries, codewords), BF16),
            pltpu.VMEM((LOW, half), BF16),
            pltpu.VMEM((codewords, feature), F32),
            pltpu.VMEM((entries, feature), F32),
            pltpu.VMEM((2, entries, feature), BF16),
            pltpu.VMEM((codewords, entries), BF16),
            pltpu.VMEM((codewords // 2, rows_here + entries), BF16),
            pltpu.SemaphoreType.DMA((2,)),
            pltpu.SemaphoreType.DMA((len(shapes),)),
        ]
        + [pltpu.VMEM(shape, F32) for shape in shapes],
        40e9,
        "sums",
    )(me, gathered, vectors, fine_codes, *sums, first, second, fine_in)

    away, other, kept = zip(*(terms[3 * at : 3 * at + 3] for at in range(len(cuts))))

    def step(at, state, *others):
        bit, (leave, *stay) = state[0][0], state[1]
        got = exchange(after(leave, *others) if others else leave, 1 << bit)
        if len(stay) == 2:
            return state[0][1:], halved(got, *stay)
        stay = stay[0]
        if stay.shape[0] == 1:
            return (), (stay + got,)
        half = stay.shape[0] // 2
        return state[0][1:], (stay[:half] + got[:half], stay[half:] + got[half:])

    a0, b0, a2, a1 = ([(0, *bits[at]), (away[at], other[at], kept[at])] for at in range(4))
    a0 = step(0, a0)
    b0 = step(1, b0, a0[1][0])
    a1 = step(3, a1, b0[1][0])
    a2 = step(2, a2, b0[1][0])
    a0_near = step(0, a0)
    b0 = step(1, b0)
    first_to = swap(after(first_to, a0[1][0]), 0)
    first_to = swap(first_to, 1)
    a1_near = step(3, a1, a0_near[1][0])
    a0 = step(0, a0_near, a1[1][0], a2[1][0], b0[1][0])
    b0 = step(1, b0)
    b0 = step(1, b0)
    for bit in range(2, top):
        first_to = swap(after(first_to, a0[1][0]), bit)
    first_own = first_to[0]
    a2 = step(2, a2, a1_near[1][0])
    a0 = step(0, a0)
    a1 = step(3, a1_near)
    a1 = step(3, a1)
    a2 = step(2, a2)
    a2 = step(2, a2)
    outs = ()
    for at, done in ((0, a0), (1, b0), (3, a1), (2, a2)):
        last_sums = done[1][0][0]
        cut = cuts[at]
        place = sum(cuts[:at]) // cut
        outs = local(
            lambda me_ref, *refs: final_kernel(
                groups, slot_count, share_rows, me_ref, *refs[:6], *refs[-3:]
            ),
            [(coarse_in.shape, F32), ((share_rows, feature), F32)],
            [
                block((owner_cells, cut), 0, place),
                block((share_rows, cut), None, place),
                block((groups, slot_count, cut), 0, 0, place),
                VMEM,
                block((share_rows, LANES), None, 0),
                block((listed, LANES), None, 0),
            ]
            + [ANY] * len(outs),
            [block((owner_cells, cut), 0, place), block((share_rows, cut), 0, place)],
            [pltpu.VMEM((listed, cut), F32)],
            1e9,
            "outputs",
            {7 + number: number for number in range(len(outs))},
        )(me, coarse_in, fine_in, first_own, last_sums, code_info, entry_info, *outs)
    return tuple(outs)


def fits_dense(mesh_groups, listed, codewords, rows_here, feature):
    entries = mesh_groups * listed
    power = mesh_groups & (mesh_groups - 1) == 0 and mesh_groups >= 4
    digits = codewords % (2 * LOW) == 0 and (codewords // LOW) * listed <= LOW
    shapes = rows_here % (2 * LANES) == 0 and feature % (6 * LANES) == 0
    return power and digits and shapes and entries * codewords <= 2**20


def per_device(vectors, row_slot, fine_codes, cell_list, coarse_in, fine_in):
    groups = lax.axis_size("cell")
    dense = fits_dense(groups, cell_list.shape[1], *fine_in.shape[:1], *vectors.shape)
    plan = dense_plan if dense else routed_plan
    return plan(vectors, row_slot, fine_codes, cell_list, coarse_in, fine_in)


def solution(mesh):
    return jax.shard_map(
        per_device,
        mesh=mesh,
        in_specs=(
            P(("parts", "cell"), None),
            P(None, ("parts", "cell")),
            P(None, ("parts", "cell")),
            P(None, ("parts", "cell")),
            P("cell", None),
            P(),
        ),
        out_specs=(P(("parts", "cell"), None), P(("parts", "cell"), None)),
        check_vma=False,
    )
```

```python
import jax
import jax.numpy as jnp
from jax import lax
from jax.experimental import pallas as pl
from jax.experimental.pallas import tpu as pltpu
from jax.sharding import PartitionSpec as P


def code_tally(code_rows, codewords):
    return jax.ops.segment_sum(
        jnp.ones(code_rows.shape, jnp.float32), code_rows, num_segments=codewords
    )


def fine_update(code_term, totals_share, old_share, share_rows):
    part_sums = lax.psum_scatter(
        code_term(jnp.int32(0), lax.axis_size("cell") * share_rows),
        "cell",
        scatter_dimension=0,
        tiled=True,
    )
    return jnp.where(
        totals_share[:, None] > 0, part_sums / jnp.maximum(totals_share, 1.0)[:, None], old_share
    )


def routed_plan(vectors, row_slot, fine_codes, cell_list, coarse_in, fine_in):
    groups = lax.axis_size("cell")
    rows_here, feature = vectors.shape
    listed = cell_list.shape[1]
    slot_count = listed // groups
    owner_cells = coarse_in.shape[0]
    codewords = fine_in.shape[0]
    share_rows = codewords // groups
    share_start = lax.axis_index("cell") * share_rows
    fine_book = fine_in
    fine_share = lax.dynamic_slice_in_dim(fine_in, share_start, share_rows, 0)
    coarse = coarse_in
    list_iota = lax.iota(jnp.int32, listed)
    for sweep in range(2):
        code_totals = lax.psum(code_tally(fine_codes[sweep], codewords), "cell")
        slot_rows = row_slot[sweep]
        code_rows = fine_codes[sweep]
        picked = jnp.take(fine_book, code_rows, axis=0)
        residual = (vectors.astype(jnp.float32) - picked).astype(jnp.bfloat16)
        slot_hot = (slot_rows[None, :] == list_iota[:, None]).astype(jnp.bfloat16)
        slot_sums = jnp.dot(slot_hot, residual, preferred_element_type=jnp.float32)
        slot_counts = jnp.sum(slot_hot, axis=1, dtype=jnp.float32)
        slot_cells = cell_list[sweep].astype(jnp.float32)
        got_sums, got_counts, got_cells = (
            lax.all_to_all(
                slot_sums.reshape(groups, slot_count, feature),
                "cell",
                split_axis=0,
                concat_axis=0,
                tiled=True,
            ),
            lax.all_to_all(
                slot_counts.reshape(groups, slot_count),
                "cell",
                split_axis=0,
                concat_axis=0,
                tiled=True,
            ),
            lax.all_to_all(
                slot_cells.reshape(groups, slot_count),
                "cell",
                split_axis=0,
                concat_axis=0,
                tiled=True,
            ),
        )
        flat_cells = got_cells.reshape(groups * slot_count).astype(jnp.int32)
        cell_sums = jax.ops.segment_sum(
            got_sums.reshape(groups * slot_count, feature), flat_cells, num_segments=owner_cells
        )
        cell_counts = jax.ops.segment_sum(
            got_counts.reshape(groups * slot_count), flat_cells, num_segments=owner_cells
        )
        coarse = jnp.where(
            cell_counts[:, None] > 0, cell_sums / jnp.maximum(cell_counts, 1.0)[:, None], coarse
        )
        returned_rows = jnp.take(coarse, flat_cells, axis=0).reshape(groups, slot_count, feature)
        arrived = lax.all_to_all(returned_rows, "cell", split_axis=0, concat_axis=0, tiled=True)
        entry_centers = arrived.reshape(listed, feature)
        row_centers = jnp.take(entry_centers, slot_rows, axis=0)
        fine_residual = (vectors.astype(jnp.float32) - row_centers).astype(jnp.bfloat16)

        def code_term(start, count, code_rows=code_rows, fine_residual=fine_residual):
            wanted = start + lax.iota(jnp.int32, count)
            code_hot = (code_rows[None, :] == wanted[:, None]).astype(jnp.bfloat16)
            return jnp.dot(code_hot, fine_residual, preferred_element_type=jnp.float32)

        totals_share = lax.dynamic_slice_in_dim(code_totals, share_start, share_rows, 0)
        if sweep == 0:
            full_sums = lax.psum(code_term(0, codewords), "cell")
            fine_book = jnp.where(
                code_totals[:, None] > 0,
                full_sums / jnp.maximum(code_totals, 1.0)[:, None],
                fine_book,
            )
            fine_share = lax.dynamic_slice_in_dim(fine_book, share_start, share_rows, 0)
        else:
            fine_share = fine_update(code_term, totals_share, fine_share, share_rows)
    return (coarse, fine_share)


F32 = jnp.float32
BF16 = jnp.bfloat16
LOW = 256
LANES = 128
PARAMS = pltpu.CompilerParams(vmem_limit_bytes=58 * 2**20)
VMEM = pl.BlockSpec(memory_space=pltpu.VMEM)
SMEM = pl.BlockSpec(memory_space=pltpu.SMEM)
ANY = pl.BlockSpec(memory_space=pl.ANY)


def iota(shape, axis):
    return lax.broadcasted_iota(jnp.int32, shape, axis)


def matmul(left, right):
    return jnp.dot(left, right, preferred_element_type=F32)


def matmul_nt(left, right):
    return lax.dot_general(left, right, (((1,), (1,)), ((), ())), preferred_element_type=F32)


def split(values):
    high = values.astype(BF16)
    return high, (values - high.astype(F32)).astype(BF16)


def hot_rows(codes, rows=LOW):
    inside = jnp.where((codes >= 0) & (codes < rows), codes, -1)
    inside = inside.astype(F32).astype(BF16)
    row = iota((rows, codes.shape[1]), 0).astype(F32).astype(BF16)
    return jnp.where(row == inside, jnp.ones((), BF16), jnp.zeros((), BF16))


def pair_block(codes, slots, listed, high):
    left = hot_rows((codes >> 8) * listed + slots, high * listed)
    return matmul_nt(left, hot_rows(codes & (LOW - 1)))


def pack_kernel(fine_codes, row_slot, cell_list, packed):
    half = fine_codes.shape[1] // 2
    listed = cell_list.shape[1]
    packed[:, half:] = jnp.zeros((8, LANES), jnp.int32)
    for number, ref in enumerate((fine_codes, row_slot)):
        for sweep in range(2):
            for part in range(2):
                row = 4 * number + 2 * sweep + part
                packed[row : row + 1, :half] = ref[
                    sweep : sweep + 1, part * half : (part + 1) * half
                ]
    packed[0:2, half : half + listed] = cell_list[...]


def own_cells_kernel(
    groups, listed, me_ref, vectors, fine_codes, row_slot, fine_in, first_ref, second_ref, to_ref
):
    high = fine_in.shape[0] // LOW
    first = matmul(hot_rows(row_slot[0:1, :], listed), vectors[...])
    second_ref[...] = matmul(hot_rows(row_slot[1:2, :], listed), vectors[...])
    pairs = pair_block(fine_codes[0:1, :], row_slot[0:1, :], listed, high)
    for digit in range(high):
        pairs_high, pairs_low = split(pairs[digit * listed : (digit + 1) * listed])
        both = jnp.concatenate([pairs_high, pairs_low], axis=0)
        book = fine_in[digit * LOW : (digit + 1) * LOW, :]
        book_high, book_low = split(book)
        taken = matmul(both, book_high) + matmul(both, book_low)
        first = first - taken[:listed] - taken[listed:]
    first_ref[...] = first
    slots = listed // groups
    top = groups.bit_length() - 1
    for owner in range(groups):
        block = owner ^ me_ref[0]
        at = sum((1 - (block >> bit & 1)) << (top - 1 - bit) for bit in range(top))
        to_ref[at, 0] = first[owner * slots : (owner + 1) * slots]


def own_codes_kernel(base, vectors, fine_codes, _, sums_ref):
    codes = fine_codes[0:1, :] - base
    for start in range(0, sums_ref.shape[0], 2 * LOW):
        hot = jnp.concatenate(
            [hot_rows(codes - start), hot_rows(codes - start - LOW)], axis=0
        )
        sums_ref[start : start + 2 * LOW, :] = matmul(hot, vectors[...])


def position(block, groups):
    return (block & 1) * (groups // 2) + (block >> 1 & 1) * (groups // 4) + (block >> 2)


def sums_kernel(
    groups,
    slot_count,
    owner_cells,
    cuts,
    orders,
    me_ref,
    codes_ref,
    vectors,
    fine_codes,
    low_sums_ref,
    high_sums_ref,
    first_ref,
    second_ref,
    share_ref,
    *refs,
):
    out_refs, refs = refs[: 3 * len(cuts)], refs[3 * len(cuts) :]
    code_info_ref, entry_info_ref, refs = refs[0], refs[1], refs[2:]
    table0, table1, cell0, cell1, wide, terms, permuted, rows_hot = refs[:8]
    fine, bracket, centers_ref, pairs_ref, left = refs[8:13]
    in_sem, out_sem, stages = refs[13], refs[14], refs[15:]
    me = me_ref[0]
    codewords, feature = fine.shape
    listed = groups * slot_count
    entries = groups * listed
    high = codewords // LOW
    half = codes_ref.shape[2] - LANES
    share_rows = share_ref.shape[0]

    loads = [
        pltpu.make_async_copy(
            ref, fine.at[pl.ds(at * (codewords // 2), codewords // 2)], in_sem.at[at]
        )
        for at, ref in enumerate((low_sums_ref, high_sums_ref))
    ]
    for load in loads:
        load.start()

    rows_hot[...] = iota(rows_hot.shape, 0).astype(F32).astype(BF16)
    one, zero = jnp.ones((), BF16), jnp.zeros((), BF16)

    def hot(codes):
        return jnp.where(rows_hot[...] == codes.astype(F32).astype(BF16), one, zero)

    def device_tables(device, carry):
        at = position(device ^ me, groups)
        for sweep, table in enumerate((table0, table1)):
            block = jnp.zeros((high * listed, LOW), F32)
            for part in range(2):
                row = 2 * sweep + part
                codes = codes_ref[at, row : row + 1, :half]
                slots = codes_ref[at, row + 4 : row + 5, :half]
                block = block + matmul_nt(
                    hot((codes >> 8) * listed + slots)[: high * listed], hot(codes & (LOW - 1))
                )
            rows = pl.ds(pl.multiple_of(device * listed, listed), listed)
            for digit in range(high):
                table[rows, digit * LOW : (digit + 1) * LOW] = block[
                    digit * listed : (digit + 1) * listed
                ]
        return carry

    lax.fori_loop(0, groups, device_tables, 0)
    for device in range(groups):
        at = position(device ^ me, groups)
        for sweep, cell in enumerate((cell0, cell1)):
            row = codes_ref[at, sweep : sweep + 1, half : half + listed]
            cell[device * slot_count : (device + 1) * slot_count, :] = jnp.broadcast_to(
                row, (slot_count, listed)
            )

    row_at = iota((entries, listed), 0)
    owner_of = row_at // listed
    slot_of = owner_of * slot_count + row_at % slot_count
    is_slot = slot_of == iota((entries, listed), 1)
    device_of = (row_at // slot_count) % groups

    def entry_cells(cell):
        tiled = jnp.concatenate([cell[...]] * groups, axis=0)
        picked = jnp.sum(jnp.where(is_slot, tiled, 0), axis=1, keepdims=True)
        return picked.astype(F32)

    owner_col = owner_of[:, :1].astype(F32)
    cells = [entry_cells(cell0), entry_cells(cell1)]
    names = [cell + owner_col * float(owner_cells) for cell in cells]

    entry_row = iota((entries, entries), 0)
    natural = (
        ((entry_row // slot_count) % groups) * listed
        + (entry_row // listed) * slot_count
        + entry_row % slot_count
    )
    order = (natural == iota((entries, entries), 1)).astype(BF16)
    code_counts = [jnp.sum(table[...], axis=0, keepdims=True) for table in (table0, table1)]
    entry_counts = []
    for table in (table0, table1):
        count_high, count_low = split(
            jnp.broadcast_to(jnp.sum(table[...], axis=1, keepdims=True), (entries, LANES))
        )
        entry_counts.append(matmul(order, count_high) + matmul(order, count_low))
    most = jnp.maximum(jnp.max(table0[...]), jnp.max(table1[...]))
    large = most > LOW
    for digit in range(high):
        columns = slice(digit * LOW, (digit + 1) * LOW)
        permuted[0, :, columns] = matmul(order, table1[:, columns].astype(BF16)).astype(BF16)

    @pl.when(large)
    def _():
        for digit in range(high):
            columns = slice(digit * LOW, (digit + 1) * LOW)
            rest = split(table1[:, columns])[1]
            permuted[1, :, columns] = matmul(order, rest).astype(BF16)

    own_row = codes_ref[0, 0:1, half : half + listed].astype(F32)
    own_row = own_row + (iota((1, listed), 1) // slot_count).astype(F32) * float(owner_cells)
    match = (names[0] == own_row).astype(BF16)
    match = lax.dot_general(match, order, (((0,), (0,)), ((), ())), preferred_element_type=F32)
    match = match.astype(BF16)
    held = jnp.zeros((listed, 1), F32)
    for digit in range(high):
        columns = slice(digit * LOW, (digit + 1) * LOW)
        table_high, table_low = split(table0[:, columns])
        used = matmul(match, table_high) + matmul(match, table_low)
        held = held + jnp.sum(used, axis=1, keepdims=True)
        used_high, used_low = split(used)
        wide[0:listed, columns] = used_high.astype(F32)
        wide[listed : 2 * listed, columns] = used_low.astype(F32)
    wide[2 * listed : 2 * listed + 8, :] = jnp.broadcast_to(code_counts[0], (8, codewords))
    wide[2 * listed + 8 : 2 * listed + 16, :] = jnp.broadcast_to(code_counts[1], (8, codewords))
    wide[2 * listed + 16 :, :] = jnp.zeros((LANES - 2 * listed - 16, codewords), F32)
    center_high, center_low = split(first_ref[...] / jnp.maximum(held, 1.0))
    blank = jnp.zeros((LANES - 2 * listed, feature), BF16)
    center_high = jnp.concatenate([center_high, center_high, blank], axis=0)
    center_low = jnp.concatenate([center_low, center_low, blank], axis=0)
    for load in loads:
        load.wait()
    for digit in range(high):
        rows = slice(digit * LOW, (digit + 1) * LOW)
        columns = wide[:, rows].T
        code_info_ref[rows, :] = columns
        taken = jnp.where(iota((LOW, LANES), 1) < 2 * listed, columns, 0.0).astype(BF16)
        first_fine = fine[rows, :] - (matmul(taken, center_high) + matmul(taken, center_low))
        scaled = first_fine / jnp.maximum(columns[:, 2 * listed : 2 * listed + 1], 1.0)
        terms[0, rows, :], terms[1, rows, :] = split(scaled)
        fine[rows, :] = jnp.where(
            columns[:, 2 * listed + 8 : 2 * listed + 9] > 0, 0.0, first_fine
        )
    mine = pl.ds(pl.multiple_of(me * share_rows, share_rows), share_rows)
    empty = code_info_ref[mine, 2 * listed : 2 * listed + 1] == 0
    for part, share in enumerate(split(share_ref[...])):
        terms[part, mine, :] = jnp.where(
            empty, share.astype(F32), terms[part, mine, :].astype(F32)
        ).astype(BF16)

    own_entry = (is_slot & (device_of == me)).astype(BF16)
    second_high, second_low = split(second_ref[...])
    bracket[...] = (
        matmul(own_entry, second_high)
        + matmul(own_entry, second_low)
        - matmul(permuted[0], terms[0])
        - matmul(permuted[0], terms[1])
    )

    @pl.when(large)
    def _():
        bracket[...] -= matmul(permuted[1], terms[0])

    same = (
        jnp.broadcast_to(names[1], (entries, entries))
        == jnp.broadcast_to(names[1], (entries, LANES)).T[0:1, :]
    ).astype(BF16)
    total_high, total_low = split(entry_counts[1])
    totals = matmul(same, total_high) + matmul(same, total_low)
    bracket_high, bracket_low = split(bracket[...])
    centers = matmul(same, bracket_high) + matmul(same, bracket_low)
    centers = centers / jnp.maximum(totals[:, :1], 1.0)
    centers_ref[0], centers_ref[1] = split(centers)
    lane = iota((entries, LANES), 1)
    info = jnp.where(lane == 0, entry_counts[0], entry_counts[1])
    info = jnp.where(lane == 2, cells[0], info)
    entry_info_ref[...] = jnp.where(lane == 3, cells[1], info)

    eye = (iota((LOW, LOW), 0) == iota((LOW, LOW), 1)).astype(BF16)
    for digit in range(high):
        rows = slice(digit * LOW, (digit + 1) * LOW)
        pairs_ref[rows, :] = -matmul_nt(eye, permuted[0, :, rows]).astype(BF16)
    rows_here = vectors.shape[0]
    codes = fine_codes[1:2, :]
    copies = []
    for odd in (1, 0):
        blocks = [at for at in range(groups) if at % 2 == odd]
        for at, block in enumerate(blocks):
            owner = me ^ block
            rows = pl.ds(pl.multiple_of(owner * share_rows, share_rows), share_rows)
            to = slice(at * share_rows, (at + 1) * share_rows)
            left[to, :rows_here] = hot_rows(codes - owner * share_rows, share_rows)
            left[to, rows_here:] = pairs_ref[rows, :]
        start = 0
        for chunk, cut in enumerate(cuts):
            columns = slice(start, start + cut)
            start += cut
            sums = (
                matmul(left[:, :rows_here], vectors[:, columns])
                + matmul(left[:, rows_here:], centers_ref[0, :, columns])
                + matmul(left[:, rows_here:], centers_ref[1, :, columns])
            )
            for part, order_of in enumerate(orders[chunk]):
                if order_of[0] % 2 != odd:
                    continue
                number = 3 * chunk + part
                stage = stages[number]
                for to, block in enumerate(order_of):
                    owner = me ^ block
                    rows = pl.ds(pl.multiple_of(owner * share_rows, share_rows), share_rows)
                    cell_rows = pl.ds(pl.multiple_of(owner * listed, listed), listed)
                    at = blocks.index(block) * share_rows
                    stage[to, :share_rows, :] = sums[at : at + share_rows] + fine[rows, columns]
                    stage[to, share_rows:, :] = bracket[cell_rows, columns]

                @pl.when(large)
                def _():
                    for to, block in enumerate(order_of):
                        owner = me ^ block
                        rows = pl.ds(pl.multiple_of(owner * share_rows, share_rows), share_rows)
                        rest = lax.dot_general(
                            permuted[1, :, rows],
                            centers_ref[0, :, columns],
                            (((0,), (0,)), ((), ())),
                            preferred_element_type=F32,
                        )
                        stage[to, :share_rows, :] -= rest

                copy = pltpu.make_async_copy(stage, out_refs[number], out_sem.at[number])
                copy.start()
                copies.append(copy)
    for copy in copies:
        copy.wait()


def final_kernel(
    groups, slot_count, share_rows, cuts, me_ref, coarse_in, fine_share, first_sums, *refs
):
    last_refs, (code_info, entry_info, coarse_out, fine_out, own_first) = refs[:-5], refs[-5:]
    listed = entry_info.shape[0]
    owner_cells = coarse_in.shape[0]
    by_lane = entry_info[...].T
    for device in range(groups):
        rows = slice(device * slot_count, (device + 1) * slot_count)
        own_first[rows, :] = first_sums[device ^ me_ref[0]]
    hits, counts = [], []
    for sweep in range(2):
        cell = by_lane[2 + sweep : 3 + sweep, :].astype(jnp.int32)
        hit = iota((owner_cells, listed), 0) == cell
        counts.append(
            jnp.sum(jnp.where(hit, by_lane[sweep : sweep + 1, :], 0.0), axis=1, keepdims=True)
        )
        hits.append(hit.astype(BF16))
    first_count = code_info[:, 2 * listed : 2 * listed + 1]
    last_count = code_info[:, 2 * listed + 8 : 2 * listed + 9]
    count = jnp.where(last_count > 0, last_count, first_count)
    start = 0
    for cut, last_sums in zip(cuts, last_refs):
        columns = slice(start, start + cut)
        start += cut
        coarse = coarse_in[:, columns]
        for sweep, sums in enumerate((own_first[:, columns], last_sums[share_rows:, :])):
            sums_high, sums_low = split(sums)
            found = matmul(hits[sweep], sums_high) + matmul(hits[sweep], sums_low)
            weight = 1.0 / jnp.maximum(counts[sweep], 1.0)
            coarse = jnp.where(counts[sweep] > 0, found * weight, coarse)
        coarse_out[:, columns] = coarse
        fine_out[:, columns] = jnp.where(
            count > 0,
            last_sums[:share_rows, :] * (1.0 / jnp.maximum(count, 1.0)),
            fine_share[:, columns],
        )


def exchange(values, step):
    groups = lax.axis_size("cell")
    return lax.ppermute(values, "cell", [(at, at ^ step) for at in range(groups)])


def block_order(bits):
    order = [0]
    for bit in list(bits)[::-1]:
        order = [block + (1 << bit) for block in order] + order
    return order


def block_orders(bits):
    order = block_order(bits)
    half = len(order) // 2
    return [block + 1 for block in order], order[:half], order[half:]


def after(values, *others):
    return lax.optimization_barrier((values, *others))[0]


def halved(got, other, kept):
    half = other.shape[0]
    return other + got[:half], kept + got[half:]


def swap(blocks, bit):
    half = blocks.shape[0] // 2
    got = exchange(blocks[:half], 1 << bit)
    return jnp.concatenate([blocks[half:], got], axis=1)


def local(kernel, shapes, in_specs, out_specs, scratch, flops, name, aliases=None):
    return pl.pallas_call(
        kernel,
        out_shape=tuple(jax.ShapeDtypeStruct(shape, dtype) for shape, dtype in shapes),
        grid_spec=pltpu.PrefetchScalarGridSpec(
            num_scalar_prefetch=1,
            grid=(1,),
            in_specs=in_specs,
            out_specs=out_specs,
            scratch_shapes=scratch,
        ),
        input_output_aliases=aliases or {},
        compiler_params=PARAMS,
        cost_estimate=pl.CostEstimate(
            flops=int(flops), bytes_accessed=10**6, transcendentals=0
        ),
        name=name,
    )


def block(shape, *place):
    return pl.BlockSpec(
        shape, lambda step, me: tuple(me[0] if at is None else at for at in place)
    )


def dense_plan(vectors, row_slot, fine_codes, cell_list, coarse_in, fine_in):
    groups = lax.axis_size("cell")
    rows_here, feature = vectors.shape
    listed = cell_list.shape[1]
    slot_count = listed // groups
    owner_cells = coarse_in.shape[0]
    codewords = fine_in.shape[0]
    share_rows = codewords // groups
    entries = groups * listed
    half = rows_here // 2
    me = lax.axis_index("cell").reshape(1).astype(jnp.int32)

    packed = local(
        lambda me_ref, *refs: pack_kernel(*refs),
        [((8, half + LANES), jnp.int32)],
        [VMEM] * 3,
        [VMEM],
        [],
        1e9,
        "pack",
    )(me, fine_codes, row_slot, cell_list)[0]
    first, second, first_to = local(
        lambda *refs: own_cells_kernel(groups, listed, *refs),
        [((listed, feature), F32)] * 2 + [((groups, 1, slot_count, feature), F32)],
        [VMEM] * 4,
        [VMEM] * 3,
        [],
        5e9,
        "own_cells",
    )(me, vectors, fine_codes, row_slot, fine_in)
    far = groups // 4
    gathered = jnp.stack([packed] + [exchange(packed, 4 * step) for step in range(1, far)])
    sums = []
    for step, base in ((2, 0), (1, codewords // 2)):
        sums += local(
            lambda me_ref, *refs, base=base: own_codes_kernel(base, *refs),
            [((codewords // 2, feature), F32)],
            [VMEM, VMEM, ANY],
            [VMEM],
            [],
            6e9,
            "own_codes",
        )(me, vectors, fine_codes, gathered)
        gathered = jnp.concatenate([gathered, exchange(gathered, step)])

    top = groups.bit_length() - 1
    near_first = list(range(1, top))
    far_first = near_first[1:] + near_first[:1]
    cuts = [feature // 3] * 3
    bits = [near_first, far_first, near_first]
    orders = [block_orders(each) for each in bits]
    shapes = [
        (len(order), share_rows + listed, cut)
        for cut, three in zip(cuts, orders)
        for order in three
    ]
    *terms, code_info, entry_info = local(
        lambda *refs: sums_kernel(groups, slot_count, owner_cells, cuts, orders, *refs),
        [(shape, F32) for shape in shapes]
        + [((codewords, LANES), F32), ((entries, LANES), F32)],
        [VMEM] * 3 + [ANY] * 2 + [VMEM] * 2 + [block((share_rows, feature), None, 0)],
        [ANY] * len(shapes) + [VMEM] * 2,
        [
            pltpu.VMEM((entries, codewords), F32),
            pltpu.VMEM((entries, codewords), F32),
            pltpu.VMEM((listed, listed), jnp.int32),
            pltpu.VMEM((listed, listed), jnp.int32),
            pltpu.VMEM((LANES, codewords), F32),
            pltpu.VMEM((2, codewords, feature), BF16),
            pltpu.VMEM((2, entries, codewords), BF16),
            pltpu.VMEM((LOW, half), BF16),
            pltpu.VMEM((codewords, feature), F32),
            pltpu.VMEM((entries, feature), F32),
            pltpu.VMEM((2, entries, feature), BF16),
            pltpu.VMEM((codewords, entries), BF16),
            pltpu.VMEM((codewords // 2, rows_here + entries), BF16),
            pltpu.SemaphoreType.DMA((2,)),
            pltpu.SemaphoreType.DMA((len(shapes),)),
        ]
        + [pltpu.VMEM(shape, F32) for shape in shapes],
        40e9,
        "sums",
    )(me, gathered, vectors, fine_codes, *sums, first, second, fine_in)

    finished = []
    for at, steps in enumerate(bits):
        away, other, kept = terms[3 * at : 3 * at + 3]
        other, kept = halved(exchange(away, 1), other, kept)
        if at == len(bits) - 1:
            for bit in range(top):
                first_to = swap(after(first_to, other), bit)
        for bit in steps[:-1]:
            got = exchange(other, 1 << bit)
            half = got.shape[0] // 2
            other, kept = halved(got, kept[:half], kept[half:])
        finished.append((kept + exchange(other, 1 << steps[-1]))[0])
    return local(
        lambda *refs: final_kernel(groups, slot_count, share_rows, cuts, *refs),
        [(coarse_in.shape, F32), ((share_rows, feature), F32)],
        [VMEM, block((share_rows, feature), None, 0)]
        + [VMEM] * (1 + len(cuts))
        + [block((share_rows, LANES), None, 0), block((listed, LANES), None, 0)],
        [VMEM] * 2,
        [pltpu.VMEM((listed, feature), F32)],
        1e9,
        "outputs",
    )(me, coarse_in, fine_in, first_to[0], *finished, code_info, entry_info)


def fits_dense(mesh_groups, listed, codewords, rows_here, feature):
    entries = mesh_groups * listed
    power = mesh_groups & (mesh_groups - 1) == 0 and mesh_groups >= 4
    digits = codewords % (2 * LOW) == 0 and (codewords // LOW) * listed <= LOW
    shapes = rows_here % (2 * LANES) == 0 and feature % (6 * LANES) == 0
    return power and digits and shapes and entries * codewords <= 2**20


def per_device(vectors, row_slot, fine_codes, cell_list, coarse_in, fine_in):
    groups = lax.axis_size("cell")
    dense = fits_dense(groups, cell_list.shape[1], *fine_in.shape[:1], *vectors.shape)
    plan = dense_plan if dense else routed_plan
    return plan(vectors, row_slot, fine_codes, cell_list, coarse_in, fine_in)


def solution(mesh):
    return jax.shard_map(
        per_device,
        mesh=mesh,
        in_specs=(
            P(("parts", "cell"), None),
            P(None, ("parts", "cell")),
            P(None, ("parts", "cell")),
            P(None, ("parts", "cell")),
            P("cell", None),
            P(),
        ),
        out_specs=(P(("parts", "cell"), None), P(("parts", "cell"), None)),
        check_vma=False,
    )
```

```python
import jax
import jax.numpy as jnp
from jax import lax
from jax.experimental import pallas as pl
from jax.experimental.pallas import tpu as pltpu
from jax.sharding import PartitionSpec as P


def code_tally(code_rows, codewords):
    return jax.ops.segment_sum(
        jnp.ones(code_rows.shape, jnp.float32), code_rows, num_segments=codewords
    )


def fine_update(code_term, totals_share, old_share, share_rows):
    part_sums = lax.psum_scatter(
        code_term(jnp.int32(0), lax.axis_size("cell") * share_rows),
        "cell",
        scatter_dimension=0,
        tiled=True,
    )
    return jnp.where(
        totals_share[:, None] > 0, part_sums / jnp.maximum(totals_share, 1.0)[:, None], old_share
    )


def routed_plan(vectors, row_slot, fine_codes, cell_list, coarse_in, fine_in):
    groups = lax.axis_size("cell")
    rows_here, feature = vectors.shape
    listed = cell_list.shape[1]
    slot_count = listed // groups
    owner_cells = coarse_in.shape[0]
    codewords = fine_in.shape[0]
    share_rows = codewords // groups
    share_start = lax.axis_index("cell") * share_rows
    fine_book = fine_in
    fine_share = lax.dynamic_slice_in_dim(fine_in, share_start, share_rows, 0)
    coarse = coarse_in
    list_iota = lax.iota(jnp.int32, listed)
    for sweep in range(2):
        code_totals = lax.psum(code_tally(fine_codes[sweep], codewords), "cell")
        slot_rows = row_slot[sweep]
        code_rows = fine_codes[sweep]
        picked = jnp.take(fine_book, code_rows, axis=0)
        residual = (vectors.astype(jnp.float32) - picked).astype(jnp.bfloat16)
        slot_hot = (slot_rows[None, :] == list_iota[:, None]).astype(jnp.bfloat16)
        slot_sums = jnp.dot(slot_hot, residual, preferred_element_type=jnp.float32)
        slot_counts = jnp.sum(slot_hot, axis=1, dtype=jnp.float32)
        slot_cells = cell_list[sweep].astype(jnp.float32)
        got_sums, got_counts, got_cells = (
            lax.all_to_all(
                slot_sums.reshape(groups, slot_count, feature),
                "cell",
                split_axis=0,
                concat_axis=0,
                tiled=True,
            ),
            lax.all_to_all(
                slot_counts.reshape(groups, slot_count),
                "cell",
                split_axis=0,
                concat_axis=0,
                tiled=True,
            ),
            lax.all_to_all(
                slot_cells.reshape(groups, slot_count),
                "cell",
                split_axis=0,
                concat_axis=0,
                tiled=True,
            ),
        )
        flat_cells = got_cells.reshape(groups * slot_count).astype(jnp.int32)
        cell_sums = jax.ops.segment_sum(
            got_sums.reshape(groups * slot_count, feature), flat_cells, num_segments=owner_cells
        )
        cell_counts = jax.ops.segment_sum(
            got_counts.reshape(groups * slot_count), flat_cells, num_segments=owner_cells
        )
        coarse = jnp.where(
            cell_counts[:, None] > 0, cell_sums / jnp.maximum(cell_counts, 1.0)[:, None], coarse
        )
        returned_rows = jnp.take(coarse, flat_cells, axis=0).reshape(groups, slot_count, feature)
        arrived = lax.all_to_all(returned_rows, "cell", split_axis=0, concat_axis=0, tiled=True)
        entry_centers = arrived.reshape(listed, feature)
        row_centers = jnp.take(entry_centers, slot_rows, axis=0)
        fine_residual = (vectors.astype(jnp.float32) - row_centers).astype(jnp.bfloat16)

        def code_term(start, count, code_rows=code_rows, fine_residual=fine_residual):
            wanted = start + lax.iota(jnp.int32, count)
            code_hot = (code_rows[None, :] == wanted[:, None]).astype(jnp.bfloat16)
            return jnp.dot(code_hot, fine_residual, preferred_element_type=jnp.float32)

        totals_share = lax.dynamic_slice_in_dim(code_totals, share_start, share_rows, 0)
        if sweep == 0:
            full_sums = lax.psum(code_term(0, codewords), "cell")
            fine_book = jnp.where(
                code_totals[:, None] > 0,
                full_sums / jnp.maximum(code_totals, 1.0)[:, None],
                fine_book,
            )
            fine_share = lax.dynamic_slice_in_dim(fine_book, share_start, share_rows, 0)
        else:
            fine_share = fine_update(code_term, totals_share, fine_share, share_rows)
    return (coarse, fine_share)


F32 = jnp.float32
BF16 = jnp.bfloat16
LOW = 256
LANES = 128
PARAMS = pltpu.CompilerParams(vmem_limit_bytes=58 * 2**20)
VMEM = pl.BlockSpec(memory_space=pltpu.VMEM)
SMEM = pl.BlockSpec(memory_space=pltpu.SMEM)
ANY = pl.BlockSpec(memory_space=pl.ANY)


def iota(shape, axis):
    return lax.broadcasted_iota(jnp.int32, shape, axis)


def matmul(left, right):
    return jnp.dot(left, right, preferred_element_type=F32)


def matmul_nt(left, right):
    return lax.dot_general(left, right, (((1,), (1,)), ((), ())), preferred_element_type=F32)


def split(values):
    high = values.astype(BF16)
    return high, (values - high.astype(F32)).astype(BF16)


def hot_rows(codes, rows=LOW):
    inside = jnp.where((codes >= 0) & (codes < rows), codes, -1)
    inside = inside.astype(F32).astype(BF16)
    row = iota((rows, codes.shape[1]), 0).astype(F32).astype(BF16)
    return jnp.where(row == inside, jnp.ones((), BF16), jnp.zeros((), BF16))


def pair_block(codes, slots, listed, high):
    left = hot_rows((codes >> 8) * listed + slots, high * listed)
    return matmul_nt(left, hot_rows(codes & (LOW - 1)))


def pack_kernel(fine_codes, row_slot, cell_list, packed):
    half = fine_codes.shape[1] // 2
    listed = cell_list.shape[1]
    packed[:, half:] = jnp.zeros((8, LANES), jnp.int32)
    for number, ref in enumerate((fine_codes, row_slot)):
        for sweep in range(2):
            for part in range(2):
                row = 4 * number + 2 * sweep + part
                packed[row : row + 1, :half] = ref[
                    sweep : sweep + 1, part * half : (part + 1) * half
                ]
    packed[0:2, half : half + listed] = cell_list[...]


def own_cells_kernel(
    groups, listed, me_ref, vectors, fine_codes, row_slot, fine_in, first_ref, second_ref, to_ref
):
    high = fine_in.shape[0] // LOW
    first = matmul(hot_rows(row_slot[0:1, :], listed), vectors[...])
    second_ref[...] = matmul(hot_rows(row_slot[1:2, :], listed), vectors[...])
    pairs = pair_block(fine_codes[0:1, :], row_slot[0:1, :], listed, high)
    for digit in range(high):
        pairs_high, pairs_low = split(pairs[digit * listed : (digit + 1) * listed])
        both = jnp.concatenate([pairs_high, pairs_low], axis=0)
        book = fine_in[digit * LOW : (digit + 1) * LOW, :]
        book_high, book_low = split(book)
        taken = matmul(both, book_high) + matmul(both, book_low)
        first = first - taken[:listed] - taken[listed:]
    first_ref[...] = first
    slots = listed // groups
    top = groups.bit_length() - 1
    for owner in range(groups):
        block = owner ^ me_ref[0]
        at = sum((1 - (block >> bit & 1)) << (top - 1 - bit) for bit in range(2))
        at = at + groups // 4 - 1 - (block >> 2)
        to_ref[at, 0] = first[owner * slots : (owner + 1) * slots]


def own_codes_kernel(base, vectors, fine_codes, _, sums_ref):
    codes = fine_codes[0:1, :] - base
    for start in range(0, sums_ref.shape[0], 2 * LOW):
        hot = jnp.concatenate(
            [hot_rows(codes - start), hot_rows(codes - start - LOW)], axis=0
        )
        sums_ref[start : start + 2 * LOW, :] = matmul(hot, vectors[...])


def position(block, groups):
    return (block & 1) * (groups // 2) + (block >> 1 & 1) * (groups // 4) + (block >> 2)


def sums_kernel(
    groups,
    slot_count,
    owner_cells,
    cuts,
    orders,
    me_ref,
    codes_ref,
    vectors,
    fine_codes,
    low_sums_ref,
    high_sums_ref,
    first_ref,
    second_ref,
    share_ref,
    *refs,
):
    out_refs, refs = refs[: 3 * len(cuts)], refs[3 * len(cuts) :]
    code_info_ref, entry_info_ref, refs = refs[0], refs[1], refs[2:]
    table0, table1, cell0, cell1, wide, terms, permuted, rows_hot = refs[:8]
    fine, bracket, centers_ref, pairs_ref, left = refs[8:13]
    in_sem, out_sem, stages = refs[13], refs[14], refs[15:]
    me = me_ref[0]
    codewords, feature = fine.shape
    listed = groups * slot_count
    entries = groups * listed
    high = codewords // LOW
    half = codes_ref.shape[2] - LANES
    share_rows = share_ref.shape[0]

    loads = [
        pltpu.make_async_copy(
            ref, fine.at[pl.ds(at * (codewords // 2), codewords // 2)], in_sem.at[at]
        )
        for at, ref in enumerate((low_sums_ref, high_sums_ref))
    ]
    for load in loads:
        load.start()

    rows_hot[...] = iota(rows_hot.shape, 0).astype(F32).astype(BF16)
    one, zero = jnp.ones((), BF16), jnp.zeros((), BF16)

    def hot(codes):
        return jnp.where(rows_hot[...] == codes.astype(F32).astype(BF16), one, zero)

    def device_tables(device, carry):
        at = position(device ^ me, groups)
        for sweep, table in enumerate((table0, table1)):
            block = jnp.zeros((high * listed, LOW), F32)
            for part in range(2):
                row = 2 * sweep + part
                codes = codes_ref[at, row : row + 1, :half]
                slots = codes_ref[at, row + 4 : row + 5, :half]
                block = block + matmul_nt(
                    hot((codes >> 8) * listed + slots)[: high * listed], hot(codes & (LOW - 1))
                )
            rows = pl.ds(pl.multiple_of(device * listed, listed), listed)
            for digit in range(high):
                table[rows, digit * LOW : (digit + 1) * LOW] = block[
                    digit * listed : (digit + 1) * listed
                ]
        return carry

    lax.fori_loop(0, groups, device_tables, 0)
    for device in range(groups):
        at = position(device ^ me, groups)
        for sweep, cell in enumerate((cell0, cell1)):
            row = codes_ref[at, sweep : sweep + 1, half : half + listed]
            cell[device * slot_count : (device + 1) * slot_count, :] = jnp.broadcast_to(
                row, (slot_count, listed)
            )

    row_at = iota((entries, listed), 0)
    owner_of = row_at // listed
    slot_of = owner_of * slot_count + row_at % slot_count
    is_slot = slot_of == iota((entries, listed), 1)
    device_of = (row_at // slot_count) % groups

    def entry_cells(cell):
        tiled = jnp.concatenate([cell[...]] * groups, axis=0)
        picked = jnp.sum(jnp.where(is_slot, tiled, 0), axis=1, keepdims=True)
        return picked.astype(F32)

    owner_col = owner_of[:, :1].astype(F32)
    cells = [entry_cells(cell0), entry_cells(cell1)]
    names = [cell + owner_col * float(owner_cells) for cell in cells]

    entry_row = iota((entries, entries), 0)
    natural = (
        ((entry_row // slot_count) % groups) * listed
        + (entry_row // listed) * slot_count
        + entry_row % slot_count
    )
    order = (natural == iota((entries, entries), 1)).astype(BF16)
    code_counts = [jnp.sum(table[...], axis=0, keepdims=True) for table in (table0, table1)]
    entry_counts = []
    for table in (table0, table1):
        count_high, count_low = split(
            jnp.broadcast_to(jnp.sum(table[...], axis=1, keepdims=True), (entries, LANES))
        )
        entry_counts.append(matmul(order, count_high) + matmul(order, count_low))
    most = jnp.maximum(jnp.max(table0[...]), jnp.max(table1[...]))
    large = most > LOW
    for digit in range(high):
        columns = slice(digit * LOW, (digit + 1) * LOW)
        permuted[0, :, columns] = matmul(order, table1[:, columns].astype(BF16)).astype(BF16)

    @pl.when(large)
    def _():
        for digit in range(high):
            columns = slice(digit * LOW, (digit + 1) * LOW)
            rest = split(table1[:, columns])[1]
            permuted[1, :, columns] = matmul(order, rest).astype(BF16)

    own_row = codes_ref[0, 0:1, half : half + listed].astype(F32)
    own_row = own_row + (iota((1, listed), 1) // slot_count).astype(F32) * float(owner_cells)
    match = (names[0] == own_row).astype(BF16)
    match = lax.dot_general(match, order, (((0,), (0,)), ((), ())), preferred_element_type=F32)
    match = match.astype(BF16)
    held = jnp.zeros((listed, 1), F32)
    for digit in range(high):
        columns = slice(digit * LOW, (digit + 1) * LOW)
        table_high, table_low = split(table0[:, columns])
        used = matmul(match, table_high) + matmul(match, table_low)
        held = held + jnp.sum(used, axis=1, keepdims=True)
        used_high, used_low = split(used)
        wide[0:listed, columns] = used_high.astype(F32)
        wide[listed : 2 * listed, columns] = used_low.astype(F32)
    wide[2 * listed : 2 * listed + 8, :] = jnp.broadcast_to(code_counts[0], (8, codewords))
    wide[2 * listed + 8 : 2 * listed + 16, :] = jnp.broadcast_to(code_counts[1], (8, codewords))
    wide[2 * listed + 16 :, :] = jnp.zeros((LANES - 2 * listed - 16, codewords), F32)
    center_high, center_low = split(first_ref[...] / jnp.maximum(held, 1.0))
    blank = jnp.zeros((LANES - 2 * listed, feature), BF16)
    center_high = jnp.concatenate([center_high, center_high, blank], axis=0)
    center_low = jnp.concatenate([center_low, center_low, blank], axis=0)
    for load in loads:
        load.wait()
    for digit in range(high):
        rows = slice(digit * LOW, (digit + 1) * LOW)
        columns = wide[:, rows].T
        code_info_ref[rows, :] = columns
        taken = jnp.where(iota((LOW, LANES), 1) < 2 * listed, columns, 0.0).astype(BF16)
        first_fine = fine[rows, :] - (matmul(taken, center_high) + matmul(taken, center_low))
        scaled = first_fine / jnp.maximum(columns[:, 2 * listed : 2 * listed + 1], 1.0)
        terms[0, rows, :], terms[1, rows, :] = split(scaled)
        fine[rows, :] = jnp.where(
            columns[:, 2 * listed + 8 : 2 * listed + 9] > 0, 0.0, first_fine
        )
    mine = pl.ds(pl.multiple_of(me * share_rows, share_rows), share_rows)
    empty = code_info_ref[mine, 2 * listed : 2 * listed + 1] == 0
    for part, share in enumerate(split(share_ref[...])):
        terms[part, mine, :] = jnp.where(
            empty, share.astype(F32), terms[part, mine, :].astype(F32)
        ).astype(BF16)

    own_entry = (is_slot & (device_of == me)).astype(BF16)
    second_high, second_low = split(second_ref[...])
    bracket[...] = (
        matmul(own_entry, second_high)
        + matmul(own_entry, second_low)
        - matmul(permuted[0], terms[0])
        - matmul(permuted[0], terms[1])
    )

    @pl.when(large)
    def _():
        bracket[...] -= matmul(permuted[1], terms[0])

    same = (
        jnp.broadcast_to(names[1], (entries, entries))
        == jnp.broadcast_to(names[1], (entries, LANES)).T[0:1, :]
    ).astype(BF16)
    total_high, total_low = split(entry_counts[1])
    totals = matmul(same, total_high) + matmul(same, total_low)
    bracket_high, bracket_low = split(bracket[...])
    centers = matmul(same, bracket_high) + matmul(same, bracket_low)
    centers = centers / jnp.maximum(totals[:, :1], 1.0)
    centers_ref[0], centers_ref[1] = split(centers)
    lane = iota((entries, LANES), 1)
    info = jnp.where(lane == 0, entry_counts[0], entry_counts[1])
    info = jnp.where(lane == 2, cells[0], info)
    entry_info_ref[...] = jnp.where(lane == 3, cells[1], info)

    eye = (iota((LOW, LOW), 0) == iota((LOW, LOW), 1)).astype(BF16)
    for digit in range(high):
        rows = slice(digit * LOW, (digit + 1) * LOW)
        pairs_ref[rows, :] = -matmul_nt(eye, permuted[0, :, rows]).astype(BF16)
    rows_here = vectors.shape[0]
    codes = fine_codes[1:2, :]
    copies = []
    for odd in (1, 0):
        blocks = [at for at in range(groups) if at % 2 == odd]
        for at, block in enumerate(blocks):
            owner = me ^ block
            rows = pl.ds(pl.multiple_of(owner * share_rows, share_rows), share_rows)
            to = slice(at * share_rows, (at + 1) * share_rows)
            left[to, :rows_here] = hot_rows(codes - owner * share_rows, share_rows)
            left[to, rows_here:] = pairs_ref[rows, :]
        start = 0
        for chunk, cut in enumerate(cuts):
            columns = slice(start, start + cut)
            start += cut
            sums = (
                matmul(left[:, :rows_here], vectors[:, columns])
                + matmul(left[:, rows_here:], centers_ref[0, :, columns])
                + matmul(left[:, rows_here:], centers_ref[1, :, columns])
            )
            for part, order_of in enumerate(orders[chunk]):
                if order_of[0] % 2 != odd:
                    continue
                number = 3 * chunk + part
                stage = stages[number]
                for to, block in enumerate(order_of):
                    owner = me ^ block
                    rows = pl.ds(pl.multiple_of(owner * share_rows, share_rows), share_rows)
                    cell_rows = pl.ds(pl.multiple_of(owner * listed, listed), listed)
                    at = blocks.index(block) * share_rows
                    stage[to, :share_rows, :] = sums[at : at + share_rows] + fine[rows, columns]
                    stage[to, share_rows:, :] = bracket[cell_rows, columns]

                @pl.when(large)
                def _():
                    for to, block in enumerate(order_of):
                        owner = me ^ block
                        rows = pl.ds(pl.multiple_of(owner * share_rows, share_rows), share_rows)
                        rest = lax.dot_general(
                            permuted[1, :, rows],
                            centers_ref[0, :, columns],
                            (((0,), (0,)), ((), ())),
                            preferred_element_type=F32,
                        )
                        stage[to, :share_rows, :] -= rest

                copy = pltpu.make_async_copy(stage, out_refs[number], out_sem.at[number])
                copy.start()
                copies.append(copy)
    for copy in copies:
        copy.wait()


def final_kernel(
    groups, slot_count, share_rows, cuts, me_ref, coarse_in, fine_share, first_sums, *refs
):
    last_refs, (code_info, entry_info, coarse_out, fine_out, own_first) = refs[:-5], refs[-5:]
    listed = entry_info.shape[0]
    owner_cells = coarse_in.shape[0]
    by_lane = entry_info[...].T
    for device in range(groups):
        rows = slice(device * slot_count, (device + 1) * slot_count)
        own_first[rows, :] = first_sums[device ^ me_ref[0]]
    hits, counts = [], []
    for sweep in range(2):
        cell = by_lane[2 + sweep : 3 + sweep, :].astype(jnp.int32)
        hit = iota((owner_cells, listed), 0) == cell
        counts.append(
            jnp.sum(jnp.where(hit, by_lane[sweep : sweep + 1, :], 0.0), axis=1, keepdims=True)
        )
        hits.append(hit.astype(BF16))
    first_count = code_info[:, 2 * listed : 2 * listed + 1]
    last_count = code_info[:, 2 * listed + 8 : 2 * listed + 9]
    count = jnp.where(last_count > 0, last_count, first_count)
    start = 0
    for cut, last_sums in zip(cuts, last_refs):
        columns = slice(start, start + cut)
        start += cut
        coarse = coarse_in[:, columns]
        for sweep, sums in enumerate((own_first[:, columns], last_sums[share_rows:, :])):
            sums_high, sums_low = split(sums)
            found = matmul(hits[sweep], sums_high) + matmul(hits[sweep], sums_low)
            weight = 1.0 / jnp.maximum(counts[sweep], 1.0)
            coarse = jnp.where(counts[sweep] > 0, found * weight, coarse)
        coarse_out[:, columns] = coarse
        fine_out[:, columns] = jnp.where(
            count > 0,
            last_sums[:share_rows, :] * (1.0 / jnp.maximum(count, 1.0)),
            fine_share[:, columns],
        )


def exchange(values, step):
    groups = lax.axis_size("cell")
    return lax.ppermute(values, "cell", [(at, at ^ step) for at in range(groups)])


def block_order(bits):
    order = [0]
    for bit in list(bits)[::-1]:
        order = [block + (1 << bit) for block in order] + order
    return order


def block_orders(bits):
    order = block_order(bits)
    half = len(order) // 2
    return [block + 1 for block in order], order[:half], order[half:]


def after(values, *others):
    return lax.optimization_barrier((values, *others))[0]


def halved(got, other, kept):
    half = other.shape[0]
    return other + got[:half], kept + got[half:]


def swap(blocks, bit):
    half = blocks.shape[0] // 2
    got = exchange(blocks[:half], 1 << bit)
    return jnp.concatenate([blocks[half:], got], axis=1)


def local(kernel, shapes, in_specs, out_specs, scratch, flops, name, aliases=None):
    return pl.pallas_call(
        kernel,
        out_shape=tuple(jax.ShapeDtypeStruct(shape, dtype) for shape, dtype in shapes),
        grid_spec=pltpu.PrefetchScalarGridSpec(
            num_scalar_prefetch=1,
            grid=(1,),
            in_specs=in_specs,
            out_specs=out_specs,
            scratch_shapes=scratch,
        ),
        input_output_aliases=aliases or {},
        compiler_params=PARAMS,
        cost_estimate=pl.CostEstimate(
            flops=int(flops), bytes_accessed=10**6, transcendentals=0
        ),
        name=name,
    )


def block(shape, *place):
    return pl.BlockSpec(
        shape, lambda step, me: tuple(me[0] if at is None else at for at in place)
    )


def dense_plan(vectors, row_slot, fine_codes, cell_list, coarse_in, fine_in):
    groups = lax.axis_size("cell")
    rows_here, feature = vectors.shape
    listed = cell_list.shape[1]
    slot_count = listed // groups
    owner_cells = coarse_in.shape[0]
    codewords = fine_in.shape[0]
    share_rows = codewords // groups
    entries = groups * listed
    half = rows_here // 2
    me = lax.axis_index("cell").reshape(1).astype(jnp.int32)

    packed = local(
        lambda me_ref, *refs: pack_kernel(*refs),
        [((8, half + LANES), jnp.int32)],
        [VMEM] * 3,
        [VMEM],
        [],
        1e9,
        "pack",
    )(me, fine_codes, row_slot, cell_list)[0]
    first, second, first_to = local(
        lambda *refs: own_cells_kernel(groups, listed, *refs),
        [((listed, feature), F32)] * 2 + [((groups, 1, slot_count, feature), F32)],
        [VMEM] * 4,
        [VMEM] * 3,
        [],
        5e9,
        "own_cells",
    )(me, vectors, fine_codes, row_slot, fine_in)
    far = groups // 4
    gathered = jnp.stack([packed] + [exchange(packed, 4 * step) for step in range(1, far)])
    sums = []
    for step, base in ((2, 0), (1, codewords // 2)):
        sums += local(
            lambda me_ref, *refs, base=base: own_codes_kernel(base, *refs),
            [((codewords // 2, feature), F32)],
            [VMEM, VMEM, ANY],
            [VMEM],
            [],
            6e9,
            "own_codes",
        )(me, vectors, fine_codes, gathered)
        gathered = jnp.concatenate([gathered, exchange(gathered, step)])
        first_to = swap(first_to, 2 - step)
    first_to = first_to[::-1]
    first_to = jnp.concatenate(
        [first_to[0]] + [exchange(first_to[step], 4 * step) for step in range(1, far)]
    )

    top = groups.bit_length() - 1
    near_first = list(range(1, top))
    far_first = near_first[1:] + near_first[:1]
    cuts = [feature // 3, feature // 6, feature // 6, feature // 3]
    bits = [near_first, far_first, near_first, near_first]
    orders = [block_orders(each) for each in bits]
    shapes = [
        (len(order), share_rows + listed, cut)
        for cut, three in zip(cuts, orders)
        for order in three
    ]
    *terms, code_info, entry_info = local(
        lambda *refs: sums_kernel(groups, slot_count, owner_cells, cuts, orders, *refs),
        [(shape, F32) for shape in shapes]
        + [((codewords, LANES), F32), ((entries, LANES), F32)],
        [VMEM] * 3 + [ANY] * 2 + [VMEM] * 2 + [block((share_rows, feature), None, 0)],
        [ANY] * len(shapes) + [VMEM] * 2,
        [
            pltpu.VMEM((entries, codewords), F32),
            pltpu.VMEM((entries, codewords), F32),
            pltpu.VMEM((listed, listed), jnp.int32),
            pltpu.VMEM((listed, listed), jnp.int32),
            pltpu.VMEM((LANES, codewords), F32),
            pltpu.VMEM((2, codewords, feature), BF16),
            pltpu.VMEM((2, entries, codewords), BF16),
            pltpu.VMEM((LOW, half), BF16),
            pltpu.VMEM((codewords, feature), F32),
            pltpu.VMEM((entries, feature), F32),
            pltpu.VMEM((2, entries, feature), BF16),
            pltpu.VMEM((codewords, entries), BF16),
            pltpu.VMEM((codewords // 2, rows_here + entries), BF16),
            pltpu.SemaphoreType.DMA((2,)),
            pltpu.SemaphoreType.DMA((len(shapes),)),
        ]
        + [pltpu.VMEM(shape, F32) for shape in shapes],
        40e9,
        "sums",
    )(me, gathered, vectors, fine_codes, *sums, first, second, fine_in)

    terms[0], first_to = lax.optimization_barrier((terms[0], first_to))
    begun = []
    for at in range(len(cuts)):
        away, other, kept = terms[3 * at : 3 * at + 3]
        begun += halved(exchange(away, 1), other, kept)
    begun = lax.optimization_barrier(tuple(begun))
    finished = []
    for at, steps in enumerate(bits):
        other, kept = begun[2 * at : 2 * at + 2]
        for bit in steps[:-1]:
            got = exchange(other, 1 << bit)
            half = got.shape[0] // 2
            other, kept = halved(got, kept[:half], kept[half:])
        finished.append((kept + exchange(other, 1 << steps[-1]))[0])
    return local(
        lambda *refs: final_kernel(groups, slot_count, share_rows, cuts, *refs),
        [(coarse_in.shape, F32), ((share_rows, feature), F32)],
        [VMEM, block((share_rows, feature), None, 0)]
        + [VMEM] * (1 + len(cuts))
        + [block((share_rows, LANES), None, 0), block((listed, LANES), None, 0)],
        [VMEM] * 2,
        [pltpu.VMEM((listed, feature), F32)],
        1e9,
        "outputs",
    )(me, coarse_in, fine_in, first_to, *finished, code_info, entry_info)


def fits_dense(mesh_groups, listed, codewords, rows_here, feature):
    entries = mesh_groups * listed
    power = mesh_groups & (mesh_groups - 1) == 0 and mesh_groups >= 4
    digits = codewords % (2 * LOW) == 0 and (codewords // LOW) * listed <= LOW
    shapes = rows_here % (2 * LANES) == 0 and feature % (6 * LANES) == 0
    return power and digits and shapes and entries * codewords <= 2**20


def per_device(vectors, row_slot, fine_codes, cell_list, coarse_in, fine_in):
    groups = lax.axis_size("cell")
    dense = fits_dense(groups, cell_list.shape[1], *fine_in.shape[:1], *vectors.shape)
    plan = dense_plan if dense else routed_plan
    return plan(vectors, row_slot, fine_codes, cell_list, coarse_in, fine_in)


def solution(mesh):
    return jax.shard_map(
        per_device,
        mesh=mesh,
        in_specs=(
            P(("parts", "cell"), None),
            P(None, ("parts", "cell")),
            P(None, ("parts", "cell")),
            P(None, ("parts", "cell")),
            P("cell", None),
            P(),
        ),
        out_specs=(P(("parts", "cell"), None), P(("parts", "cell"), None)),
        check_vma=False,
    )
```

```python
import jax
import jax.numpy as jnp
from jax import lax
from jax.experimental import pallas as pl
from jax.experimental.pallas import tpu as pltpu
from jax.sharding import PartitionSpec as P


def code_tally(code_rows, codewords):
    return jax.ops.segment_sum(
        jnp.ones(code_rows.shape, jnp.float32), code_rows, num_segments=codewords
    )


def fine_update(code_term, totals_share, old_share, share_rows):
    part_sums = lax.psum_scatter(
        code_term(jnp.int32(0), lax.axis_size("cell") * share_rows),
        "cell",
        scatter_dimension=0,
        tiled=True,
    )
    return jnp.where(
        totals_share[:, None] > 0, part_sums / jnp.maximum(totals_share, 1.0)[:, None], old_share
    )


def routed_plan(vectors, row_slot, fine_codes, cell_list, coarse_in, fine_in):
    groups = lax.axis_size("cell")
    rows_here, feature = vectors.shape
    listed = cell_list.shape[1]
    slot_count = listed // groups
    owner_cells = coarse_in.shape[0]
    codewords = fine_in.shape[0]
    share_rows = codewords // groups
    share_start = lax.axis_index("cell") * share_rows
    fine_book = fine_in
    fine_share = lax.dynamic_slice_in_dim(fine_in, share_start, share_rows, 0)
    coarse = coarse_in
    list_iota = lax.iota(jnp.int32, listed)
    for sweep in range(2):
        code_totals = lax.psum(code_tally(fine_codes[sweep], codewords), "cell")
        slot_rows = row_slot[sweep]
        code_rows = fine_codes[sweep]
        picked = jnp.take(fine_book, code_rows, axis=0)
        residual = (vectors.astype(jnp.float32) - picked).astype(jnp.bfloat16)
        slot_hot = (slot_rows[None, :] == list_iota[:, None]).astype(jnp.bfloat16)
        slot_sums = jnp.dot(slot_hot, residual, preferred_element_type=jnp.float32)
        slot_counts = jnp.sum(slot_hot, axis=1, dtype=jnp.float32)
        slot_cells = cell_list[sweep].astype(jnp.float32)
        got_sums, got_counts, got_cells = (
            lax.all_to_all(
                slot_sums.reshape(groups, slot_count, feature),
                "cell",
                split_axis=0,
                concat_axis=0,
                tiled=True,
            ),
            lax.all_to_all(
                slot_counts.reshape(groups, slot_count),
                "cell",
                split_axis=0,
                concat_axis=0,
                tiled=True,
            ),
            lax.all_to_all(
                slot_cells.reshape(groups, slot_count),
                "cell",
                split_axis=0,
                concat_axis=0,
                tiled=True,
            ),
        )
        flat_cells = got_cells.reshape(groups * slot_count).astype(jnp.int32)
        cell_sums = jax.ops.segment_sum(
            got_sums.reshape(groups * slot_count, feature), flat_cells, num_segments=owner_cells
        )
        cell_counts = jax.ops.segment_sum(
            got_counts.reshape(groups * slot_count), flat_cells, num_segments=owner_cells
        )
        coarse = jnp.where(
            cell_counts[:, None] > 0, cell_sums / jnp.maximum(cell_counts, 1.0)[:, None], coarse
        )
        returned_rows = jnp.take(coarse, flat_cells, axis=0).reshape(groups, slot_count, feature)
        arrived = lax.all_to_all(returned_rows, "cell", split_axis=0, concat_axis=0, tiled=True)
        entry_centers = arrived.reshape(listed, feature)
        row_centers = jnp.take(entry_centers, slot_rows, axis=0)
        fine_residual = (vectors.astype(jnp.float32) - row_centers).astype(jnp.bfloat16)

        def code_term(start, count, code_rows=code_rows, fine_residual=fine_residual):
            wanted = start + lax.iota(jnp.int32, count)
            code_hot = (code_rows[None, :] == wanted[:, None]).astype(jnp.bfloat16)
            return jnp.dot(code_hot, fine_residual, preferred_element_type=jnp.float32)

        totals_share = lax.dynamic_slice_in_dim(code_totals, share_start, share_rows, 0)
        if sweep == 0:
            full_sums = lax.psum(code_term(0, codewords), "cell")
            fine_book = jnp.where(
                code_totals[:, None] > 0,
                full_sums / jnp.maximum(code_totals, 1.0)[:, None],
                fine_book,
            )
            fine_share = lax.dynamic_slice_in_dim(fine_book, share_start, share_rows, 0)
        else:
            fine_share = fine_update(code_term, totals_share, fine_share, share_rows)
    return (coarse, fine_share)


F32 = jnp.float32
BF16 = jnp.bfloat16
LOW = 256
LANES = 128
PARAMS = pltpu.CompilerParams(vmem_limit_bytes=58 * 2**20)
VMEM = pl.BlockSpec(memory_space=pltpu.VMEM)
SMEM = pl.BlockSpec(memory_space=pltpu.SMEM)
ANY = pl.BlockSpec(memory_space=pl.ANY)


def iota(shape, axis):
    return lax.broadcasted_iota(jnp.int32, shape, axis)


def matmul(left, right):
    return jnp.dot(left, right, preferred_element_type=F32)


def matmul_nt(left, right):
    return lax.dot_general(left, right, (((1,), (1,)), ((), ())), preferred_element_type=F32)


def split(values):
    high = values.astype(BF16)
    return high, (values - high.astype(F32)).astype(BF16)


def hot_rows(codes, rows=LOW):
    inside = jnp.where((codes >= 0) & (codes < rows), codes, -1)
    inside = inside.astype(F32).astype(BF16)
    row = iota((rows, codes.shape[1]), 0).astype(F32).astype(BF16)
    return jnp.where(row == inside, jnp.ones((), BF16), jnp.zeros((), BF16))


def pair_block(codes, slots, listed, high):
    left = hot_rows((codes >> 8) * listed + slots, high * listed)
    return matmul_nt(left, hot_rows(codes & (LOW - 1)))


def pack_kernel(fine_codes, row_slot, cell_list, packed):
    half = fine_codes.shape[1] // 2
    listed = cell_list.shape[1]
    packed[:, half:] = jnp.zeros((8, LANES), jnp.int32)
    for number, ref in enumerate((fine_codes, row_slot)):
        for sweep in range(2):
            for part in range(2):
                row = 4 * number + 2 * sweep + part
                packed[row : row + 1, :half] = ref[
                    sweep : sweep + 1, part * half : (part + 1) * half
                ]
    packed[0:2, half : half + listed] = cell_list[...]


def own_cells_kernel(
    groups, listed, me_ref, vectors, fine_codes, row_slot, fine_in, first_ref, second_ref, to_ref
):
    high = fine_in.shape[0] // LOW
    first = matmul(hot_rows(row_slot[0:1, :], listed), vectors[...])
    second_ref[...] = matmul(hot_rows(row_slot[1:2, :], listed), vectors[...])
    pairs = pair_block(fine_codes[0:1, :], row_slot[0:1, :], listed, high)
    for digit in range(high):
        pairs_high, pairs_low = split(pairs[digit * listed : (digit + 1) * listed])
        both = jnp.concatenate([pairs_high, pairs_low], axis=0)
        book = fine_in[digit * LOW : (digit + 1) * LOW, :]
        book_high, book_low = split(book)
        taken = matmul(both, book_high) + matmul(both, book_low)
        first = first - taken[:listed] - taken[listed:]
    first_ref[...] = first
    slots = listed // groups
    top = groups.bit_length() - 1
    for owner in range(groups):
        block = owner ^ me_ref[0]
        at = sum((1 - (block >> bit & 1)) << (top - 1 - bit) for bit in range(2))
        at = at + groups // 4 - 1 - (block >> 2)
        to_ref[at, 0] = first[owner * slots : (owner + 1) * slots]


def own_codes_kernel(base, vectors, fine_codes, _, sums_ref):
    codes = fine_codes[0:1, :] - base
    for start in range(0, sums_ref.shape[0], 2 * LOW):
        hot = jnp.concatenate(
            [hot_rows(codes - start), hot_rows(codes - start - LOW)], axis=0
        )
        sums_ref[start : start + 2 * LOW, :] = matmul(hot, vectors[...])


def position(block, groups):
    return (block & 1) * (groups // 2) + (block >> 1 & 1) * (groups // 4) + (block >> 2)


def sums_kernel(
    groups,
    slot_count,
    owner_cells,
    cuts,
    orders,
    me_ref,
    codes_ref,
    vectors,
    fine_codes,
    low_sums_ref,
    high_sums_ref,
    first_ref,
    second_ref,
    share_ref,
    *refs,
):
    out_refs, refs = refs[: 3 * len(cuts)], refs[3 * len(cuts) :]
    code_info_ref, entry_info_ref, refs = refs[0], refs[1], refs[2:]
    table0, table1, cell0, cell1, wide, terms, permuted, rows_hot = refs[:8]
    fine, bracket, centers_ref, pairs_ref, left = refs[8:13]
    in_sem, out_sem, stages = refs[13], refs[14], refs[15:]
    me = me_ref[0]
    codewords, feature = fine.shape
    listed = groups * slot_count
    entries = groups * listed
    high = codewords // LOW
    half = codes_ref.shape[2] - LANES
    share_rows = share_ref.shape[0]

    loads = [
        pltpu.make_async_copy(
            ref, fine.at[pl.ds(at * (codewords // 2), codewords // 2)], in_sem.at[at]
        )
        for at, ref in enumerate((low_sums_ref, high_sums_ref))
    ]
    for load in loads:
        load.start()

    rows_hot[...] = iota(rows_hot.shape, 0).astype(F32).astype(BF16)
    one, zero = jnp.ones((), BF16), jnp.zeros((), BF16)

    def hot(codes):
        return jnp.where(rows_hot[...] == codes.astype(F32).astype(BF16), one, zero)

    def device_tables(device, carry):
        at = position(device ^ me, groups)
        for sweep, table in enumerate((table0, table1)):
            block = jnp.zeros((high * listed, LOW), F32)
            for part in range(2):
                row = 2 * sweep + part
                codes = codes_ref[at, row : row + 1, :half]
                slots = codes_ref[at, row + 4 : row + 5, :half]
                block = block + matmul_nt(
                    hot((codes >> 8) * listed + slots)[: high * listed], hot(codes & (LOW - 1))
                )
            rows = pl.ds(pl.multiple_of(device * listed, listed), listed)
            for digit in range(high):
                table[rows, digit * LOW : (digit + 1) * LOW] = block[
                    digit * listed : (digit + 1) * listed
                ]
        return carry

    lax.fori_loop(0, groups, device_tables, 0)
    for device in range(groups):
        at = position(device ^ me, groups)
        for sweep, cell in enumerate((cell0, cell1)):
            row = codes_ref[at, sweep : sweep + 1, half : half + listed]
            cell[device * slot_count : (device + 1) * slot_count, :] = jnp.broadcast_to(
                row, (slot_count, listed)
            )

    row_at = iota((entries, listed), 0)
    owner_of = row_at // listed
    slot_of = owner_of * slot_count + row_at % slot_count
    is_slot = slot_of == iota((entries, listed), 1)
    device_of = (row_at // slot_count) % groups

    def entry_cells(cell):
        tiled = jnp.concatenate([cell[...]] * groups, axis=0)
        picked = jnp.sum(jnp.where(is_slot, tiled, 0), axis=1, keepdims=True)
        return picked.astype(F32)

    owner_col = owner_of[:, :1].astype(F32)
    cells = [entry_cells(cell0), entry_cells(cell1)]
    names = [cell + owner_col * float(owner_cells) for cell in cells]

    entry_row = iota((entries, entries), 0)
    natural = (
        ((entry_row // slot_count) % groups) * listed
        + (entry_row // listed) * slot_count
        + entry_row % slot_count
    )
    order = (natural == iota((entries, entries), 1)).astype(BF16)
    code_counts = [jnp.sum(table[...], axis=0, keepdims=True) for table in (table0, table1)]
    entry_counts = []
    for table in (table0, table1):
        count_high, count_low = split(
            jnp.broadcast_to(jnp.sum(table[...], axis=1, keepdims=True), (entries, LANES))
        )
        entry_counts.append(matmul(order, count_high) + matmul(order, count_low))
    most = jnp.maximum(jnp.max(table0[...]), jnp.max(table1[...]))
    large = most > LOW
    for digit in range(high):
        columns = slice(digit * LOW, (digit + 1) * LOW)
        permuted[0, :, columns] = matmul(order, table1[:, columns].astype(BF16)).astype(BF16)

    @pl.when(large)
    def _():
        for digit in range(high):
            columns = slice(digit * LOW, (digit + 1) * LOW)
            rest = split(table1[:, columns])[1]
            permuted[1, :, columns] = matmul(order, rest).astype(BF16)

    own_row = codes_ref[0, 0:1, half : half + listed].astype(F32)
    own_row = own_row + (iota((1, listed), 1) // slot_count).astype(F32) * float(owner_cells)
    match = (names[0] == own_row).astype(BF16)
    match = lax.dot_general(match, order, (((0,), (0,)), ((), ())), preferred_element_type=F32)
    match = match.astype(BF16)
    held = jnp.zeros((listed, 1), F32)
    for digit in range(high):
        columns = slice(digit * LOW, (digit + 1) * LOW)
        table_high, table_low = split(table0[:, columns])
        used = matmul(match, table_high) + matmul(match, table_low)
        held = held + jnp.sum(used, axis=1, keepdims=True)
        used_high, used_low = split(used)
        wide[0:listed, columns] = used_high.astype(F32)
        wide[listed : 2 * listed, columns] = used_low.astype(F32)
    wide[2 * listed : 2 * listed + 8, :] = jnp.broadcast_to(code_counts[0], (8, codewords))
    wide[2 * listed + 8 : 2 * listed + 16, :] = jnp.broadcast_to(code_counts[1], (8, codewords))
    wide[2 * listed + 16 :, :] = jnp.zeros((LANES - 2 * listed - 16, codewords), F32)
    center_high, center_low = split(first_ref[...] / jnp.maximum(held, 1.0))
    blank = jnp.zeros((LANES - 2 * listed, feature), BF16)
    center_high = jnp.concatenate([center_high, center_high, blank], axis=0)
    center_low = jnp.concatenate([center_low, center_low, blank], axis=0)
    for load in loads:
        load.wait()
    for digit in range(high):
        rows = slice(digit * LOW, (digit + 1) * LOW)
        columns = wide[:, rows].T
        code_info_ref[rows, :] = columns
        taken = jnp.where(iota((LOW, LANES), 1) < 2 * listed, columns, 0.0).astype(BF16)
        first_fine = fine[rows, :] - (matmul(taken, center_high) + matmul(taken, center_low))
        scaled = first_fine / jnp.maximum(columns[:, 2 * listed : 2 * listed + 1], 1.0)
        terms[0, rows, :], terms[1, rows, :] = split(scaled)
        fine[rows, :] = jnp.where(
            columns[:, 2 * listed + 8 : 2 * listed + 9] > 0, 0.0, first_fine
        )
    mine = pl.ds(pl.multiple_of(me * share_rows, share_rows), share_rows)
    empty = code_info_ref[mine, 2 * listed : 2 * listed + 1] == 0
    for part, share in enumerate(split(share_ref[...])):
        terms[part, mine, :] = jnp.where(
            empty, share.astype(F32), terms[part, mine, :].astype(F32)
        ).astype(BF16)

    own_entry = (is_slot & (device_of == me)).astype(BF16)
    second_high, second_low = split(second_ref[...])
    bracket[...] = (
        matmul(own_entry, second_high)
        + matmul(own_entry, second_low)
        - matmul(permuted[0], terms[0])
        - matmul(permuted[0], terms[1])
    )

    @pl.when(large)
    def _():
        bracket[...] -= matmul(permuted[1], terms[0])

    same = (
        jnp.broadcast_to(names[1], (entries, entries))
        == jnp.broadcast_to(names[1], (entries, LANES)).T[0:1, :]
    ).astype(BF16)
    total_high, total_low = split(entry_counts[1])
    totals = matmul(same, total_high) + matmul(same, total_low)
    bracket_high, bracket_low = split(bracket[...])
    centers = matmul(same, bracket_high) + matmul(same, bracket_low)
    centers = centers / jnp.maximum(totals[:, :1], 1.0)
    centers_ref[0], centers_ref[1] = split(centers)
    lane = iota((entries, LANES), 1)
    info = jnp.where(lane == 0, entry_counts[0], entry_counts[1])
    info = jnp.where(lane == 2, cells[0], info)
    entry_info_ref[...] = jnp.where(lane == 3, cells[1], info)

    eye = (iota((LOW, LOW), 0) == iota((LOW, LOW), 1)).astype(BF16)
    for digit in range(high):
        rows = slice(digit * LOW, (digit + 1) * LOW)
        pairs_ref[rows, :] = -matmul_nt(eye, permuted[0, :, rows]).astype(BF16)
    rows_here = vectors.shape[0]
    codes = fine_codes[1:2, :]
    copies = []
    for odd in (1, 0):
        blocks = [at for at in range(groups) if at % 2 == odd]
        for at, block in enumerate(blocks):
            owner = me ^ block
            rows = pl.ds(pl.multiple_of(owner * share_rows, share_rows), share_rows)
            to = slice(at * share_rows, (at + 1) * share_rows)
            left[to, :rows_here] = hot_rows(codes - owner * share_rows, share_rows)
            left[to, rows_here:] = pairs_ref[rows, :]
        start = 0
        for chunk, cut in enumerate(cuts):
            columns = slice(start, start + cut)
            start += cut
            sums = (
                matmul(left[:, :rows_here], vectors[:, columns])
                + matmul(left[:, rows_here:], centers_ref[0, :, columns])
                + matmul(left[:, rows_here:], centers_ref[1, :, columns])
            )
            for part, order_of in enumerate(orders[chunk]):
                if order_of[0] % 2 != odd:
                    continue
                number = 3 * chunk + part
                stage = stages[number]
                for to, block in enumerate(order_of):
                    owner = me ^ block
                    rows = pl.ds(pl.multiple_of(owner * share_rows, share_rows), share_rows)
                    cell_rows = pl.ds(pl.multiple_of(owner * listed, listed), listed)
                    at = blocks.index(block) * share_rows
                    stage[to, :share_rows, :] = sums[at : at + share_rows] + fine[rows, columns]
                    stage[to, share_rows:, :] = bracket[cell_rows, columns]

                @pl.when(large)
                def _():
                    for to, block in enumerate(order_of):
                        owner = me ^ block
                        rows = pl.ds(pl.multiple_of(owner * share_rows, share_rows), share_rows)
                        rest = lax.dot_general(
                            permuted[1, :, rows],
                            centers_ref[0, :, columns],
                            (((0,), (0,)), ((), ())),
                            preferred_element_type=F32,
                        )
                        stage[to, :share_rows, :] -= rest

                copy = pltpu.make_async_copy(stage, out_refs[number], out_sem.at[number])
                copy.start()
                copies.append(copy)
    for copy in copies:
        copy.wait()


def final_kernel(
    groups, slot_count, share_rows, cuts, me_ref, coarse_in, fine_share, first_sums, *refs
):
    last_refs, (code_info, entry_info, coarse_out, fine_out, own_first) = refs[:-5], refs[-5:]
    listed = entry_info.shape[0]
    owner_cells = coarse_in.shape[0]
    by_lane = entry_info[...].T
    for device in range(groups):
        rows = slice(device * slot_count, (device + 1) * slot_count)
        own_first[rows, :] = first_sums[device ^ me_ref[0]]
    hits, counts = [], []
    for sweep in range(2):
        cell = by_lane[2 + sweep : 3 + sweep, :].astype(jnp.int32)
        hit = iota((owner_cells, listed), 0) == cell
        counts.append(
            jnp.sum(jnp.where(hit, by_lane[sweep : sweep + 1, :], 0.0), axis=1, keepdims=True)
        )
        hits.append(hit.astype(BF16))
    first_count = code_info[:, 2 * listed : 2 * listed + 1]
    last_count = code_info[:, 2 * listed + 8 : 2 * listed + 9]
    count = jnp.where(last_count > 0, last_count, first_count)
    start = 0
    for cut, last_sums in zip(cuts, last_refs):
        columns = slice(start, start + cut)
        start += cut
        coarse = coarse_in[:, columns]
        for sweep, sums in enumerate((own_first[:, columns], last_sums[share_rows:, :])):
            sums_high, sums_low = split(sums)
            found = matmul(hits[sweep], sums_high) + matmul(hits[sweep], sums_low)
            weight = 1.0 / jnp.maximum(counts[sweep], 1.0)
            coarse = jnp.where(counts[sweep] > 0, found * weight, coarse)
        coarse_out[:, columns] = coarse
        fine_out[:, columns] = jnp.where(
            count > 0,
            last_sums[:share_rows, :] * (1.0 / jnp.maximum(count, 1.0)),
            fine_share[:, columns],
        )


def exchange(values, step):
    groups = lax.axis_size("cell")
    return lax.ppermute(values, "cell", [(at, at ^ step) for at in range(groups)])


def block_order(bits):
    order = [0]
    for bit in list(bits)[::-1]:
        order = [block + (1 << bit) for block in order] + order
    return order


def block_orders(bits):
    order = block_order(bits)
    half = len(order) // 2
    return [block + 1 for block in order], order[:half], order[half:]


def after(values, *others):
    return lax.optimization_barrier((values, *others))[0]


def halved(got, other, kept):
    half = other.shape[0]
    return other + got[:half], kept + got[half:]


def swap(blocks, bit):
    half = blocks.shape[0] // 2
    got = exchange(blocks[:half], 1 << bit)
    return jnp.concatenate([blocks[half:], got], axis=1)


def local(kernel, shapes, in_specs, out_specs, scratch, flops, name, aliases=None):
    return pl.pallas_call(
        kernel,
        out_shape=tuple(jax.ShapeDtypeStruct(shape, dtype) for shape, dtype in shapes),
        grid_spec=pltpu.PrefetchScalarGridSpec(
            num_scalar_prefetch=1,
            grid=(1,),
            in_specs=in_specs,
            out_specs=out_specs,
            scratch_shapes=scratch,
        ),
        input_output_aliases=aliases or {},
        compiler_params=PARAMS,
        cost_estimate=pl.CostEstimate(
            flops=int(flops), bytes_accessed=10**6, transcendentals=0
        ),
        name=name,
    )


def block(shape, *place):
    return pl.BlockSpec(
        shape, lambda step, me: tuple(me[0] if at is None else at for at in place)
    )


def dense_plan(vectors, row_slot, fine_codes, cell_list, coarse_in, fine_in):
    groups = lax.axis_size("cell")
    rows_here, feature = vectors.shape
    listed = cell_list.shape[1]
    slot_count = listed // groups
    owner_cells = coarse_in.shape[0]
    codewords = fine_in.shape[0]
    share_rows = codewords // groups
    entries = groups * listed
    half = rows_here // 2
    me = lax.axis_index("cell").reshape(1).astype(jnp.int32)

    packed = local(
        lambda me_ref, *refs: pack_kernel(*refs),
        [((8, half + LANES), jnp.int32)],
        [VMEM] * 3,
        [VMEM],
        [],
        1e9,
        "pack",
    )(me, fine_codes, row_slot, cell_list)[0]
    first, second, first_to = local(
        lambda *refs: own_cells_kernel(groups, listed, *refs),
        [((listed, feature), F32)] * 2 + [((groups, 1, slot_count, feature), F32)],
        [VMEM] * 4,
        [VMEM] * 3,
        [],
        5e9,
        "own_cells",
    )(me, vectors, fine_codes, row_slot, fine_in)
    far = groups // 4
    gathered = jnp.stack([packed] + [exchange(packed, 4 * step) for step in range(1, far)])
    sums = []
    for step, base in ((2, 0), (1, codewords // 2)):
        sums += local(
            lambda me_ref, *refs, base=base: own_codes_kernel(base, *refs),
            [((codewords // 2, feature), F32)],
            [VMEM, VMEM, ANY],
            [VMEM],
            [],
            6e9,
            "own_codes",
        )(me, vectors, fine_codes, gathered)
        gathered = jnp.concatenate([gathered, exchange(gathered, step)])
        if step == 2:
            first_to = swap(first_to, 0)

    top = groups.bit_length() - 1
    near_first = list(range(1, top))
    far_first = near_first[1:] + near_first[:1]
    cuts = [feature // 3] * 3
    bits = [near_first, far_first, near_first]
    orders = [block_orders(each) for each in bits]
    shapes = [
        (len(order), share_rows + listed, cut)
        for cut, three in zip(cuts, orders)
        for order in three
    ]
    *terms, code_info, entry_info = local(
        lambda *refs: sums_kernel(groups, slot_count, owner_cells, cuts, orders, *refs),
        [(shape, F32) for shape in shapes]
        + [((codewords, LANES), F32), ((entries, LANES), F32)],
        [VMEM] * 3 + [ANY] * 2 + [VMEM] * 2 + [block((share_rows, feature), None, 0)],
        [ANY] * len(shapes) + [VMEM] * 2,
        [
            pltpu.VMEM((entries, codewords), F32),
            pltpu.VMEM((entries, codewords), F32),
            pltpu.VMEM((listed, listed), jnp.int32),
            pltpu.VMEM((listed, listed), jnp.int32),
            pltpu.VMEM((LANES, codewords), F32),
            pltpu.VMEM((2, codewords, feature), BF16),
            pltpu.VMEM((2, entries, codewords), BF16),
            pltpu.VMEM((LOW, half), BF16),
            pltpu.VMEM((codewords, feature), F32),
            pltpu.VMEM((entries, feature), F32),
            pltpu.VMEM((2, entries, feature), BF16),
            pltpu.VMEM((codewords, entries), BF16),
            pltpu.VMEM((codewords // 2, rows_here + entries), BF16),
            pltpu.SemaphoreType.DMA((2,)),
            pltpu.SemaphoreType.DMA((len(shapes),)),
        ]
        + [pltpu.VMEM(shape, F32) for shape in shapes],
        40e9,
        "sums",
    )(me, gathered, vectors, fine_codes, *sums, first, second, fine_in)

    first_to = swap(after(first_to, terms[0]), 1)
    finished = []
    for at, steps in enumerate(bits):
        away, other, kept = terms[3 * at : 3 * at + 3]
        other, kept = halved(exchange(away, 1), other, kept)
        if at == len(bits) - 1:
            first_to = after(first_to, other)[::-1]
            first_to = jnp.concatenate(
                [first_to[0]] + [exchange(first_to[z], 4 * z) for z in range(1, far)]
            )
        for bit in steps[:-1]:
            got = exchange(other, 1 << bit)
            half = got.shape[0] // 2
            other, kept = halved(got, kept[:half], kept[half:])
        finished.append((kept + exchange(other, 1 << steps[-1]))[0])
    return local(
        lambda *refs: final_kernel(groups, slot_count, share_rows, cuts, *refs),
        [(coarse_in.shape, F32), ((share_rows, feature), F32)],
        [VMEM, block((share_rows, feature), None, 0)]
        + [VMEM] * (1 + len(cuts))
        + [block((share_rows, LANES), None, 0), block((listed, LANES), None, 0)],
        [VMEM] * 2,
        [pltpu.VMEM((listed, feature), F32)],
        1e9,
        "outputs",
    )(me, coarse_in, fine_in, first_to, *finished, code_info, entry_info)


def fits_dense(mesh_groups, listed, codewords, rows_here, feature):
    entries = mesh_groups * listed
    power = mesh_groups & (mesh_groups - 1) == 0 and mesh_groups >= 4
    digits = codewords % (2 * LOW) == 0 and (codewords // LOW) * listed <= LOW
    shapes = rows_here % (2 * LANES) == 0 and feature % (6 * LANES) == 0
    return power and digits and shapes and entries * codewords <= 2**20


def per_device(vectors, row_slot, fine_codes, cell_list, coarse_in, fine_in):
    groups = lax.axis_size("cell")
    dense = fits_dense(groups, cell_list.shape[1], *fine_in.shape[:1], *vectors.shape)
    plan = dense_plan if dense else routed_plan
    return plan(vectors, row_slot, fine_codes, cell_list, coarse_in, fine_in)


def solution(mesh):
    return jax.shard_map(
        per_device,
        mesh=mesh,
        in_specs=(
            P(("parts", "cell"), None),
            P(None, ("parts", "cell")),
            P(None, ("parts", "cell")),
            P(None, ("parts", "cell")),
            P("cell", None),
            P(),
        ),
        out_specs=(P(("parts", "cell"), None), P(("parts", "cell"), None)),
        check_vma=False,
    )
```

```python
import jax
import jax.numpy as jnp
from jax import lax
from jax.experimental import pallas as pl
from jax.experimental.pallas import tpu as pltpu
from jax.sharding import PartitionSpec as P


def code_tally(code_rows, codewords):
    return jax.ops.segment_sum(
        jnp.ones(code_rows.shape, jnp.float32), code_rows, num_segments=codewords
    )


def fine_update(code_term, totals_share, old_share, share_rows):
    part_sums = lax.psum_scatter(
        code_term(jnp.int32(0), lax.axis_size("cell") * share_rows),
        "cell",
        scatter_dimension=0,
        tiled=True,
    )
    return jnp.where(
        totals_share[:, None] > 0, part_sums / jnp.maximum(totals_share, 1.0)[:, None], old_share
    )


def routed_plan(vectors, row_slot, fine_codes, cell_list, coarse_in, fine_in):
    groups = lax.axis_size("cell")
    rows_here, feature = vectors.shape
    listed = cell_list.shape[1]
    slot_count = listed // groups
    owner_cells = coarse_in.shape[0]
    codewords = fine_in.shape[0]
    share_rows = codewords // groups
    share_start = lax.axis_index("cell") * share_rows
    fine_book = fine_in
    fine_share = lax.dynamic_slice_in_dim(fine_in, share_start, share_rows, 0)
    coarse = coarse_in
    list_iota = lax.iota(jnp.int32, listed)
    for sweep in range(2):
        code_totals = lax.psum(code_tally(fine_codes[sweep], codewords), "cell")
        slot_rows = row_slot[sweep]
        code_rows = fine_codes[sweep]
        picked = jnp.take(fine_book, code_rows, axis=0)
        residual = (vectors.astype(jnp.float32) - picked).astype(jnp.bfloat16)
        slot_hot = (slot_rows[None, :] == list_iota[:, None]).astype(jnp.bfloat16)
        slot_sums = jnp.dot(slot_hot, residual, preferred_element_type=jnp.float32)
        slot_counts = jnp.sum(slot_hot, axis=1, dtype=jnp.float32)
        slot_cells = cell_list[sweep].astype(jnp.float32)
        got_sums, got_counts, got_cells = (
            lax.all_to_all(
                slot_sums.reshape(groups, slot_count, feature),
                "cell",
                split_axis=0,
                concat_axis=0,
                tiled=True,
            ),
            lax.all_to_all(
                slot_counts.reshape(groups, slot_count),
                "cell",
                split_axis=0,
                concat_axis=0,
                tiled=True,
            ),
            lax.all_to_all(
                slot_cells.reshape(groups, slot_count),
                "cell",
                split_axis=0,
                concat_axis=0,
                tiled=True,
            ),
        )
        flat_cells = got_cells.reshape(groups * slot_count).astype(jnp.int32)
        cell_sums = jax.ops.segment_sum(
            got_sums.reshape(groups * slot_count, feature), flat_cells, num_segments=owner_cells
        )
        cell_counts = jax.ops.segment_sum(
            got_counts.reshape(groups * slot_count), flat_cells, num_segments=owner_cells
        )
        coarse = jnp.where(
            cell_counts[:, None] > 0, cell_sums / jnp.maximum(cell_counts, 1.0)[:, None], coarse
        )
        returned_rows = jnp.take(coarse, flat_cells, axis=0).reshape(groups, slot_count, feature)
        arrived = lax.all_to_all(returned_rows, "cell", split_axis=0, concat_axis=0, tiled=True)
        entry_centers = arrived.reshape(listed, feature)
        row_centers = jnp.take(entry_centers, slot_rows, axis=0)
        fine_residual = (vectors.astype(jnp.float32) - row_centers).astype(jnp.bfloat16)

        def code_term(start, count, code_rows=code_rows, fine_residual=fine_residual):
            wanted = start + lax.iota(jnp.int32, count)
            code_hot = (code_rows[None, :] == wanted[:, None]).astype(jnp.bfloat16)
            return jnp.dot(code_hot, fine_residual, preferred_element_type=jnp.float32)

        totals_share = lax.dynamic_slice_in_dim(code_totals, share_start, share_rows, 0)
        if sweep == 0:
            full_sums = lax.psum(code_term(0, codewords), "cell")
            fine_book = jnp.where(
                code_totals[:, None] > 0,
                full_sums / jnp.maximum(code_totals, 1.0)[:, None],
                fine_book,
            )
            fine_share = lax.dynamic_slice_in_dim(fine_book, share_start, share_rows, 0)
        else:
            fine_share = fine_update(code_term, totals_share, fine_share, share_rows)
    return (coarse, fine_share)


F32 = jnp.float32
BF16 = jnp.bfloat16
LOW = 256
LANES = 128
PARAMS = pltpu.CompilerParams(vmem_limit_bytes=58 * 2**20)
VMEM = pl.BlockSpec(memory_space=pltpu.VMEM)
SMEM = pl.BlockSpec(memory_space=pltpu.SMEM)
ANY = pl.BlockSpec(memory_space=pl.ANY)


def iota(shape, axis):
    return lax.broadcasted_iota(jnp.int32, shape, axis)


def matmul(left, right):
    return jnp.dot(left, right, preferred_element_type=F32)


def matmul_nt(left, right):
    return lax.dot_general(left, right, (((1,), (1,)), ((), ())), preferred_element_type=F32)


def split(values):
    high = values.astype(BF16)
    return high, (values - high.astype(F32)).astype(BF16)


def hot_rows(codes, rows=LOW):
    inside = jnp.where((codes >= 0) & (codes < rows), codes, -1)
    inside = inside.astype(F32).astype(BF16)
    row = iota((rows, codes.shape[1]), 0).astype(F32).astype(BF16)
    return jnp.where(row == inside, jnp.ones((), BF16), jnp.zeros((), BF16))


def pair_block(codes, slots, listed, high):
    left = hot_rows((codes >> 8) * listed + slots, high * listed)
    return matmul_nt(left, hot_rows(codes & (LOW - 1)))


def pack_kernel(fine_codes, row_slot, cell_list, packed):
    half = fine_codes.shape[1] // 2
    listed = cell_list.shape[1]
    packed[:, half:] = jnp.zeros((8, LANES), jnp.int32)
    for number, ref in enumerate((fine_codes, row_slot)):
        for sweep in range(2):
            for part in range(2):
                row = 4 * number + 2 * sweep + part
                packed[row : row + 1, :half] = ref[
                    sweep : sweep + 1, part * half : (part + 1) * half
                ]
    packed[0:2, half : half + listed] = cell_list[...]


def own_cells_kernel(
    groups, listed, me_ref, vectors, fine_codes, row_slot, fine_in, first_ref, second_ref, to_ref
):
    high = fine_in.shape[0] // LOW
    first = matmul(hot_rows(row_slot[0:1, :], listed), vectors[...])
    second_ref[...] = matmul(hot_rows(row_slot[1:2, :], listed), vectors[...])
    pairs = pair_block(fine_codes[0:1, :], row_slot[0:1, :], listed, high)
    for digit in range(high):
        pairs_high, pairs_low = split(pairs[digit * listed : (digit + 1) * listed])
        both = jnp.concatenate([pairs_high, pairs_low], axis=0)
        book = fine_in[digit * LOW : (digit + 1) * LOW, :]
        book_high, book_low = split(book)
        taken = matmul(both, book_high) + matmul(both, book_low)
        first = first - taken[:listed] - taken[listed:]
    first_ref[...] = first
    slots = listed // groups
    top = groups.bit_length() - 1
    for owner in range(groups):
        block = owner ^ me_ref[0]
        at = sum((1 - (block >> bit & 1)) << (top - 1 - bit) for bit in range(2))
        at = at + groups // 4 - 1 - (block >> 2)
        to_ref[at, 0] = first[owner * slots : (owner + 1) * slots]


def own_codes_kernel(base, vectors, fine_codes, _, sums_ref):
    codes = fine_codes[0:1, :] - base
    for start in range(0, sums_ref.shape[0], 2 * LOW):
        hot = jnp.concatenate(
            [hot_rows(codes - start), hot_rows(codes - start - LOW)], axis=0
        )
        sums_ref[start : start + 2 * LOW, :] = matmul(hot, vectors[...])


def position(block, groups):
    return (block & 1) * (groups // 2) + (block >> 1 & 1) * (groups // 4) + (block >> 2)


def sums_kernel(
    groups,
    slot_count,
    owner_cells,
    cuts,
    orders,
    me_ref,
    codes_ref,
    vectors,
    fine_codes,
    low_sums_ref,
    high_sums_ref,
    first_ref,
    second_ref,
    share_ref,
    _,
    *refs,
):
    out_refs, refs = refs[: 3 * len(cuts)], refs[3 * len(cuts) :]
    code_info_ref, entry_info_ref, refs = refs[0], refs[1], refs[2:]
    table0, table1, cell0, cell1, wide, terms, permuted, rows_hot = refs[:8]
    fine, bracket, centers_ref, pairs_ref, left = refs[8:13]
    in_sem, out_sem, stages = refs[13], refs[14], refs[15:]
    me = me_ref[0]
    codewords, feature = fine.shape
    listed = groups * slot_count
    entries = groups * listed
    high = codewords // LOW
    half = codes_ref.shape[2] - LANES
    share_rows = share_ref.shape[0]

    loads = [
        pltpu.make_async_copy(
            ref, fine.at[pl.ds(at * (codewords // 2), codewords // 2)], in_sem.at[at]
        )
        for at, ref in enumerate((low_sums_ref, high_sums_ref))
    ]
    for load in loads:
        load.start()

    rows_hot[...] = iota(rows_hot.shape, 0).astype(F32).astype(BF16)
    one, zero = jnp.ones((), BF16), jnp.zeros((), BF16)

    def hot(codes):
        rows = rows_hot[:, : codes.shape[1]]
        return jnp.where(rows == codes.astype(F32).astype(BF16), one, zero)

    def device_tables(device, carry):
        at = position(device ^ me, groups)
        for sweep, table in enumerate((table0, table1)):
            block = jnp.zeros((high * listed, LOW), F32)
            for part in range(2):
                row = 2 * sweep + part
                codes = codes_ref[at, row : row + 1, :half]
                slots = codes_ref[at, row + 4 : row + 5, :half]
                block = block + matmul_nt(
                    hot((codes >> 8) * listed + slots)[: high * listed], hot(codes & (LOW - 1))
                )
            rows = pl.ds(pl.multiple_of(device * listed, listed), listed)
            for digit in range(high):
                table[rows, digit * LOW : (digit + 1) * LOW] = block[
                    digit * listed : (digit + 1) * listed
                ]
        return carry

    lax.fori_loop(0, groups, device_tables, 0)
    for device in range(groups):
        at = position(device ^ me, groups)
        for sweep, cell in enumerate((cell0, cell1)):
            row = codes_ref[at, sweep : sweep + 1, half : half + listed]
            cell[device * slot_count : (device + 1) * slot_count, :] = jnp.broadcast_to(
                row, (slot_count, listed)
            )

    row_at = iota((entries, listed), 0)
    owner_of = row_at // listed
    slot_of = owner_of * slot_count + row_at % slot_count
    is_slot = slot_of == iota((entries, listed), 1)
    device_of = (row_at // slot_count) % groups

    def entry_cells(cell):
        tiled = jnp.concatenate([cell[...]] * groups, axis=0)
        picked = jnp.sum(jnp.where(is_slot, tiled, 0), axis=1, keepdims=True)
        return picked.astype(F32)

    owner_col = owner_of[:, :1].astype(F32)
    cells = [entry_cells(cell0), entry_cells(cell1)]
    names = [cell + owner_col * float(owner_cells) for cell in cells]

    entry_row = iota((entries, entries), 0)
    natural = (
        ((entry_row // slot_count) % groups) * listed
        + (entry_row // listed) * slot_count
        + entry_row % slot_count
    )
    order = (natural == iota((entries, entries), 1)).astype(BF16)
    code_counts = [jnp.sum(table[...], axis=0, keepdims=True) for table in (table0, table1)]
    entry_counts, most = [], 0.0
    for sweep, table in enumerate((table0, table1)):
        entry_count = jnp.sum(table[...], axis=1, keepdims=True)
        most = jnp.maximum(
            most, jnp.minimum(jnp.max(entry_count), jnp.max(code_counts[sweep]))
        )
        count_high, count_low = split(jnp.broadcast_to(entry_count, (entries, LANES)))
        entry_counts.append(matmul(order, count_high) + matmul(order, count_low))
    large = most > LOW
    for digit in range(high):
        columns = slice(digit * LOW, (digit + 1) * LOW)
        permuted[0, :, columns] = matmul(order, table1[:, columns].astype(BF16)).astype(BF16)

    @pl.when(large)
    def _():
        for digit in range(high):
            columns = slice(digit * LOW, (digit + 1) * LOW)
            rest = split(table1[:, columns])[1]
            permuted[1, :, columns] = matmul(order, rest).astype(BF16)

    own_row = codes_ref[0, 0:1, half : half + listed].astype(F32)
    own_row = own_row + (iota((1, listed), 1) // slot_count).astype(F32) * float(owner_cells)
    match = (names[0] == own_row).astype(BF16)
    match = lax.dot_general(match, order, (((0,), (0,)), ((), ())), preferred_element_type=F32)
    match = match.astype(BF16)
    for digit in range(high):
        columns = slice(digit * LOW, (digit + 1) * LOW)
        wide[0:listed, columns] = matmul(match, table0[:, columns].astype(BF16))

    @pl.when(large)
    def _():
        for digit in range(high):
            columns = slice(digit * LOW, (digit + 1) * LOW)
            wide[0:listed, columns] += matmul(match, split(table0[:, columns])[1])

    held = jnp.sum(wide[0:listed, :], axis=1, keepdims=True)
    used_high, used_low = split(wide[0:listed, :])
    wide[0:listed, :] = used_high.astype(F32)
    wide[listed : 2 * listed, :] = used_low.astype(F32)
    wide[2 * listed : 2 * listed + 8, :] = jnp.broadcast_to(code_counts[0], (8, codewords))
    wide[2 * listed + 8 : 2 * listed + 16, :] = jnp.broadcast_to(code_counts[1], (8, codewords))
    wide[2 * listed + 16 :, :] = jnp.zeros((LANES - 2 * listed - 16, codewords), F32)
    center_high, center_low = split(first_ref[...] / jnp.maximum(held, 1.0))
    blank = jnp.zeros((LANES - 2 * listed, feature), BF16)
    center_high = jnp.concatenate([center_high, center_high, blank], axis=0)
    center_low = jnp.concatenate([center_low, center_low, blank], axis=0)
    for load in loads:
        load.wait()
    for digit in range(high):
        rows = slice(digit * LOW, (digit + 1) * LOW)
        columns = wide[:, rows].T
        code_info_ref[rows, :] = columns
        taken = jnp.where(iota((LOW, LANES), 1) < 2 * listed, columns, 0.0).astype(BF16)
        first_fine = fine[rows, :] - (matmul(taken, center_high) + matmul(taken, center_low))
        scaled = first_fine * (1.0 / jnp.maximum(columns[:, 2 * listed : 2 * listed + 1], 1.0))
        terms[0, rows, :], terms[1, rows, :] = split(scaled)
        fine[rows, :] = jnp.where(
            columns[:, 2 * listed + 8 : 2 * listed + 9] > 0, 0.0, first_fine
        )
    mine = pl.ds(pl.multiple_of(me * share_rows, share_rows), share_rows)
    empty = code_info_ref[mine, 2 * listed : 2 * listed + 1] == 0
    for part, share in enumerate(split(share_ref[...])):
        terms[part, mine, :] = jnp.where(
            empty, share.astype(F32), terms[part, mine, :].astype(F32)
        ).astype(BF16)

    own_entry = (is_slot & (device_of == me)).astype(BF16)
    second_high, second_low = split(second_ref[...])
    bracket[...] = (
        matmul(own_entry, second_high)
        + matmul(own_entry, second_low)
        - matmul(permuted[0], terms[0])
        - matmul(permuted[0], terms[1])
    )

    @pl.when(large)
    def _():
        bracket[...] -= matmul(permuted[1], terms[0])

    same = (
        jnp.broadcast_to(names[1], (entries, entries))
        == jnp.broadcast_to(names[1], (entries, LANES)).T[0:1, :]
    ).astype(BF16)
    total_high, total_low = split(entry_counts[1])
    totals = matmul(same, total_high) + matmul(same, total_low)
    bracket_high, bracket_low = split(bracket[...])
    centers = matmul(same, bracket_high) + matmul(same, bracket_low)
    centers = centers * (1.0 / jnp.maximum(totals[:, :1], 1.0))
    centers_ref[0], centers_ref[1] = split(centers)
    lane = iota((entries, LANES), 1)
    info = jnp.where(lane == 0, entry_counts[0], entry_counts[1])
    info = jnp.where(lane == 2, cells[0], info)
    entry_info_ref[...] = jnp.where(lane == 3, cells[1], info)

    eye = (iota((LOW, LOW), 0) == iota((LOW, LOW), 1)).astype(BF16)
    for digit in range(high):
        rows = slice(digit * LOW, (digit + 1) * LOW)
        pairs_ref[rows, :] = -matmul_nt(eye, permuted[0, :, rows]).astype(BF16)
    rows_here = vectors.shape[0]
    codes = fine_codes[1:2, :]
    copies = []
    for odd in (1, 0):
        blocks = [at for at in range(groups) if at % 2 == odd]
        for at, block in enumerate(blocks):
            owner = me ^ block
            rows = pl.ds(pl.multiple_of(owner * share_rows, share_rows), share_rows)
            to = slice(at * share_rows, (at + 1) * share_rows)
            own = codes - owner * share_rows
            own = jnp.where((own >= 0) & (own < share_rows), own, -1)
            left[to, :rows_here] = hot(own)[:share_rows]
            left[to, rows_here:] = pairs_ref[rows, :]
        start = 0
        for chunk, cut in enumerate(cuts):
            columns = slice(start, start + cut)
            start += cut
            sums = (
                matmul(left[:, :rows_here], vectors[:, columns])
                + matmul(left[:, rows_here:], centers_ref[0, :, columns])
                + matmul(left[:, rows_here:], centers_ref[1, :, columns])
            )
            for part, order_of in enumerate(orders[chunk]):
                if order_of[0] % 2 != odd:
                    continue
                number = 3 * chunk + part
                stage = stages[number]
                for to, block in enumerate(order_of):
                    owner = me ^ block
                    rows = pl.ds(pl.multiple_of(owner * share_rows, share_rows), share_rows)
                    cell_rows = pl.ds(pl.multiple_of(owner * listed, listed), listed)
                    at = blocks.index(block) * share_rows
                    stage[to, :share_rows, :] = sums[at : at + share_rows] + fine[rows, columns]
                    stage[to, share_rows:, :] = bracket[cell_rows, columns]

                @pl.when(large)
                def _():
                    for to, block in enumerate(order_of):
                        owner = me ^ block
                        rows = pl.ds(pl.multiple_of(owner * share_rows, share_rows), share_rows)
                        rest = lax.dot_general(
                            permuted[1, :, rows],
                            centers_ref[0, :, columns],
                            (((0,), (0,)), ((), ())),
                            preferred_element_type=F32,
                        )
                        stage[to, :share_rows, :] -= rest

                copy = pltpu.make_async_copy(stage, out_refs[number], out_sem.at[number])
                copy.start()
                copies.append(copy)
    for copy in copies:
        copy.wait()


def final_kernel(
    groups, slot_count, share_rows, cuts, me_ref, coarse_in, fine_share, first_sums, *refs
):
    last_refs, (code_info, entry_info, coarse_out, fine_out, own_first) = refs[:-5], refs[-5:]
    listed = entry_info.shape[0]
    owner_cells = coarse_in.shape[0]
    by_lane = entry_info[...].T
    for device in range(groups):
        rows = slice(device * slot_count, (device + 1) * slot_count)
        own_first[rows, :] = first_sums[device ^ me_ref[0]]
    hits, counts = [], []
    for sweep in range(2):
        cell = by_lane[2 + sweep : 3 + sweep, :].astype(jnp.int32)
        hit = iota((owner_cells, listed), 0) == cell
        counts.append(
            jnp.sum(jnp.where(hit, by_lane[sweep : sweep + 1, :], 0.0), axis=1, keepdims=True)
        )
        hits.append(hit.astype(BF16))
    first_count = code_info[:, 2 * listed : 2 * listed + 1]
    last_count = code_info[:, 2 * listed + 8 : 2 * listed + 9]
    count = jnp.where(last_count > 0, last_count, first_count)
    start = 0
    for cut, kept, got in zip(cuts, last_refs[::2], last_refs[1::2]):
        last_sums = kept[0] + got[0]
        columns = slice(start, start + cut)
        start += cut
        coarse = coarse_in[:, columns]
        for sweep, sums in enumerate((own_first[:, columns], last_sums[share_rows:, :])):
            sums_high, sums_low = split(sums)
            found = matmul(hits[sweep], sums_high) + matmul(hits[sweep], sums_low)
            weight = 1.0 / jnp.maximum(counts[sweep], 1.0)
            coarse = jnp.where(counts[sweep] > 0, found * weight, coarse)
        coarse_out[:, columns] = coarse
        fine_out[:, columns] = jnp.where(
            count > 0,
            last_sums[:share_rows, :] * (1.0 / jnp.maximum(count, 1.0)),
            fine_share[:, columns],
        )


def exchange(values, step):
    groups = lax.axis_size("cell")
    return lax.ppermute(values, "cell", [(at, at ^ step) for at in range(groups)])


def block_order(bits):
    order = [0]
    for bit in list(bits)[::-1]:
        order = [block + (1 << bit) for block in order] + order
    return order


def block_orders(bits):
    order = block_order(bits)
    half = len(order) // 2
    return [block + 1 for block in order], order[:half], order[half:]


def after(values, *others):
    return lax.optimization_barrier((values, *others))[0]


def halved(got, other, kept):
    half = other.shape[0]
    return other + got[:half], kept + got[half:]


def swap(blocks, bit):
    half = blocks.shape[0] // 2
    got = exchange(blocks[:half], 1 << bit)
    return jnp.concatenate([blocks[half:], got], axis=1)


def local(kernel, shapes, in_specs, out_specs, scratch, flops, name, aliases=None):
    return pl.pallas_call(
        kernel,
        out_shape=tuple(jax.ShapeDtypeStruct(shape, dtype) for shape, dtype in shapes),
        grid_spec=pltpu.PrefetchScalarGridSpec(
            num_scalar_prefetch=1,
            grid=(1,),
            in_specs=in_specs,
            out_specs=out_specs,
            scratch_shapes=scratch,
        ),
        input_output_aliases=aliases or {},
        compiler_params=PARAMS,
        cost_estimate=pl.CostEstimate(
            flops=int(flops), bytes_accessed=10**6, transcendentals=0
        ),
        name=name,
    )


def block(shape, *place):
    return pl.BlockSpec(
        shape, lambda step, me: tuple(me[0] if at is None else at for at in place)
    )


def dense_plan(vectors, row_slot, fine_codes, cell_list, coarse_in, fine_in):
    groups = lax.axis_size("cell")
    rows_here, feature = vectors.shape
    listed = cell_list.shape[1]
    slot_count = listed // groups
    owner_cells = coarse_in.shape[0]
    codewords = fine_in.shape[0]
    share_rows = codewords // groups
    entries = groups * listed
    half = rows_here // 2
    me = lax.axis_index("cell").reshape(1).astype(jnp.int32)

    packed = local(
        lambda me_ref, *refs: pack_kernel(*refs),
        [((8, half + LANES), jnp.int32)],
        [VMEM] * 3,
        [VMEM],
        [],
        1e9,
        "pack",
    )(me, fine_codes, row_slot, cell_list)[0]
    first, second, first_to = local(
        lambda *refs: own_cells_kernel(groups, listed, *refs),
        [((listed, feature), F32)] * 2 + [((groups, 1, slot_count, feature), F32)],
        [VMEM] * 4,
        [VMEM] * 3,
        [],
        5e9,
        "own_cells",
    )(me, vectors, fine_codes, row_slot, fine_in)
    far = groups // 4
    gathered = jnp.stack([packed] + [exchange(packed, 4 * step) for step in range(1, far)])
    sums = []
    for step, base in ((2, 0), (1, codewords // 2)):
        sums += local(
            lambda me_ref, *refs, base=base: own_codes_kernel(base, *refs),
            [((codewords // 2, feature), F32)],
            [VMEM, VMEM, ANY],
            [VMEM],
            [],
            6e9,
            "own_codes",
        )(me, vectors, fine_codes, gathered)
        first_to = swap(after(first_to, gathered), 2 - step)
        gathered = jnp.concatenate([gathered, exchange(gathered, step)])

    top = groups.bit_length() - 1
    near_first = list(range(1, top))
    far_first = near_first[1:] + near_first[:1]
    cuts = [feature // 3] * 3
    bits = [near_first, far_first, near_first]
    orders = [block_orders(each) for each in bits]
    shapes = [
        (len(order), share_rows + listed, cut)
        for cut, three in zip(cuts, orders)
        for order in three
    ]
    *terms, code_info, entry_info = local(
        lambda *refs: sums_kernel(groups, slot_count, owner_cells, cuts, orders, *refs),
        [(shape, F32) for shape in shapes]
        + [((codewords, LANES), F32), ((entries, LANES), F32)],
        [VMEM] * 3 + [ANY] * 2 + [VMEM] * 2 + [block((share_rows, feature), None, 0), ANY],
        [ANY] * len(shapes) + [VMEM] * 2,
        [
            pltpu.VMEM((entries, codewords), F32),
            pltpu.VMEM((entries, codewords), F32),
            pltpu.VMEM((listed, listed), jnp.int32),
            pltpu.VMEM((listed, listed), jnp.int32),
            pltpu.VMEM((LANES, codewords), F32),
            pltpu.VMEM((2, codewords, feature), BF16),
            pltpu.VMEM((2, entries, codewords), BF16),
            pltpu.VMEM((LOW, rows_here), BF16),
            pltpu.VMEM((codewords, feature), F32),
            pltpu.VMEM((entries, feature), F32),
            pltpu.VMEM((2, entries, feature), BF16),
            pltpu.VMEM((codewords, entries), BF16),
            pltpu.VMEM((codewords // 2, rows_here + entries), BF16),
            pltpu.SemaphoreType.DMA((2,)),
            pltpu.SemaphoreType.DMA((len(shapes),)),
        ]
        + [pltpu.VMEM(shape, F32) for shape in shapes],
        40e9,
        "sums",
    )(me, gathered, vectors, fine_codes, *sums, first, second, fine_in, first_to)

    finished = []
    for at, steps in enumerate(bits):
        away, other, kept = terms[3 * at : 3 * at + 3]
        other, kept = halved(exchange(away, 1), other, kept)
        if at == len(bits) - 1:
            first_to = after(first_to, other)[::-1]
            first_to = jnp.concatenate(
                [first_to[0]] + [exchange(first_to[z], 4 * z) for z in range(1, far)]
            )
        for bit in steps[:-1]:
            got = exchange(other, 1 << bit)
            half = got.shape[0] // 2
            other, kept = halved(got, kept[:half], kept[half:])
        finished += [kept, exchange(other, 1 << steps[-1])]
    return local(
        lambda *refs: final_kernel(groups, slot_count, share_rows, cuts, *refs),
        [(coarse_in.shape, F32), ((share_rows, feature), F32)],
        [VMEM, block((share_rows, feature), None, 0)]
        + [VMEM] * (1 + 2 * len(cuts))
        + [block((share_rows, LANES), None, 0), block((listed, LANES), None, 0)],
        [VMEM] * 2,
        [pltpu.VMEM((listed, feature), F32)],
        1e9,
        "outputs",
    )(me, coarse_in, fine_in, first_to, *finished, code_info, entry_info)


def fits_dense(mesh_groups, listed, codewords, rows_here, feature):
    entries = mesh_groups * listed
    power = mesh_groups & (mesh_groups - 1) == 0 and mesh_groups >= 4
    digits = codewords % (2 * LOW) == 0 and (codewords // LOW) * listed <= LOW
    shapes = rows_here % (2 * LANES) == 0 and feature % (6 * LANES) == 0
    return power and digits and shapes and entries * codewords <= 2**20


def per_device(vectors, row_slot, fine_codes, cell_list, coarse_in, fine_in):
    groups = lax.axis_size("cell")
    dense = fits_dense(groups, cell_list.shape[1], *fine_in.shape[:1], *vectors.shape)
    plan = dense_plan if dense else routed_plan
    return plan(vectors, row_slot, fine_codes, cell_list, coarse_in, fine_in)


def solution(mesh):
    return jax.shard_map(
        per_device,
        mesh=mesh,
        in_specs=(
            P(("parts", "cell"), None),
            P(None, ("parts", "cell")),
            P(None, ("parts", "cell")),
            P(None, ("parts", "cell")),
            P("cell", None),
            P(),
        ),
        out_specs=(P(("parts", "cell"), None), P(("parts", "cell"), None)),
        check_vma=False,
    )
```

```python
import jax
import jax.numpy as jnp
from jax import lax
from jax.experimental import pallas as pl
from jax.experimental.pallas import tpu as pltpu
from jax.sharding import PartitionSpec as P


def code_tally(code_rows, codewords):
    return jax.ops.segment_sum(
        jnp.ones(code_rows.shape, jnp.float32), code_rows, num_segments=codewords
    )


def fine_update(code_term, totals_share, old_share, share_rows):
    part_sums = lax.psum_scatter(
        code_term(jnp.int32(0), lax.axis_size("cell") * share_rows),
        "cell",
        scatter_dimension=0,
        tiled=True,
    )
    return jnp.where(
        totals_share[:, None] > 0, part_sums / jnp.maximum(totals_share, 1.0)[:, None], old_share
    )


def routed_plan(vectors, row_slot, fine_codes, cell_list, coarse_in, fine_in):
    groups = lax.axis_size("cell")
    rows_here, feature = vectors.shape
    listed = cell_list.shape[1]
    slot_count = listed // groups
    owner_cells = coarse_in.shape[0]
    codewords = fine_in.shape[0]
    share_rows = codewords // groups
    share_start = lax.axis_index("cell") * share_rows
    fine_book = fine_in
    fine_share = lax.dynamic_slice_in_dim(fine_in, share_start, share_rows, 0)
    coarse = coarse_in
    list_iota = lax.iota(jnp.int32, listed)
    for sweep in range(2):
        code_totals = lax.psum(code_tally(fine_codes[sweep], codewords), "cell")
        slot_rows = row_slot[sweep]
        code_rows = fine_codes[sweep]
        picked = jnp.take(fine_book, code_rows, axis=0)
        residual = (vectors.astype(jnp.float32) - picked).astype(jnp.bfloat16)
        slot_hot = (slot_rows[None, :] == list_iota[:, None]).astype(jnp.bfloat16)
        slot_sums = jnp.dot(slot_hot, residual, preferred_element_type=jnp.float32)
        slot_counts = jnp.sum(slot_hot, axis=1, dtype=jnp.float32)
        slot_cells = cell_list[sweep].astype(jnp.float32)
        got_sums, got_counts, got_cells = (
            lax.all_to_all(
                slot_sums.reshape(groups, slot_count, feature),
                "cell",
                split_axis=0,
                concat_axis=0,
                tiled=True,
            ),
            lax.all_to_all(
                slot_counts.reshape(groups, slot_count),
                "cell",
                split_axis=0,
                concat_axis=0,
                tiled=True,
            ),
            lax.all_to_all(
                slot_cells.reshape(groups, slot_count),
                "cell",
                split_axis=0,
                concat_axis=0,
                tiled=True,
            ),
        )
        flat_cells = got_cells.reshape(groups * slot_count).astype(jnp.int32)
        cell_sums = jax.ops.segment_sum(
            got_sums.reshape(groups * slot_count, feature), flat_cells, num_segments=owner_cells
        )
        cell_counts = jax.ops.segment_sum(
            got_counts.reshape(groups * slot_count), flat_cells, num_segments=owner_cells
        )
        coarse = jnp.where(
            cell_counts[:, None] > 0, cell_sums / jnp.maximum(cell_counts, 1.0)[:, None], coarse
        )
        returned_rows = jnp.take(coarse, flat_cells, axis=0).reshape(groups, slot_count, feature)
        arrived = lax.all_to_all(returned_rows, "cell", split_axis=0, concat_axis=0, tiled=True)
        entry_centers = arrived.reshape(listed, feature)
        row_centers = jnp.take(entry_centers, slot_rows, axis=0)
        fine_residual = (vectors.astype(jnp.float32) - row_centers).astype(jnp.bfloat16)

        def code_term(start, count, code_rows=code_rows, fine_residual=fine_residual):
            wanted = start + lax.iota(jnp.int32, count)
            code_hot = (code_rows[None, :] == wanted[:, None]).astype(jnp.bfloat16)
            return jnp.dot(code_hot, fine_residual, preferred_element_type=jnp.float32)

        totals_share = lax.dynamic_slice_in_dim(code_totals, share_start, share_rows, 0)
        if sweep == 0:
            full_sums = lax.psum(code_term(0, codewords), "cell")
            fine_book = jnp.where(
                code_totals[:, None] > 0,
                full_sums / jnp.maximum(code_totals, 1.0)[:, None],
                fine_book,
            )
            fine_share = lax.dynamic_slice_in_dim(fine_book, share_start, share_rows, 0)
        else:
            fine_share = fine_update(code_term, totals_share, fine_share, share_rows)
    return (coarse, fine_share)


F32 = jnp.float32
BF16 = jnp.bfloat16
LOW = 256
LANES = 128
PARAMS = pltpu.CompilerParams(vmem_limit_bytes=58 * 2**20)
VMEM = pl.BlockSpec(memory_space=pltpu.VMEM)
SMEM = pl.BlockSpec(memory_space=pltpu.SMEM)
ANY = pl.BlockSpec(memory_space=pl.ANY)


def iota(shape, axis):
    return lax.broadcasted_iota(jnp.int32, shape, axis)


def matmul(left, right):
    return jnp.dot(left, right, preferred_element_type=F32)


def matmul_nt(left, right):
    return lax.dot_general(left, right, (((1,), (1,)), ((), ())), preferred_element_type=F32)


def split(values):
    high = values.astype(BF16)
    return high, (values - high.astype(F32)).astype(BF16)


def hot_rows(codes, rows=LOW):
    inside = jnp.where((codes >= 0) & (codes < rows), codes, -1)
    inside = inside.astype(F32).astype(BF16)
    row = iota((rows, codes.shape[1]), 0).astype(F32).astype(BF16)
    return jnp.where(row == inside, jnp.ones((), BF16), jnp.zeros((), BF16))


def pair_block(codes, slots, listed, high):
    left = hot_rows((codes >> 8) * listed + slots, high * listed)
    return matmul_nt(left, hot_rows(codes & (LOW - 1)))


def pack_kernel(fine_codes, row_slot, cell_list, packed):
    half = fine_codes.shape[1] // 2
    listed = cell_list.shape[1]
    packed[:, half:] = jnp.zeros((8, LANES), jnp.int32)
    for number, ref in enumerate((fine_codes, row_slot)):
        for sweep in range(2):
            for part in range(2):
                row = 4 * number + 2 * sweep + part
                packed[row : row + 1, :half] = ref[
                    sweep : sweep + 1, part * half : (part + 1) * half
                ]
    packed[0:2, half : half + listed] = cell_list[...]


def own_cells_kernel(
    groups, listed, me_ref, vectors, fine_codes, row_slot, fine_in, first_ref, second_ref, to_ref
):
    high = fine_in.shape[0] // LOW
    first = matmul(hot_rows(row_slot[0:1, :], listed), vectors[...])
    second_ref[...] = matmul(hot_rows(row_slot[1:2, :], listed), vectors[...])
    pairs = pair_block(fine_codes[0:1, :], row_slot[0:1, :], listed, high)
    for digit in range(high):
        pairs_high, pairs_low = split(pairs[digit * listed : (digit + 1) * listed])
        both = jnp.concatenate([pairs_high, pairs_low], axis=0)
        book = fine_in[digit * LOW : (digit + 1) * LOW, :]
        book_high, book_low = split(book)
        taken = matmul(both, book_high) + matmul(both, book_low)
        first = first - taken[:listed] - taken[listed:]
    first_ref[...] = first
    slots = listed // groups
    top = groups.bit_length() - 1
    for owner in range(groups):
        block = owner ^ me_ref[0]
        at = sum((1 - (block >> bit & 1)) << (top - 1 - bit) for bit in range(2))
        at = at + groups // 4 - 1 - (block >> 2)
        to_ref[at, 0] = first[owner * slots : (owner + 1) * slots]


def own_codes_kernel(base, vectors, fine_codes, _, sums_ref):
    codes = fine_codes[0:1, :] - base
    for start in range(0, sums_ref.shape[0], 2 * LOW):
        hot = jnp.concatenate(
            [hot_rows(codes - start), hot_rows(codes - start - LOW)], axis=0
        )
        sums_ref[start : start + 2 * LOW, :] = matmul(hot, vectors[...])


def position(block, groups):
    return (block & 1) * (groups // 2) + (block >> 1 & 1) * (groups // 4) + (block >> 2)


def sums_kernel(
    groups,
    slot_count,
    owner_cells,
    cuts,
    orders,
    me_ref,
    codes_ref,
    vectors,
    fine_codes,
    low_sums_ref,
    high_sums_ref,
    first_ref,
    second_ref,
    share_ref,
    _,
    *refs,
):
    out_refs, refs = refs[: 3 * len(cuts)], refs[3 * len(cuts) :]
    code_info_ref, entry_info_ref, refs = refs[0], refs[1], refs[2:]
    table0, table1, cell0, cell1, wide, terms, permuted, rows_hot = refs[:8]
    fine, bracket, centers_ref, pairs_ref, left = refs[8:13]
    in_sem, out_sem, stages = refs[13], refs[14], refs[15:]
    me = me_ref[0]
    codewords, feature = fine.shape
    listed = groups * slot_count
    entries = groups * listed
    high = codewords // LOW
    half = codes_ref.shape[2] - LANES
    share_rows = share_ref.shape[0]

    loads = [
        pltpu.make_async_copy(
            ref, fine.at[pl.ds(at * (codewords // 2), codewords // 2)], in_sem.at[at]
        )
        for at, ref in enumerate((low_sums_ref, high_sums_ref))
    ]
    for load in loads:
        load.start()

    rows_hot[...] = iota(rows_hot.shape, 0).astype(F32).astype(BF16)
    one, zero = jnp.ones((), BF16), jnp.zeros((), BF16)

    def hot(codes):
        rows = rows_hot[:, : codes.shape[1]]
        return jnp.where(rows == codes.astype(F32).astype(BF16), one, zero)

    def device_tables(device, carry):
        at = position(device ^ me, groups)
        for sweep, table in enumerate((table0, table1)):
            block = jnp.zeros((high * listed, LOW), F32)
            for part in range(2):
                row = 2 * sweep + part
                codes = codes_ref[at, row : row + 1, :half]
                slots = codes_ref[at, row + 4 : row + 5, :half]
                block = block + matmul_nt(
                    hot((codes >> 8) * listed + slots)[: high * listed], hot(codes & (LOW - 1))
                )
            rows = pl.ds(pl.multiple_of(device * listed, listed), listed)
            for digit in range(high):
                table[rows, digit * LOW : (digit + 1) * LOW] = block[
                    digit * listed : (digit + 1) * listed
                ]
        return carry

    lax.fori_loop(0, groups, device_tables, 0)
    for device in range(groups):
        at = position(device ^ me, groups)
        for sweep, cell in enumerate((cell0, cell1)):
            row = codes_ref[at, sweep : sweep + 1, half : half + listed]
            cell[device * slot_count : (device + 1) * slot_count, :] = jnp.broadcast_to(
                row, (slot_count, listed)
            )

    row_at = iota((entries, listed), 0)
    owner_of = row_at // listed
    slot_of = owner_of * slot_count + row_at % slot_count
    is_slot = slot_of == iota((entries, listed), 1)
    device_of = (row_at // slot_count) % groups

    def entry_cells(cell):
        tiled = jnp.concatenate([cell[...]] * groups, axis=0)
        picked = jnp.sum(jnp.where(is_slot, tiled, 0), axis=1, keepdims=True)
        return picked.astype(F32)

    owner_col = owner_of[:, :1].astype(F32)
    cells = [entry_cells(cell0), entry_cells(cell1)]
    names = [cell + owner_col * float(owner_cells) for cell in cells]

    entry_row = iota((entries, entries), 0)
    natural = (
        ((entry_row // slot_count) % groups) * listed
        + (entry_row // listed) * slot_count
        + entry_row % slot_count
    )
    order = (natural == iota((entries, entries), 1)).astype(BF16)
    code_counts = [jnp.sum(table[...], axis=0, keepdims=True) for table in (table0, table1)]
    entry_counts, most = [], 0.0
    for sweep, table in enumerate((table0, table1)):
        entry_count = jnp.sum(table[...], axis=1, keepdims=True)
        most = jnp.maximum(
            most, jnp.minimum(jnp.max(entry_count), jnp.max(code_counts[sweep]))
        )
        count_high, count_low = split(jnp.broadcast_to(entry_count, (entries, LANES)))
        entry_counts.append(matmul(order, count_high) + matmul(order, count_low))
    large = most > LOW
    for digit in range(high):
        columns = slice(digit * LOW, (digit + 1) * LOW)
        permuted[0, :, columns] = matmul(order, table1[:, columns].astype(BF16)).astype(BF16)

    @pl.when(large)
    def _():
        for digit in range(high):
            columns = slice(digit * LOW, (digit + 1) * LOW)
            rest = split(table1[:, columns])[1]
            permuted[1, :, columns] = matmul(order, rest).astype(BF16)

    own_row = codes_ref[0, 0:1, half : half + listed].astype(F32)
    own_row = own_row + (iota((1, listed), 1) // slot_count).astype(F32) * float(owner_cells)
    match = (names[0] == own_row).astype(BF16)
    match = lax.dot_general(match, order, (((0,), (0,)), ((), ())), preferred_element_type=F32)
    match = match.astype(BF16)
    for digit in range(high):
        columns = slice(digit * LOW, (digit + 1) * LOW)
        wide[0:listed, columns] = matmul(match, table0[:, columns].astype(BF16))

    @pl.when(large)
    def _():
        for digit in range(high):
            columns = slice(digit * LOW, (digit + 1) * LOW)
            wide[0:listed, columns] += matmul(match, split(table0[:, columns])[1])

    held = jnp.sum(wide[0:listed, :], axis=1, keepdims=True)
    used_high, used_low = split(wide[0:listed, :])
    wide[0:listed, :] = used_high.astype(F32)
    wide[listed : 2 * listed, :] = used_low.astype(F32)
    wide[2 * listed : 2 * listed + 8, :] = jnp.broadcast_to(code_counts[0], (8, codewords))
    wide[2 * listed + 8 : 2 * listed + 16, :] = jnp.broadcast_to(code_counts[1], (8, codewords))
    wide[2 * listed + 16 :, :] = jnp.zeros((LANES - 2 * listed - 16, codewords), F32)
    center_high, center_low = split(first_ref[...] / jnp.maximum(held, 1.0))
    blank = jnp.zeros((LANES - 2 * listed, feature), BF16)
    center_high = jnp.concatenate([center_high, center_high, blank], axis=0)
    center_low = jnp.concatenate([center_low, center_low, blank], axis=0)
    for load in loads:
        load.wait()
    for digit in range(high):
        rows = slice(digit * LOW, (digit + 1) * LOW)
        columns = wide[:, rows].T
        code_info_ref[rows, :] = columns
        taken = jnp.where(iota((LOW, LANES), 1) < 2 * listed, columns, 0.0).astype(BF16)
        first_fine = fine[rows, :] - (matmul(taken, center_high) + matmul(taken, center_low))
        scaled = first_fine * (1.0 / jnp.maximum(columns[:, 2 * listed : 2 * listed + 1], 1.0))
        terms[0, rows, :], terms[1, rows, :] = split(scaled)
        fine[rows, :] = jnp.where(
            columns[:, 2 * listed + 8 : 2 * listed + 9] > 0, 0.0, first_fine
        )
    mine = pl.ds(pl.multiple_of(me * share_rows, share_rows), share_rows)
    empty = code_info_ref[mine, 2 * listed : 2 * listed + 1] == 0
    for part, share in enumerate(split(share_ref[...])):
        terms[part, mine, :] = jnp.where(
            empty, share.astype(F32), terms[part, mine, :].astype(F32)
        ).astype(BF16)

    own_entry = (is_slot & (device_of == me)).astype(BF16)
    second_high, second_low = split(second_ref[...])
    bracket[...] = (
        matmul(own_entry, second_high)
        + matmul(own_entry, second_low)
        - matmul(permuted[0], terms[0])
        - matmul(permuted[0], terms[1])
    )

    @pl.when(large)
    def _():
        bracket[...] -= matmul(permuted[1], terms[0])

    same = (
        jnp.broadcast_to(names[1], (entries, entries))
        == jnp.broadcast_to(names[1], (entries, LANES)).T[0:1, :]
    ).astype(BF16)
    total_high, total_low = split(entry_counts[1])
    totals = matmul(same, total_high) + matmul(same, total_low)
    bracket_high, bracket_low = split(bracket[...])
    centers = matmul(same, bracket_high) + matmul(same, bracket_low)
    centers = centers * (1.0 / jnp.maximum(totals[:, :1], 1.0))
    centers_ref[0], centers_ref[1] = split(centers)
    lane = iota((entries, LANES), 1)
    info = jnp.where(lane == 0, entry_counts[0], entry_counts[1])
    info = jnp.where(lane == 2, cells[0], info)
    entry_info_ref[...] = jnp.where(lane == 3, cells[1], info)

    eye = (iota((LOW, LOW), 0) == iota((LOW, LOW), 1)).astype(BF16)
    for digit in range(high):
        rows = slice(digit * LOW, (digit + 1) * LOW)
        pairs_ref[rows, :] = -matmul_nt(eye, permuted[0, :, rows]).astype(BF16)
    rows_here = vectors.shape[0]
    codes = fine_codes[1:2, :]
    copies = []
    for odd in (1, 0):
        blocks = [at for at in range(groups) if at % 2 == odd]
        for at, block in enumerate(blocks):
            owner = me ^ block
            rows = pl.ds(pl.multiple_of(owner * share_rows, share_rows), share_rows)
            to = slice(at * share_rows, (at + 1) * share_rows)
            own = codes - owner * share_rows
            own = jnp.where((own >= 0) & (own < share_rows), own, -1)
            left[to, :rows_here] = hot(own)[:share_rows]
            left[to, rows_here:] = pairs_ref[rows, :]
        start = 0
        for chunk, cut in enumerate(cuts):
            columns = slice(start, start + cut)
            start += cut
            sums = (
                matmul(left[:, :rows_here], vectors[:, columns])
                + matmul(left[:, rows_here:], centers_ref[0, :, columns])
                + matmul(left[:, rows_here:], centers_ref[1, :, columns])
            )
            for part, order_of in enumerate(orders[chunk]):
                if order_of[0] % 2 != odd:
                    continue
                number = 3 * chunk + part
                stage = stages[number]
                for to, block in enumerate(order_of):
                    owner = me ^ block
                    rows = pl.ds(pl.multiple_of(owner * share_rows, share_rows), share_rows)
                    cell_rows = pl.ds(pl.multiple_of(owner * listed, listed), listed)
                    at = blocks.index(block) * share_rows
                    stage[to, :share_rows, :] = sums[at : at + share_rows] + fine[rows, columns]
                    stage[to, share_rows:, :] = bracket[cell_rows, columns]

                @pl.when(large)
                def _():
                    for to, block in enumerate(order_of):
                        owner = me ^ block
                        rows = pl.ds(pl.multiple_of(owner * share_rows, share_rows), share_rows)
                        rest = lax.dot_general(
                            permuted[1, :, rows],
                            centers_ref[0, :, columns],
                            (((0,), (0,)), ((), ())),
                            preferred_element_type=F32,
                        )
                        stage[to, :share_rows, :] -= rest

                copy = pltpu.make_async_copy(stage, out_refs[number], out_sem.at[number])
                copy.start()
                copies.append(copy)
    for copy in copies:
        copy.wait()


def final_kernel(
    groups, slot_count, share_rows, cuts, me_ref, coarse_in, fine_share, first_sums, *refs
):
    last_refs, (code_info, entry_info, coarse_out, fine_out, own_first) = refs[:-5], refs[-5:]
    listed = entry_info.shape[0]
    owner_cells = coarse_in.shape[0]
    by_lane = entry_info[...].T
    for device in range(groups):
        rows = slice(device * slot_count, (device + 1) * slot_count)
        own_first[rows, :] = first_sums[device ^ me_ref[0]]
    hits, counts = [], []
    for sweep in range(2):
        cell = by_lane[2 + sweep : 3 + sweep, :].astype(jnp.int32)
        hit = iota((owner_cells, listed), 0) == cell
        counts.append(
            jnp.sum(jnp.where(hit, by_lane[sweep : sweep + 1, :], 0.0), axis=1, keepdims=True)
        )
        hits.append(hit.astype(BF16))
    first_count = code_info[:, 2 * listed : 2 * listed + 1]
    last_count = code_info[:, 2 * listed + 8 : 2 * listed + 9]
    count = jnp.where(last_count > 0, last_count, first_count)
    start = 0
    for cut, last_sums in zip(cuts, last_refs):
        columns = slice(start, start + cut)
        start += cut
        coarse = coarse_in[:, columns]
        for sweep, sums in enumerate((own_first[:, columns], last_sums[share_rows:, :])):
            sums_high, sums_low = split(sums)
            found = matmul(hits[sweep], sums_high) + matmul(hits[sweep], sums_low)
            weight = 1.0 / jnp.maximum(counts[sweep], 1.0)
            coarse = jnp.where(counts[sweep] > 0, found * weight, coarse)
        coarse_out[:, columns] = coarse
        fine_out[:, columns] = jnp.where(
            count > 0,
            last_sums[:share_rows, :] * (1.0 / jnp.maximum(count, 1.0)),
            fine_share[:, columns],
        )


def exchange(values, step):
    groups = lax.axis_size("cell")
    return lax.ppermute(values, "cell", [(at, at ^ step) for at in range(groups)])


def block_order(bits):
    order = [0]
    for bit in list(bits)[::-1]:
        order = [block + (1 << bit) for block in order] + order
    return order


def block_orders(bits):
    order = block_order(bits)
    half = len(order) // 2
    return [block + 1 for block in order], order[:half], order[half:]


def after(values, *others):
    return lax.optimization_barrier((values, *others))[0]


def halved(got, other, kept):
    half = other.shape[0]
    return other + got[:half], kept + got[half:]


def swap(blocks, bit):
    half = blocks.shape[0] // 2
    got = exchange(blocks[:half], 1 << bit)
    return jnp.concatenate([blocks[half:], got], axis=1)


def local(kernel, shapes, in_specs, out_specs, scratch, flops, name, aliases=None):
    return pl.pallas_call(
        kernel,
        out_shape=tuple(jax.ShapeDtypeStruct(shape, dtype) for shape, dtype in shapes),
        grid_spec=pltpu.PrefetchScalarGridSpec(
            num_scalar_prefetch=1,
            grid=(1,),
            in_specs=in_specs,
            out_specs=out_specs,
            scratch_shapes=scratch,
        ),
        input_output_aliases=aliases or {},
        compiler_params=PARAMS,
        cost_estimate=pl.CostEstimate(
            flops=int(flops), bytes_accessed=10**6, transcendentals=0
        ),
        name=name,
    )


def block(shape, *place):
    return pl.BlockSpec(
        shape, lambda step, me: tuple(me[0] if at is None else at for at in place)
    )


def dense_plan(vectors, row_slot, fine_codes, cell_list, coarse_in, fine_in):
    groups = lax.axis_size("cell")
    rows_here, feature = vectors.shape
    listed = cell_list.shape[1]
    slot_count = listed // groups
    owner_cells = coarse_in.shape[0]
    codewords = fine_in.shape[0]
    share_rows = codewords // groups
    entries = groups * listed
    half = rows_here // 2
    me = lax.axis_index("cell").reshape(1).astype(jnp.int32)

    packed = local(
        lambda me_ref, *refs: pack_kernel(*refs),
        [((8, half + LANES), jnp.int32)],
        [VMEM] * 3,
        [VMEM],
        [],
        1e9,
        "pack",
    )(me, fine_codes, row_slot, cell_list)[0]
    first, second, first_to = local(
        lambda *refs: own_cells_kernel(groups, listed, *refs),
        [((listed, feature), F32)] * 2 + [((groups, 1, slot_count, feature), F32)],
        [VMEM] * 4,
        [VMEM] * 3,
        [],
        5e9,
        "own_cells",
    )(me, vectors, fine_codes, row_slot, fine_in)
    far = groups // 4
    gathered = jnp.stack([packed] + [exchange(packed, 4 * step) for step in range(1, far)])
    sums = []
    for step, base in ((2, 0), (1, codewords // 2)):
        sums += local(
            lambda me_ref, *refs, base=base: own_codes_kernel(base, *refs),
            [((codewords // 2, feature), F32)],
            [VMEM, VMEM, ANY],
            [VMEM],
            [],
            6e9,
            "own_codes",
        )(me, vectors, fine_codes, gathered)
        if step == 2:
            first_to = swap(after(first_to, gathered), 0)
        gathered = jnp.concatenate([gathered, exchange(gathered, step)])

    top = groups.bit_length() - 1
    near_first = list(range(1, top))
    far_first = near_first[1:] + near_first[:1]
    cuts = [feature // 3] * 3
    bits = [near_first, far_first, near_first]
    orders = [block_orders(each) for each in bits]
    shapes = [
        (len(order), share_rows + listed, cut)
        for cut, three in zip(cuts, orders)
        for order in three
    ]
    *terms, code_info, entry_info = local(
        lambda *refs: sums_kernel(groups, slot_count, owner_cells, cuts, orders, *refs),
        [(shape, F32) for shape in shapes]
        + [((codewords, LANES), F32), ((entries, LANES), F32)],
        [VMEM] * 3 + [ANY] * 2 + [VMEM] * 2 + [block((share_rows, feature), None, 0), ANY],
        [ANY] * len(shapes) + [VMEM] * 2,
        [
            pltpu.VMEM((entries, codewords), F32),
            pltpu.VMEM((entries, codewords), F32),
            pltpu.VMEM((listed, listed), jnp.int32),
            pltpu.VMEM((listed, listed), jnp.int32),
            pltpu.VMEM((LANES, codewords), F32),
            pltpu.VMEM((2, codewords, feature), BF16),
            pltpu.VMEM((2, entries, codewords), BF16),
            pltpu.VMEM((LOW, rows_here), BF16),
            pltpu.VMEM((codewords, feature), F32),
            pltpu.VMEM((entries, feature), F32),
            pltpu.VMEM((2, entries, feature), BF16),
            pltpu.VMEM((codewords, entries), BF16),
            pltpu.VMEM((codewords // 2, rows_here + entries), BF16),
            pltpu.SemaphoreType.DMA((2,)),
            pltpu.SemaphoreType.DMA((len(shapes),)),
        ]
        + [pltpu.VMEM(shape, F32) for shape in shapes],
        40e9,
        "sums",
    )(me, gathered, vectors, fine_codes, *sums, first, second, fine_in, first_to)

    first_to = swap(after(first_to, terms[0]), 1)
    finished = []
    for at, steps in enumerate(bits):
        away, other, kept = terms[3 * at : 3 * at + 3]
        other, kept = halved(exchange(away, 1), other, kept)
        if at == len(bits) - 1:
            first_to = after(first_to, other)[::-1]
            first_to = jnp.concatenate(
                [first_to[0]] + [exchange(first_to[z], 4 * z) for z in range(1, far)]
            )
        for bit in steps[:-1]:
            got = exchange(other, 1 << bit)
            half = got.shape[0] // 2
            other, kept = halved(got, kept[:half], kept[half:])
        finished.append((kept + exchange(other, 1 << steps[-1]))[0])
    return local(
        lambda *refs: final_kernel(groups, slot_count, share_rows, cuts, *refs),
        [(coarse_in.shape, F32), ((share_rows, feature), F32)],
        [VMEM, block((share_rows, feature), None, 0)]
        + [VMEM] * (1 + len(cuts))
        + [block((share_rows, LANES), None, 0), block((listed, LANES), None, 0)],
        [VMEM] * 2,
        [pltpu.VMEM((listed, feature), F32)],
        1e9,
        "outputs",
    )(me, coarse_in, fine_in, first_to, *finished, code_info, entry_info)


def fits_dense(mesh_groups, listed, codewords, rows_here, feature):
    entries = mesh_groups * listed
    power = mesh_groups & (mesh_groups - 1) == 0 and mesh_groups >= 4
    digits = codewords % (2 * LOW) == 0 and (codewords // LOW) * listed <= LOW
    shapes = rows_here % (2 * LANES) == 0 and feature % (6 * LANES) == 0
    return power and digits and shapes and entries * codewords <= 2**20


def per_device(vectors, row_slot, fine_codes, cell_list, coarse_in, fine_in):
    groups = lax.axis_size("cell")
    dense = fits_dense(groups, cell_list.shape[1], *fine_in.shape[:1], *vectors.shape)
    plan = dense_plan if dense else routed_plan
    return plan(vectors, row_slot, fine_codes, cell_list, coarse_in, fine_in)


def solution(mesh):
    return jax.shard_map(
        per_device,
        mesh=mesh,
        in_specs=(
            P(("parts", "cell"), None),
            P(None, ("parts", "cell")),
            P(None, ("parts", "cell")),
            P(None, ("parts", "cell")),
            P("cell", None),
            P(),
        ),
        out_specs=(P(("parts", "cell"), None), P(("parts", "cell"), None)),
        check_vma=False,
    )
```

```python
import jax
import jax.numpy as jnp
from jax import lax
from jax.experimental import pallas as pl
from jax.experimental.pallas import tpu as pltpu
from jax.sharding import PartitionSpec as P


def code_tally(code_rows, codewords):
    return jax.ops.segment_sum(
        jnp.ones(code_rows.shape, jnp.float32), code_rows, num_segments=codewords
    )


def fine_update(code_term, totals_share, old_share, share_rows):
    part_sums = lax.psum_scatter(
        code_term(jnp.int32(0), lax.axis_size("cell") * share_rows),
        "cell",
        scatter_dimension=0,
        tiled=True,
    )
    return jnp.where(
        totals_share[:, None] > 0, part_sums / jnp.maximum(totals_share, 1.0)[:, None], old_share
    )


def routed_plan(vectors, row_slot, fine_codes, cell_list, coarse_in, fine_in):
    groups = lax.axis_size("cell")
    rows_here, feature = vectors.shape
    listed = cell_list.shape[1]
    slot_count = listed // groups
    owner_cells = coarse_in.shape[0]
    codewords = fine_in.shape[0]
    share_rows = codewords // groups
    share_start = lax.axis_index("cell") * share_rows
    fine_book = fine_in
    fine_share = lax.dynamic_slice_in_dim(fine_in, share_start, share_rows, 0)
    coarse = coarse_in
    list_iota = lax.iota(jnp.int32, listed)
    for sweep in range(2):
        code_totals = lax.psum(code_tally(fine_codes[sweep], codewords), "cell")
        slot_rows = row_slot[sweep]
        code_rows = fine_codes[sweep]
        picked = jnp.take(fine_book, code_rows, axis=0)
        residual = (vectors.astype(jnp.float32) - picked).astype(jnp.bfloat16)
        slot_hot = (slot_rows[None, :] == list_iota[:, None]).astype(jnp.bfloat16)
        slot_sums = jnp.dot(slot_hot, residual, preferred_element_type=jnp.float32)
        slot_counts = jnp.sum(slot_hot, axis=1, dtype=jnp.float32)
        slot_cells = cell_list[sweep].astype(jnp.float32)
        got_sums, got_counts, got_cells = (
            lax.all_to_all(
                slot_sums.reshape(groups, slot_count, feature),
                "cell",
                split_axis=0,
                concat_axis=0,
                tiled=True,
            ),
            lax.all_to_all(
                slot_counts.reshape(groups, slot_count),
                "cell",
                split_axis=0,
                concat_axis=0,
                tiled=True,
            ),
            lax.all_to_all(
                slot_cells.reshape(groups, slot_count),
                "cell",
                split_axis=0,
                concat_axis=0,
                tiled=True,
            ),
        )
        flat_cells = got_cells.reshape(groups * slot_count).astype(jnp.int32)
        cell_sums = jax.ops.segment_sum(
            got_sums.reshape(groups * slot_count, feature), flat_cells, num_segments=owner_cells
        )
        cell_counts = jax.ops.segment_sum(
            got_counts.reshape(groups * slot_count), flat_cells, num_segments=owner_cells
        )
        coarse = jnp.where(
            cell_counts[:, None] > 0, cell_sums / jnp.maximum(cell_counts, 1.0)[:, None], coarse
        )
        returned_rows = jnp.take(coarse, flat_cells, axis=0).reshape(groups, slot_count, feature)
        arrived = lax.all_to_all(returned_rows, "cell", split_axis=0, concat_axis=0, tiled=True)
        entry_centers = arrived.reshape(listed, feature)
        row_centers = jnp.take(entry_centers, slot_rows, axis=0)
        fine_residual = (vectors.astype(jnp.float32) - row_centers).astype(jnp.bfloat16)

        def code_term(start, count, code_rows=code_rows, fine_residual=fine_residual):
            wanted = start + lax.iota(jnp.int32, count)
            code_hot = (code_rows[None, :] == wanted[:, None]).astype(jnp.bfloat16)
            return jnp.dot(code_hot, fine_residual, preferred_element_type=jnp.float32)

        totals_share = lax.dynamic_slice_in_dim(code_totals, share_start, share_rows, 0)
        if sweep == 0:
            full_sums = lax.psum(code_term(0, codewords), "cell")
            fine_book = jnp.where(
                code_totals[:, None] > 0,
                full_sums / jnp.maximum(code_totals, 1.0)[:, None],
                fine_book,
            )
            fine_share = lax.dynamic_slice_in_dim(fine_book, share_start, share_rows, 0)
        else:
            fine_share = fine_update(code_term, totals_share, fine_share, share_rows)
    return (coarse, fine_share)


F32 = jnp.float32
BF16 = jnp.bfloat16
LOW = 256
LANES = 128
PARAMS = pltpu.CompilerParams(vmem_limit_bytes=58 * 2**20)
VMEM = pl.BlockSpec(memory_space=pltpu.VMEM)
SMEM = pl.BlockSpec(memory_space=pltpu.SMEM)
ANY = pl.BlockSpec(memory_space=pl.ANY)


def iota(shape, axis):
    return lax.broadcasted_iota(jnp.int32, shape, axis)


def matmul(left, right):
    return jnp.dot(left, right, preferred_element_type=F32)


def matmul_nt(left, right):
    return lax.dot_general(left, right, (((1,), (1,)), ((), ())), preferred_element_type=F32)


def split(values):
    high = values.astype(BF16)
    return high, (values - high.astype(F32)).astype(BF16)


def hot_rows(codes, rows=LOW):
    inside = jnp.where((codes >= 0) & (codes < rows), codes, -1)
    inside = inside.astype(F32).astype(BF16)
    row = iota((rows, codes.shape[1]), 0).astype(F32).astype(BF16)
    return jnp.where(row == inside, jnp.ones((), BF16), jnp.zeros((), BF16))


def pair_block(codes, slots, listed, high):
    left = hot_rows((codes >> 8) * listed + slots, high * listed)
    return matmul_nt(left, hot_rows(codes & (LOW - 1)))


def pack_kernel(fine_codes, row_slot, cell_list, packed):
    half = fine_codes.shape[1] // 2
    listed = cell_list.shape[1]
    packed[:, half:] = jnp.zeros((8, LANES), jnp.int32)
    for number, ref in enumerate((fine_codes, row_slot)):
        for sweep in range(2):
            for part in range(2):
                row = 4 * number + 2 * sweep + part
                packed[row : row + 1, :half] = ref[
                    sweep : sweep + 1, part * half : (part + 1) * half
                ]
    packed[0:2, half : half + listed] = cell_list[...]


def own_cells_kernel(
    groups, listed, me_ref, vectors, fine_codes, row_slot, fine_in, first_ref, second_ref, to_ref
):
    high = fine_in.shape[0] // LOW
    first = matmul(hot_rows(row_slot[0:1, :], listed), vectors[...])
    second_ref[...] = matmul(hot_rows(row_slot[1:2, :], listed), vectors[...])
    pairs = pair_block(fine_codes[0:1, :], row_slot[0:1, :], listed, high)
    for digit in range(high):
        pairs_high, pairs_low = split(pairs[digit * listed : (digit + 1) * listed])
        both = jnp.concatenate([pairs_high, pairs_low], axis=0)
        book = fine_in[digit * LOW : (digit + 1) * LOW, :]
        book_high, book_low = split(book)
        taken = matmul(both, book_high) + matmul(both, book_low)
        first = first - taken[:listed] - taken[listed:]
    first_ref[...] = first
    slots = listed // groups
    top = groups.bit_length() - 1
    for owner in range(groups):
        block = owner ^ me_ref[0]
        at = sum((1 - (block >> bit & 1)) << (top - 1 - bit) for bit in range(2))
        at = at + groups // 4 - 1 - (block >> 2)
        to_ref[at, 0] = first[owner * slots : (owner + 1) * slots]


def own_codes_kernel(base, vectors, fine_codes, _, sums_ref):
    codes = fine_codes[0:1, :] - base
    for start in range(0, sums_ref.shape[0], 2 * LOW):
        hot = jnp.concatenate(
            [hot_rows(codes - start), hot_rows(codes - start - LOW)], axis=0
        )
        sums_ref[start : start + 2 * LOW, :] = matmul(hot, vectors[...])


def position(block, groups):
    return (block & 1) * (groups // 2) + (block >> 1 & 1) * (groups // 4) + (block >> 2)


def sums_kernel(
    groups,
    slot_count,
    owner_cells,
    cuts,
    starts,
    orders,
    me_ref,
    codes_ref,
    vectors_ref,
    fine_codes,
    low_sums_ref,
    high_sums_ref,
    first_ref,
    second_ref,
    share_ref,
    _,
    *refs,
):
    out_refs, refs = refs[: 3 * len(cuts)], refs[3 * len(cuts) :]
    code_info_ref, entry_info_ref, refs = refs[0], refs[1], refs[2:]
    table0, table1, cell0, cell1, wide, terms, permuted, rows_hot = refs[:8]
    fine, bracket, centers_ref, pairs_ref, left = refs[8:13]
    in_sem, out_sem, vectors, stages = refs[13], refs[14], refs[15], refs[16:]
    me = me_ref[0]
    codewords, feature = fine.shape
    listed = groups * slot_count
    entries = groups * listed
    high = codewords // LOW
    half = codes_ref.shape[2] - LANES
    share_rows = share_ref.shape[0]

    loads = [
        pltpu.make_async_copy(
            ref, fine.at[pl.ds(at * (codewords // 2), codewords // 2)], in_sem.at[at]
        )
        for at, ref in enumerate((low_sums_ref, high_sums_ref))
    ]
    loads.append(pltpu.make_async_copy(vectors_ref, vectors, in_sem.at[2]))
    for load in loads:
        load.start()

    rows_hot[...] = iota(rows_hot.shape, 0).astype(F32).astype(BF16)
    one, zero = jnp.ones((), BF16), jnp.zeros((), BF16)

    def hot(codes):
        rows = rows_hot[:, : codes.shape[1]]
        return jnp.where(rows == codes.astype(F32).astype(BF16), one, zero)

    def device_tables(device, carry):
        at = position(device ^ me, groups)
        for sweep, table in enumerate((table0, table1)):
            block = jnp.zeros((high * listed, LOW), F32)
            for part in range(2):
                row = 2 * sweep + part
                codes = codes_ref[at, row : row + 1, :half]
                slots = codes_ref[at, row + 4 : row + 5, :half]
                block = block + matmul_nt(
                    hot((codes >> 8) * listed + slots)[: high * listed], hot(codes & (LOW - 1))
                )
            rows = pl.ds(pl.multiple_of(device * listed, listed), listed)
            for digit in range(high):
                table[rows, digit * LOW : (digit + 1) * LOW] = block[
                    digit * listed : (digit + 1) * listed
                ]
        return carry

    lax.fori_loop(0, groups, device_tables, 0)
    for device in range(groups):
        at = position(device ^ me, groups)
        for sweep, cell in enumerate((cell0, cell1)):
            row = codes_ref[at, sweep : sweep + 1, half : half + listed]
            cell[device * slot_count : (device + 1) * slot_count, :] = jnp.broadcast_to(
                row, (slot_count, listed)
            )

    row_at = iota((entries, listed), 0)
    owner_of = row_at // listed
    slot_of = owner_of * slot_count + row_at % slot_count
    is_slot = slot_of == iota((entries, listed), 1)
    device_of = (row_at // slot_count) % groups

    def entry_cells(cell):
        tiled = jnp.concatenate([cell[...]] * groups, axis=0)
        picked = jnp.sum(jnp.where(is_slot, tiled, 0), axis=1, keepdims=True)
        return picked.astype(F32)

    owner_col = owner_of[:, :1].astype(F32)
    cells = [entry_cells(cell0), entry_cells(cell1)]
    names = [cell + owner_col * float(owner_cells) for cell in cells]

    entry_row = iota((entries, entries), 0)
    natural = (
        ((entry_row // slot_count) % groups) * listed
        + (entry_row // listed) * slot_count
        + entry_row % slot_count
    )
    order = (natural == iota((entries, entries), 1)).astype(BF16)
    code_counts = [jnp.sum(table[...], axis=0, keepdims=True) for table in (table0, table1)]
    entry_counts, most = [], 0.0
    for sweep, table in enumerate((table0, table1)):
        entry_count = jnp.sum(table[...], axis=1, keepdims=True)
        most = jnp.maximum(
            most, jnp.minimum(jnp.max(entry_count), jnp.max(code_counts[sweep]))
        )
        count_high, count_low = split(jnp.broadcast_to(entry_count, (entries, LANES)))
        entry_counts.append(matmul(order, count_high) + matmul(order, count_low))
    large = most > LOW
    for digit in range(high):
        columns = slice(digit * LOW, (digit + 1) * LOW)
        permuted[0, :, columns] = matmul(order, table1[:, columns].astype(BF16)).astype(BF16)

    @pl.when(large)
    def _():
        for digit in range(high):
            columns = slice(digit * LOW, (digit + 1) * LOW)
            rest = split(table1[:, columns])[1]
            permuted[1, :, columns] = matmul(order, rest).astype(BF16)

    own_row = codes_ref[0, 0:1, half : half + listed].astype(F32)
    own_row = own_row + (iota((1, listed), 1) // slot_count).astype(F32) * float(owner_cells)
    match = (names[0] == own_row).astype(BF16)
    match = lax.dot_general(match, order, (((0,), (0,)), ((), ())), preferred_element_type=F32)
    match = match.astype(BF16)
    for digit in range(high):
        columns = slice(digit * LOW, (digit + 1) * LOW)
        wide[0:listed, columns] = matmul(match, table0[:, columns].astype(BF16))

    @pl.when(large)
    def _():
        for digit in range(high):
            columns = slice(digit * LOW, (digit + 1) * LOW)
            wide[0:listed, columns] += matmul(match, split(table0[:, columns])[1])

    held = jnp.sum(wide[0:listed, :], axis=1, keepdims=True)
    used_high, used_low = split(wide[0:listed, :])
    wide[0:listed, :] = used_high.astype(F32)
    wide[listed : 2 * listed, :] = used_low.astype(F32)
    wide[2 * listed : 2 * listed + 8, :] = jnp.broadcast_to(code_counts[0], (8, codewords))
    wide[2 * listed + 8 : 2 * listed + 16, :] = jnp.broadcast_to(code_counts[1], (8, codewords))
    wide[2 * listed + 16 :, :] = jnp.zeros((LANES - 2 * listed - 16, codewords), F32)
    center_high, center_low = split(first_ref[...] / jnp.maximum(held, 1.0))
    blank = jnp.zeros((LANES - 2 * listed, feature), BF16)
    center_high = jnp.concatenate([center_high, center_high, blank], axis=0)
    center_low = jnp.concatenate([center_low, center_low, blank], axis=0)
    for load in loads:
        load.wait()
    for digit in range(high):
        rows = slice(digit * LOW, (digit + 1) * LOW)
        columns = wide[:, rows].T
        code_info_ref[rows, :] = columns
        taken = jnp.where(iota((LOW, LANES), 1) < 2 * listed, columns, 0.0).astype(BF16)
        first_fine = fine[rows, :] - (matmul(taken, center_high) + matmul(taken, center_low))
        scaled = first_fine * (1.0 / jnp.maximum(columns[:, 2 * listed : 2 * listed + 1], 1.0))
        terms[0, rows, :], terms[1, rows, :] = split(scaled)
        fine[rows, :] = jnp.where(
            columns[:, 2 * listed + 8 : 2 * listed + 9] > 0, 0.0, first_fine
        )
    mine = pl.ds(pl.multiple_of(me * share_rows, share_rows), share_rows)
    empty = code_info_ref[mine, 2 * listed : 2 * listed + 1] == 0
    for part, share in enumerate(split(share_ref[...])):
        terms[part, mine, :] = jnp.where(
            empty, share.astype(F32), terms[part, mine, :].astype(F32)
        ).astype(BF16)

    own_entry = (is_slot & (device_of == me)).astype(BF16)
    second_high, second_low = split(second_ref[...])
    bracket[...] = (
        matmul(own_entry, second_high)
        + matmul(own_entry, second_low)
        - matmul(permuted[0], terms[0])
        - matmul(permuted[0], terms[1])
    )

    @pl.when(large)
    def _():
        bracket[...] -= matmul(permuted[1], terms[0])

    same = (
        jnp.broadcast_to(names[1], (entries, entries))
        == jnp.broadcast_to(names[1], (entries, LANES)).T[0:1, :]
    ).astype(BF16)
    total_high, total_low = split(entry_counts[1])
    totals = matmul(same, total_high) + matmul(same, total_low)
    bracket_high, bracket_low = split(bracket[...])
    centers = matmul(same, bracket_high) + matmul(same, bracket_low)
    centers = centers * (1.0 / jnp.maximum(totals[:, :1], 1.0))
    centers_ref[0], centers_ref[1] = split(centers)
    lane = iota((entries, LANES), 1)
    info = jnp.where(lane == 0, entry_counts[0], entry_counts[1])
    info = jnp.where(lane == 2, cells[0], info)
    entry_info_ref[...] = jnp.where(lane == 3, cells[1], info)

    eye = (iota((LOW, LOW), 0) == iota((LOW, LOW), 1)).astype(BF16)
    for digit in range(high):
        rows = slice(digit * LOW, (digit + 1) * LOW)
        pairs_ref[rows, :] = -matmul_nt(eye, permuted[0, :, rows]).astype(BF16)
    rows_here = vectors.shape[0]
    codes = fine_codes[1:2, :]
    copies = []
    for odd in (1, 0):
        blocks = [at for at in range(groups) if at % 2 == odd]
        for at, block in enumerate(blocks):
            owner = me ^ block
            rows = pl.ds(pl.multiple_of(owner * share_rows, share_rows), share_rows)
            to = slice(at * share_rows, (at + 1) * share_rows)
            own = codes - owner * share_rows
            own = jnp.where((own >= 0) & (own < share_rows), own, -1)
            left[to, :rows_here] = hot(own)[:share_rows]
            left[to, rows_here:] = pairs_ref[rows, :]
        for chunk, (start, cut) in enumerate(zip(starts, cuts)):
            columns = slice(start, start + cut)
            sums = (
                matmul(left[:, :rows_here], vectors[:, columns])
                + matmul(left[:, rows_here:], centers_ref[0, :, columns])
                + matmul(left[:, rows_here:], centers_ref[1, :, columns])
            )
            for part, order_of in enumerate(orders[chunk]):
                if order_of[0] % 2 != odd:
                    continue
                number = 3 * chunk + part
                stage = stages[number]
                for to, block in enumerate(order_of):
                    owner = me ^ block
                    rows = pl.ds(pl.multiple_of(owner * share_rows, share_rows), share_rows)
                    cell_rows = pl.ds(pl.multiple_of(owner * listed, listed), listed)
                    at = blocks.index(block) * share_rows
                    stage[to, :share_rows, :] = sums[at : at + share_rows] + fine[rows, columns]
                    stage[to, share_rows:, :] = bracket[cell_rows, columns]

                @pl.when(large)
                def _():
                    for to, block in enumerate(order_of):
                        owner = me ^ block
                        rows = pl.ds(pl.multiple_of(owner * share_rows, share_rows), share_rows)
                        rest = lax.dot_general(
                            permuted[1, :, rows],
                            centers_ref[0, :, columns],
                            (((0,), (0,)), ((), ())),
                            preferred_element_type=F32,
                        )
                        stage[to, :share_rows, :] -= rest

                copy = pltpu.make_async_copy(stage, out_refs[number], out_sem.at[number])
                copy.start()
                copies.append(copy)
    for copy in copies:
        copy.wait()


def final_kernel(
    groups,
    slot_count,
    share_rows,
    starts,
    me_ref,
    coarse_in,
    fine_share,
    first_sums,
    code_info,
    entry_info,
    *refs,
):
    last_refs, (coarse_out, fine_out, own_first) = refs[: len(starts)], refs[-3:]
    listed = entry_info.shape[0]
    owner_cells = coarse_in.shape[0]
    by_lane = entry_info[...].T
    for device in range(groups):
        rows = slice(device * slot_count, (device + 1) * slot_count)
        own_first[rows, :] = first_sums[device ^ me_ref[0]]
    hits, counts = [], []
    for sweep in range(2):
        cell = by_lane[2 + sweep : 3 + sweep, :].astype(jnp.int32)
        hit = iota((owner_cells, listed), 0) == cell
        counts.append(
            jnp.sum(jnp.where(hit, by_lane[sweep : sweep + 1, :], 0.0), axis=1, keepdims=True)
        )
        hits.append(hit.astype(BF16))
    first_count = code_info[:, 2 * listed : 2 * listed + 1]
    last_count = code_info[:, 2 * listed + 8 : 2 * listed + 9]
    count = jnp.where(last_count > 0, last_count, first_count)
    for start, last_sums in zip(starts, last_refs):
        columns = slice(start, start + last_sums.shape[1])
        coarse = coarse_in[:, columns]
        for sweep, sums in enumerate((own_first[:, columns], last_sums[share_rows:, :])):
            sums_high, sums_low = split(sums)
            found = matmul(hits[sweep], sums_high) + matmul(hits[sweep], sums_low)
            weight = 1.0 / jnp.maximum(counts[sweep], 1.0)
            coarse = jnp.where(counts[sweep] > 0, found * weight, coarse)
        coarse_out[:, columns] = coarse
        fine_out[:, columns] = jnp.where(
            count > 0,
            last_sums[:share_rows, :] * (1.0 / jnp.maximum(count, 1.0)),
            fine_share[:, columns],
        )


def exchange(values, step):
    groups = lax.axis_size("cell")
    return lax.ppermute(values, "cell", [(at, at ^ step) for at in range(groups)])


def block_order(bits):
    order = [0]
    for bit in list(bits)[::-1]:
        order = [block + (1 << bit) for block in order] + order
    return order


def block_orders(bits):
    order = block_order(bits)
    half = len(order) // 2
    return [block + 1 for block in order], order[:half], order[half:]


def after(values, *others):
    return lax.optimization_barrier((values, *others))[0]


def halved(got, other, kept):
    half = other.shape[0]
    return other + got[:half], kept + got[half:]


def swap(blocks, bit):
    half = blocks.shape[0] // 2
    got = exchange(blocks[:half], 1 << bit)
    return jnp.concatenate([blocks[half:], got], axis=1)


def local(kernel, shapes, in_specs, out_specs, scratch, flops, name, aliases=None):
    return pl.pallas_call(
        kernel,
        out_shape=tuple(jax.ShapeDtypeStruct(shape, dtype) for shape, dtype in shapes),
        grid_spec=pltpu.PrefetchScalarGridSpec(
            num_scalar_prefetch=1,
            grid=(1,),
            in_specs=in_specs,
            out_specs=out_specs,
            scratch_shapes=scratch,
        ),
        input_output_aliases=aliases or {},
        compiler_params=PARAMS,
        cost_estimate=pl.CostEstimate(
            flops=int(flops), bytes_accessed=10**6, transcendentals=0
        ),
        name=name,
    )


def block(shape, *place):
    return pl.BlockSpec(
        shape, lambda step, me: tuple(me[0] if at is None else at for at in place)
    )


def dense_plan(vectors, row_slot, fine_codes, cell_list, coarse_in, fine_in):
    groups = lax.axis_size("cell")
    rows_here, feature = vectors.shape
    listed = cell_list.shape[1]
    slot_count = listed // groups
    owner_cells = coarse_in.shape[0]
    codewords = fine_in.shape[0]
    share_rows = codewords // groups
    entries = groups * listed
    half = rows_here // 2
    me = lax.axis_index("cell").reshape(1).astype(jnp.int32)

    packed = local(
        lambda me_ref, *refs: pack_kernel(*refs),
        [((8, half + LANES), jnp.int32)],
        [VMEM] * 3,
        [VMEM],
        [],
        1e9,
        "pack",
    )(me, fine_codes, row_slot, cell_list)[0]
    first, second, first_to = local(
        lambda *refs: own_cells_kernel(groups, listed, *refs),
        [((listed, feature), F32)] * 2 + [((groups, 1, slot_count, feature), F32)],
        [VMEM] * 4,
        [VMEM] * 3,
        [],
        5e9,
        "own_cells",
    )(me, vectors, fine_codes, row_slot, fine_in)
    far = groups // 4
    gathered = jnp.stack([packed] + [exchange(packed, 4 * step) for step in range(1, far)])
    sums = []
    for step, base in ((2, 0), (1, codewords // 2)):
        sums += local(
            lambda me_ref, *refs, base=base: own_codes_kernel(base, *refs),
            [((codewords // 2, feature), F32)],
            [VMEM, VMEM, ANY],
            [VMEM],
            [],
            6e9,
            "own_codes",
        )(me, vectors, fine_codes, gathered)
        if step == 2:
            first_to = swap(after(first_to, gathered), 0)
        gathered = jnp.concatenate([gathered, exchange(gathered, step)])

    top = groups.bit_length() - 1
    near_first = list(range(1, top))
    far_first = near_first[1:] + near_first[:1]
    cuts = [feature // 3] * 3
    bits = [near_first, far_first, near_first]
    starts = [feature - cuts[0], cuts[0], 0]
    orders = [block_orders(each) for each in bits]
    shapes = [
        (len(order), share_rows + listed, cut)
        for cut, three in zip(cuts, orders)
        for order in three
    ]
    *terms, code_info, entry_info = local(
        lambda *refs: sums_kernel(
            groups, slot_count, owner_cells, cuts, starts, orders, *refs
        ),
        [(shape, F32) for shape in shapes]
        + [((codewords, LANES), F32), ((entries, LANES), F32)],
        [VMEM, ANY, VMEM] + [ANY] * 2 + [VMEM] * 2 + [block((share_rows, feature), None, 0), ANY],
        [ANY] * len(shapes) + [VMEM] * 2,
        [
            pltpu.VMEM((entries, codewords), F32),
            pltpu.VMEM((entries, codewords), F32),
            pltpu.VMEM((listed, listed), jnp.int32),
            pltpu.VMEM((listed, listed), jnp.int32),
            pltpu.VMEM((LANES, codewords), F32),
            pltpu.VMEM((2, codewords, feature), BF16),
            pltpu.VMEM((2, entries, codewords), BF16),
            pltpu.VMEM((LOW, rows_here), BF16),
            pltpu.VMEM((codewords, feature), F32),
            pltpu.VMEM((entries, feature), F32),
            pltpu.VMEM((2, entries, feature), BF16),
            pltpu.VMEM((codewords, entries), BF16),
            pltpu.VMEM((codewords // 2, rows_here + entries), BF16),
            pltpu.SemaphoreType.DMA((3,)),
            pltpu.SemaphoreType.DMA((len(shapes),)),
            pltpu.VMEM(vectors.shape, BF16),
        ]
        + [pltpu.VMEM(shape, F32) for shape in shapes],
        40e9,
        "sums",
    )(me, gathered, vectors, fine_codes, *sums, first, second, fine_in, first_to)

    first_to = swap(after(first_to, terms[0]), 1)
    finished = []
    for at, steps in enumerate(bits):
        away, other, kept = terms[3 * at : 3 * at + 3]
        other, kept = halved(exchange(away, 1), other, kept)
        if at == len(bits) - 1:
            first_to = after(first_to, other)[::-1]
            first_to = jnp.concatenate(
                [first_to[0]] + [exchange(first_to[z], 4 * z) for z in range(1, far)]
            )
        for bit in steps[:-1]:
            got = exchange(other, 1 << bit)
            half = got.shape[0] // 2
            other, kept = halved(got, kept[:half], kept[half:])
        finished.append((kept + exchange(other, 1 << steps[-1]))[0])
    outs = ()
    for chunks, width in ((range(1, len(cuts)), feature), ((0,), cuts[0])):
        place = feature // width - 1
        outs = local(
            lambda *refs, chunks=chunks, width=width, place=place: final_kernel(
                groups,
                slot_count,
                share_rows,
                [starts[at] - place * width for at in chunks],
                *refs,
            ),
            [(coarse_in.shape, F32), ((share_rows, feature), F32)],
            [
                block((owner_cells, width), 0, place),
                block((share_rows, width), None, place),
                block((groups, slot_count, width), 0, 0, place),
                block((share_rows, LANES), None, 0),
                block((listed, LANES), None, 0),
            ]
            + [VMEM] * len(chunks)
            + [ANY] * len(outs),
            [block((owner_cells, width), 0, place), block((share_rows, width), 0, place)],
            [pltpu.VMEM((listed, width), F32)],
            1e9,
            "outputs",
            {6 + len(chunks) + number: number for number in range(len(outs))},
        )(
            me,
            coarse_in,
            fine_in,
            first_to,
            code_info,
            entry_info,
            *(finished[at] for at in chunks),
            *outs,
        )
    return tuple(outs)


def fits_dense(mesh_groups, listed, codewords, rows_here, feature):
    entries = mesh_groups * listed
    power = mesh_groups & (mesh_groups - 1) == 0 and mesh_groups >= 4
    digits = codewords % (2 * LOW) == 0 and (codewords // LOW) * listed <= LOW
    shapes = rows_here % (2 * LANES) == 0 and feature % (6 * LANES) == 0
    return power and digits and shapes and entries * codewords <= 2**20


def per_device(vectors, row_slot, fine_codes, cell_list, coarse_in, fine_in):
    groups = lax.axis_size("cell")
    dense = fits_dense(groups, cell_list.shape[1], *fine_in.shape[:1], *vectors.shape)
    plan = dense_plan if dense else routed_plan
    return plan(vectors, row_slot, fine_codes, cell_list, coarse_in, fine_in)


def solution(mesh):
    return jax.shard_map(
        per_device,
        mesh=mesh,
        in_specs=(
            P(("parts", "cell"), None),
            P(None, ("parts", "cell")),
            P(None, ("parts", "cell")),
            P(None, ("parts", "cell")),
            P("cell", None),
            P(),
        ),
        out_specs=(P(("parts", "cell"), None), P(("parts", "cell"), None)),
        check_vma=False,
    )
```

```python
import jax
import jax.numpy as jnp
from jax import lax
from jax.experimental import pallas as pl
from jax.experimental.pallas import tpu as pltpu
from jax.sharding import PartitionSpec as P


def code_tally(code_rows, codewords):
    return jax.ops.segment_sum(
        jnp.ones(code_rows.shape, jnp.float32), code_rows, num_segments=codewords
    )


def fine_update(code_term, totals_share, old_share, share_rows):
    part_sums = lax.psum_scatter(
        code_term(jnp.int32(0), lax.axis_size("cell") * share_rows),
        "cell",
        scatter_dimension=0,
        tiled=True,
    )
    return jnp.where(
        totals_share[:, None] > 0, part_sums / jnp.maximum(totals_share, 1.0)[:, None], old_share
    )


def routed_plan(vectors, row_slot, fine_codes, cell_list, coarse_in, fine_in):
    groups = lax.axis_size("cell")
    rows_here, feature = vectors.shape
    listed = cell_list.shape[1]
    slot_count = listed // groups
    owner_cells = coarse_in.shape[0]
    codewords = fine_in.shape[0]
    share_rows = codewords // groups
    share_start = lax.axis_index("cell") * share_rows
    fine_book = fine_in
    fine_share = lax.dynamic_slice_in_dim(fine_in, share_start, share_rows, 0)
    coarse = coarse_in
    list_iota = lax.iota(jnp.int32, listed)
    for sweep in range(2):
        code_totals = lax.psum(code_tally(fine_codes[sweep], codewords), "cell")
        slot_rows = row_slot[sweep]
        code_rows = fine_codes[sweep]
        picked = jnp.take(fine_book, code_rows, axis=0)
        residual = (vectors.astype(jnp.float32) - picked).astype(jnp.bfloat16)
        slot_hot = (slot_rows[None, :] == list_iota[:, None]).astype(jnp.bfloat16)
        slot_sums = jnp.dot(slot_hot, residual, preferred_element_type=jnp.float32)
        slot_counts = jnp.sum(slot_hot, axis=1, dtype=jnp.float32)
        slot_cells = cell_list[sweep].astype(jnp.float32)
        got_sums, got_counts, got_cells = (
            lax.all_to_all(
                slot_sums.reshape(groups, slot_count, feature),
                "cell",
                split_axis=0,
                concat_axis=0,
                tiled=True,
            ),
            lax.all_to_all(
                slot_counts.reshape(groups, slot_count),
                "cell",
                split_axis=0,
                concat_axis=0,
                tiled=True,
            ),
            lax.all_to_all(
                slot_cells.reshape(groups, slot_count),
                "cell",
                split_axis=0,
                concat_axis=0,
                tiled=True,
            ),
        )
        flat_cells = got_cells.reshape(groups * slot_count).astype(jnp.int32)
        cell_sums = jax.ops.segment_sum(
            got_sums.reshape(groups * slot_count, feature), flat_cells, num_segments=owner_cells
        )
        cell_counts = jax.ops.segment_sum(
            got_counts.reshape(groups * slot_count), flat_cells, num_segments=owner_cells
        )
        coarse = jnp.where(
            cell_counts[:, None] > 0, cell_sums / jnp.maximum(cell_counts, 1.0)[:, None], coarse
        )
        returned_rows = jnp.take(coarse, flat_cells, axis=0).reshape(groups, slot_count, feature)
        arrived = lax.all_to_all(returned_rows, "cell", split_axis=0, concat_axis=0, tiled=True)
        entry_centers = arrived.reshape(listed, feature)
        row_centers = jnp.take(entry_centers, slot_rows, axis=0)
        fine_residual = (vectors.astype(jnp.float32) - row_centers).astype(jnp.bfloat16)

        def code_term(start, count, code_rows=code_rows, fine_residual=fine_residual):
            wanted = start + lax.iota(jnp.int32, count)
            code_hot = (code_rows[None, :] == wanted[:, None]).astype(jnp.bfloat16)
            return jnp.dot(code_hot, fine_residual, preferred_element_type=jnp.float32)

        totals_share = lax.dynamic_slice_in_dim(code_totals, share_start, share_rows, 0)
        if sweep == 0:
            full_sums = lax.psum(code_term(0, codewords), "cell")
            fine_book = jnp.where(
                code_totals[:, None] > 0,
                full_sums / jnp.maximum(code_totals, 1.0)[:, None],
                fine_book,
            )
            fine_share = lax.dynamic_slice_in_dim(fine_book, share_start, share_rows, 0)
        else:
            fine_share = fine_update(code_term, totals_share, fine_share, share_rows)
    return (coarse, fine_share)


F32 = jnp.float32
BF16 = jnp.bfloat16
LOW = 256
LANES = 128
PARAMS = pltpu.CompilerParams(vmem_limit_bytes=58 * 2**20)
VMEM = pl.BlockSpec(memory_space=pltpu.VMEM)
SMEM = pl.BlockSpec(memory_space=pltpu.SMEM)
ANY = pl.BlockSpec(memory_space=pl.ANY)


def iota(shape, axis):
    return lax.broadcasted_iota(jnp.int32, shape, axis)


def matmul(left, right):
    return jnp.dot(left, right, preferred_element_type=F32)


def matmul_nt(left, right):
    return lax.dot_general(left, right, (((1,), (1,)), ((), ())), preferred_element_type=F32)


def split(values):
    high = values.astype(BF16)
    return high, (values - high.astype(F32)).astype(BF16)


def hot_rows(codes, rows=LOW):
    inside = jnp.where((codes >= 0) & (codes < rows), codes, -1)
    inside = inside.astype(F32).astype(BF16)
    row = iota((rows, codes.shape[1]), 0).astype(F32).astype(BF16)
    return jnp.where(row == inside, jnp.ones((), BF16), jnp.zeros((), BF16))


def pair_block(codes, slots, listed, high):
    left = hot_rows((codes >> 8) * listed + slots, high * listed)
    return matmul_nt(left, hot_rows(codes & (LOW - 1)))


def pack_kernel(fine_codes, row_slot, cell_list, packed):
    half = fine_codes.shape[1] // 2
    listed = cell_list.shape[1]
    packed[:, half:] = jnp.zeros((8, LANES), jnp.int32)
    for number, ref in enumerate((fine_codes, row_slot)):
        for sweep in range(2):
            for part in range(2):
                row = 4 * number + 2 * sweep + part
                packed[row : row + 1, :half] = ref[
                    sweep : sweep + 1, part * half : (part + 1) * half
                ]
    packed[0:2, half : half + listed] = cell_list[...]


def own_cells_kernel(
    groups, listed, me_ref, vectors, fine_codes, row_slot, fine_in, first_ref, second_ref, to_ref
):
    high = fine_in.shape[0] // LOW
    first = matmul(hot_rows(row_slot[0:1, :], listed), vectors[...])
    second_ref[...] = matmul(hot_rows(row_slot[1:2, :], listed), vectors[...])
    pairs = pair_block(fine_codes[0:1, :], row_slot[0:1, :], listed, high)
    for digit in range(high):
        pairs_high, pairs_low = split(pairs[digit * listed : (digit + 1) * listed])
        both = jnp.concatenate([pairs_high, pairs_low], axis=0)
        book = fine_in[digit * LOW : (digit + 1) * LOW, :]
        book_high, book_low = split(book)
        taken = matmul(both, book_high) + matmul(both, book_low)
        first = first - taken[:listed] - taken[listed:]
    first_ref[...] = first
    slots = listed // groups
    top = groups.bit_length() - 1
    for owner in range(groups):
        block = owner ^ me_ref[0]
        at = sum((1 - (block >> bit & 1)) << (top - 1 - bit) for bit in range(2))
        at = at + groups // 4 - 1 - (block >> 2)
        to_ref[at, 0] = first[owner * slots : (owner + 1) * slots]


def own_codes_kernel(base, vectors, fine_codes, _, sums_ref):
    codes = fine_codes[0:1, :] - base
    for start in range(0, sums_ref.shape[0], 2 * LOW):
        hot = jnp.concatenate(
            [hot_rows(codes - start), hot_rows(codes - start - LOW)], axis=0
        )
        sums_ref[start : start + 2 * LOW, :] = matmul(hot, vectors[...])


def position(block, groups):
    return (block & 1) * (groups // 2) + (block >> 1 & 1) * (groups // 4) + (block >> 2)


def sums_kernel(
    groups,
    slot_count,
    owner_cells,
    cuts,
    starts,
    orders,
    me_ref,
    codes_ref,
    vectors_ref,
    fine_codes,
    low_sums_ref,
    high_sums_ref,
    first_ref,
    second_ref,
    share_ref,
    _,
    *refs,
):
    out_refs, refs = refs[: 3 * len(cuts)], refs[3 * len(cuts) :]
    code_info_ref, entry_info_ref, refs = refs[0], refs[1], refs[2:]
    table0, table1, cell0, cell1, wide, terms, permuted, rows_hot = refs[:8]
    fine, bracket, centers_ref, pairs_ref, left = refs[8:13]
    in_sem, out_sem, vectors, stages = refs[13], refs[14], refs[15], refs[16:]
    me = me_ref[0]
    codewords, feature = fine.shape
    listed = groups * slot_count
    entries = groups * listed
    high = codewords // LOW
    half = codes_ref.shape[2] - LANES
    share_rows = share_ref.shape[0]

    loads = [
        pltpu.make_async_copy(
            ref, fine.at[pl.ds(at * (codewords // 2), codewords // 2)], in_sem.at[at]
        )
        for at, ref in enumerate((low_sums_ref, high_sums_ref))
    ]
    loads.append(pltpu.make_async_copy(vectors_ref, vectors, in_sem.at[2]))
    for load in loads:
        load.start()

    rows_hot[...] = iota(rows_hot.shape, 0).astype(F32).astype(BF16)
    one, zero = jnp.ones((), BF16), jnp.zeros((), BF16)

    def hot(codes):
        rows = rows_hot[:, : codes.shape[1]]
        return jnp.where(rows == codes.astype(F32).astype(BF16), one, zero)

    def device_tables(device, carry):
        at = position(device ^ me, groups)
        for sweep, table in enumerate((table0, table1)):
            block = jnp.zeros((high * listed, LOW), F32)
            for part in range(2):
                row = 2 * sweep + part
                codes = codes_ref[at, row : row + 1, :half]
                slots = codes_ref[at, row + 4 : row + 5, :half]
                block = block + matmul_nt(
                    hot((codes >> 8) * listed + slots)[: high * listed], hot(codes & (LOW - 1))
                )
            rows = pl.ds(pl.multiple_of(device * listed, listed), listed)
            for digit in range(high):
                table[rows, digit * LOW : (digit + 1) * LOW] = block[
                    digit * listed : (digit + 1) * listed
                ]
        return carry

    lax.fori_loop(0, groups, device_tables, 0)
    for device in range(groups):
        at = position(device ^ me, groups)
        for sweep, cell in enumerate((cell0, cell1)):
            row = codes_ref[at, sweep : sweep + 1, half : half + listed]
            cell[device * slot_count : (device + 1) * slot_count, :] = jnp.broadcast_to(
                row, (slot_count, listed)
            )

    row_at = iota((entries, listed), 0)
    owner_of = row_at // listed
    slot_of = owner_of * slot_count + row_at % slot_count
    is_slot = slot_of == iota((entries, listed), 1)
    device_of = (row_at // slot_count) % groups

    def entry_cells(cell):
        tiled = jnp.concatenate([cell[...]] * groups, axis=0)
        picked = jnp.sum(jnp.where(is_slot, tiled, 0), axis=1, keepdims=True)
        return picked.astype(F32)

    owner_col = owner_of[:, :1].astype(F32)
    cells = [entry_cells(cell0), entry_cells(cell1)]
    names = [cell + owner_col * float(owner_cells) for cell in cells]

    entry_row = iota((entries, entries), 0)
    natural = (
        ((entry_row // slot_count) % groups) * listed
        + (entry_row // listed) * slot_count
        + entry_row % slot_count
    )
    order = (natural == iota((entries, entries), 1)).astype(BF16)
    code_counts = [jnp.sum(table[...], axis=0, keepdims=True) for table in (table0, table1)]
    entry_counts, most = [], 0.0
    for sweep, table in enumerate((table0, table1)):
        entry_count = jnp.sum(table[...], axis=1, keepdims=True)
        most = jnp.maximum(
            most, jnp.minimum(jnp.max(entry_count), jnp.max(code_counts[sweep]))
        )
        count_high, count_low = split(jnp.broadcast_to(entry_count, (entries, LANES)))
        entry_counts.append(matmul(order, count_high) + matmul(order, count_low))
    large = most > LOW
    for digit in range(high):
        columns = slice(digit * LOW, (digit + 1) * LOW)
        permuted[0, :, columns] = matmul(order, table1[:, columns].astype(BF16)).astype(BF16)

    @pl.when(large)
    def _():
        for digit in range(high):
            columns = slice(digit * LOW, (digit + 1) * LOW)
            rest = split(table1[:, columns])[1]
            permuted[1, :, columns] = matmul(order, rest).astype(BF16)

    own_row = codes_ref[0, 0:1, half : half + listed].astype(F32)
    own_row = own_row + (iota((1, listed), 1) // slot_count).astype(F32) * float(owner_cells)
    match = (names[0] == own_row).astype(BF16)
    match = lax.dot_general(match, order, (((0,), (0,)), ((), ())), preferred_element_type=F32)
    match = match.astype(BF16)
    for digit in range(high):
        columns = slice(digit * LOW, (digit + 1) * LOW)
        wide[0:listed, columns] = matmul(match, table0[:, columns].astype(BF16))

    @pl.when(large)
    def _():
        for digit in range(high):
            columns = slice(digit * LOW, (digit + 1) * LOW)
            wide[0:listed, columns] += matmul(match, split(table0[:, columns])[1])

    held = jnp.sum(wide[0:listed, :], axis=1, keepdims=True)
    used_high, used_low = split(wide[0:listed, :])
    wide[0:listed, :] = used_high.astype(F32)
    wide[listed : 2 * listed, :] = used_low.astype(F32)
    wide[2 * listed : 2 * listed + 8, :] = jnp.broadcast_to(code_counts[0], (8, codewords))
    wide[2 * listed + 8 : 2 * listed + 16, :] = jnp.broadcast_to(code_counts[1], (8, codewords))
    wide[2 * listed + 16 :, :] = jnp.zeros((LANES - 2 * listed - 16, codewords), F32)
    center_high, center_low = split(first_ref[...] / jnp.maximum(held, 1.0))
    blank = jnp.zeros((LANES - 2 * listed, feature), BF16)
    center_high = jnp.concatenate([center_high, center_high, blank], axis=0)
    center_low = jnp.concatenate([center_low, center_low, blank], axis=0)
    for load in loads:
        load.wait()
    for digit in range(high):
        rows = slice(digit * LOW, (digit + 1) * LOW)
        columns = wide[:, rows].T
        code_info_ref[rows, :] = columns
        taken = jnp.where(iota((LOW, LANES), 1) < 2 * listed, columns, 0.0).astype(BF16)
        first_fine = fine[rows, :] - (matmul(taken, center_high) + matmul(taken, center_low))
        scaled = first_fine * (1.0 / jnp.maximum(columns[:, 2 * listed : 2 * listed + 1], 1.0))
        terms[0, rows, :], terms[1, rows, :] = split(scaled)
        fine[rows, :] = jnp.where(
            columns[:, 2 * listed + 8 : 2 * listed + 9] > 0, 0.0, first_fine
        )
    mine = pl.ds(pl.multiple_of(me * share_rows, share_rows), share_rows)
    empty = code_info_ref[mine, 2 * listed : 2 * listed + 1] == 0
    for part, share in enumerate(split(share_ref[...])):
        terms[part, mine, :] = jnp.where(
            empty, share.astype(F32), terms[part, mine, :].astype(F32)
        ).astype(BF16)

    own_entry = (is_slot & (device_of == me)).astype(BF16)
    second_high, second_low = split(second_ref[...])
    bracket[...] = (
        matmul(own_entry, second_high)
        + matmul(own_entry, second_low)
        - matmul(permuted[0], terms[0])
        - matmul(permuted[0], terms[1])
    )

    @pl.when(large)
    def _():
        bracket[...] -= matmul(permuted[1], terms[0])

    same = (
        jnp.broadcast_to(names[1], (entries, entries))
        == jnp.broadcast_to(names[1], (entries, LANES)).T[0:1, :]
    ).astype(BF16)
    total_high, total_low = split(entry_counts[1])
    totals = matmul(same, total_high) + matmul(same, total_low)
    bracket_high, bracket_low = split(bracket[...])
    centers = matmul(same, bracket_high) + matmul(same, bracket_low)
    centers = centers * (1.0 / jnp.maximum(totals[:, :1], 1.0))
    centers_ref[0], centers_ref[1] = split(centers)
    lane = iota((entries, LANES), 1)
    info = jnp.where(lane == 0, entry_counts[0], entry_counts[1])
    info = jnp.where(lane == 2, cells[0], info)
    entry_info_ref[...] = jnp.where(lane == 3, cells[1], info)

    eye = (iota((LOW, LOW), 0) == iota((LOW, LOW), 1)).astype(BF16)
    for digit in range(high):
        rows = slice(digit * LOW, (digit + 1) * LOW)
        pairs_ref[rows, :] = -matmul_nt(eye, permuted[0, :, rows]).astype(BF16)
    rows_here = vectors.shape[0]
    codes = fine_codes[1:2, :]
    copies = []
    for odd in (1, 0):
        blocks = [at for at in range(groups) if at % 2 == odd]
        for at, block in enumerate(blocks):
            owner = me ^ block
            rows = pl.ds(pl.multiple_of(owner * share_rows, share_rows), share_rows)
            to = slice(at * share_rows, (at + 1) * share_rows)
            own = codes - owner * share_rows
            own = jnp.where((own >= 0) & (own < share_rows), own, -1)
            left[to, :rows_here] = hot(own)[:share_rows]
            left[to, rows_here:] = pairs_ref[rows, :]
        for chunk, (start, cut) in enumerate(zip(starts, cuts)):
            columns = slice(start, start + cut)
            sums = (
                matmul(left[:, :rows_here], vectors[:, columns])
                + matmul(left[:, rows_here:], centers_ref[0, :, columns])
                + matmul(left[:, rows_here:], centers_ref[1, :, columns])
            )
            for part, order_of in enumerate(orders[chunk]):
                if order_of[0] % 2 != odd:
                    continue
                number = 3 * chunk + part
                stage = stages[number]
                for to, block in enumerate(order_of):
                    owner = me ^ block
                    rows = pl.ds(pl.multiple_of(owner * share_rows, share_rows), share_rows)
                    cell_rows = pl.ds(pl.multiple_of(owner * listed, listed), listed)
                    at = blocks.index(block) * share_rows
                    stage[to, :share_rows, :] = sums[at : at + share_rows] + fine[rows, columns]
                    stage[to, share_rows:, :] = bracket[cell_rows, columns]

                @pl.when(large)
                def _():
                    for to, block in enumerate(order_of):
                        owner = me ^ block
                        rows = pl.ds(pl.multiple_of(owner * share_rows, share_rows), share_rows)
                        rest = lax.dot_general(
                            permuted[1, :, rows],
                            centers_ref[0, :, columns],
                            (((0,), (0,)), ((), ())),
                            preferred_element_type=F32,
                        )
                        stage[to, :share_rows, :] -= rest

                copy = pltpu.make_async_copy(stage, out_refs[number], out_sem.at[number])
                copy.start()
                copies.append(copy)
    for copy in copies:
        copy.wait()


def final_kernel(
    groups,
    slot_count,
    share_rows,
    starts,
    me_ref,
    coarse_in,
    fine_share,
    first_sums,
    code_info,
    entry_info,
    *refs,
):
    last_refs, (coarse_out, fine_out, own_first) = refs[: len(starts)], refs[-3:]
    listed = entry_info.shape[0]
    owner_cells = coarse_in.shape[0]
    by_lane = entry_info[...].T
    for device in range(groups):
        rows = slice(device * slot_count, (device + 1) * slot_count)
        own_first[rows, :] = first_sums[device ^ me_ref[0]]
    hits, counts = [], []
    for sweep in range(2):
        cell = by_lane[2 + sweep : 3 + sweep, :].astype(jnp.int32)
        hit = iota((owner_cells, listed), 0) == cell
        counts.append(
            jnp.sum(jnp.where(hit, by_lane[sweep : sweep + 1, :], 0.0), axis=1, keepdims=True)
        )
        hits.append(hit.astype(BF16))
    first_count = code_info[:, 2 * listed : 2 * listed + 1]
    last_count = code_info[:, 2 * listed + 8 : 2 * listed + 9]
    count = jnp.where(last_count > 0, last_count, first_count)
    for start, last_sums in zip(starts, last_refs):
        columns = slice(start, start + last_sums.shape[1])
        coarse = coarse_in[:, columns]
        for sweep, sums in enumerate((own_first[:, columns], last_sums[share_rows:, :])):
            sums_high, sums_low = split(sums)
            found = matmul(hits[sweep], sums_high) + matmul(hits[sweep], sums_low)
            weight = 1.0 / jnp.maximum(counts[sweep], 1.0)
            coarse = jnp.where(counts[sweep] > 0, found * weight, coarse)
        coarse_out[:, columns] = coarse
        fine_out[:, columns] = jnp.where(
            count > 0,
            last_sums[:share_rows, :] * (1.0 / jnp.maximum(count, 1.0)),
            fine_share[:, columns],
        )


def exchange(values, step):
    groups = lax.axis_size("cell")
    return lax.ppermute(values, "cell", [(at, at ^ step) for at in range(groups)])


def block_order(bits):
    order = [0]
    for bit in list(bits)[::-1]:
        order = [block + (1 << bit) for block in order] + order
    return order


def block_orders(bits):
    order = block_order(bits)
    half = len(order) // 2
    return [block + 1 for block in order], order[:half], order[half:]


def after(values, *others):
    return lax.optimization_barrier((values, *others))[0]


def halved(got, other, kept):
    half = other.shape[0]
    return other + got[:half], kept + got[half:]


def swap(blocks, bit):
    half = blocks.shape[0] // 2
    got = exchange(blocks[:half], 1 << bit)
    return jnp.concatenate([blocks[half:], got], axis=1)


def local(kernel, shapes, in_specs, out_specs, scratch, flops, name, aliases=None):
    return pl.pallas_call(
        kernel,
        out_shape=tuple(jax.ShapeDtypeStruct(shape, dtype) for shape, dtype in shapes),
        grid_spec=pltpu.PrefetchScalarGridSpec(
            num_scalar_prefetch=1,
            grid=(1,),
            in_specs=in_specs,
            out_specs=out_specs,
            scratch_shapes=scratch,
        ),
        input_output_aliases=aliases or {},
        compiler_params=PARAMS,
        cost_estimate=pl.CostEstimate(
            flops=int(flops), bytes_accessed=10**6, transcendentals=0
        ),
        name=name,
    )


def block(shape, *place):
    return pl.BlockSpec(
        shape, lambda step, me: tuple(me[0] if at is None else at for at in place)
    )


def dense_plan(vectors, row_slot, fine_codes, cell_list, coarse_in, fine_in):
    groups = lax.axis_size("cell")
    rows_here, feature = vectors.shape
    listed = cell_list.shape[1]
    slot_count = listed // groups
    owner_cells = coarse_in.shape[0]
    codewords = fine_in.shape[0]
    share_rows = codewords // groups
    entries = groups * listed
    half = rows_here // 2
    me = lax.axis_index("cell").reshape(1).astype(jnp.int32)

    packed = local(
        lambda me_ref, *refs: pack_kernel(*refs),
        [((8, half + LANES), jnp.int32)],
        [VMEM] * 3,
        [VMEM],
        [],
        1e9,
        "pack",
    )(me, fine_codes, row_slot, cell_list)[0]
    first, second, first_to = local(
        lambda *refs: own_cells_kernel(groups, listed, *refs),
        [((listed, feature), F32)] * 2 + [((groups, 1, slot_count, feature), F32)],
        [VMEM] * 4,
        [VMEM] * 3,
        [],
        5e9,
        "own_cells",
    )(me, vectors, fine_codes, row_slot, fine_in)
    far = groups // 4
    gathered = jnp.stack([packed] + [exchange(packed, 4 * step) for step in range(1, far)])
    sums = []
    for step, base in ((2, 0), (1, codewords // 2)):
        sums += local(
            lambda me_ref, *refs, base=base: own_codes_kernel(base, *refs),
            [((codewords // 2, feature), F32)],
            [VMEM, VMEM, ANY],
            [VMEM],
            [],
            6e9,
            "own_codes",
        )(me, vectors, fine_codes, gathered)
        first_to = swap(after(first_to, gathered), 2 - step)
        gathered = jnp.concatenate([gathered, exchange(gathered, step)])

    top = groups.bit_length() - 1
    near_first = list(range(1, top))
    far_first = near_first[1:] + near_first[:1]
    cuts = [feature // 3] * 3
    bits = [near_first, far_first, near_first]
    starts = [feature - cuts[0], cuts[0], 0]
    orders = [block_orders(each) for each in bits]
    shapes = [
        (len(order), share_rows + listed, cut)
        for cut, three in zip(cuts, orders)
        for order in three
    ]
    *terms, code_info, entry_info = local(
        lambda *refs: sums_kernel(
            groups, slot_count, owner_cells, cuts, starts, orders, *refs
        ),
        [(shape, F32) for shape in shapes]
        + [((codewords, LANES), F32), ((entries, LANES), F32)],
        [VMEM, ANY, VMEM] + [ANY] * 2 + [VMEM] * 2 + [block((share_rows, feature), None, 0), ANY],
        [ANY] * len(shapes) + [VMEM] * 2,
        [
            pltpu.VMEM((entries, codewords), F32),
            pltpu.VMEM((entries, codewords), F32),
            pltpu.VMEM((listed, listed), jnp.int32),
            pltpu.VMEM((listed, listed), jnp.int32),
            pltpu.VMEM((LANES, codewords), F32),
            pltpu.VMEM((2, codewords, feature), BF16),
            pltpu.VMEM((2, entries, codewords), BF16),
            pltpu.VMEM((LOW, rows_here), BF16),
            pltpu.VMEM((codewords, feature), F32),
            pltpu.VMEM((entries, feature), F32),
            pltpu.VMEM((2, entries, feature), BF16),
            pltpu.VMEM((codewords, entries), BF16),
            pltpu.VMEM((codewords // 2, rows_here + entries), BF16),
            pltpu.SemaphoreType.DMA((3,)),
            pltpu.SemaphoreType.DMA((len(shapes),)),
            pltpu.VMEM(vectors.shape, BF16),
        ]
        + [pltpu.VMEM(shape, F32) for shape in shapes],
        40e9,
        "sums",
    )(me, gathered, vectors, fine_codes, *sums, first, second, fine_in, first_to)

    finished = []
    for at, steps in enumerate(bits):
        away, other, kept = terms[3 * at : 3 * at + 3]
        other, kept = halved(exchange(away, 1), other, kept)
        if at == 0:
            first_to = after(first_to, other)[::-1]
            first_to = jnp.concatenate(
                [first_to[0]] + [exchange(first_to[z], 4 * z) for z in range(1, far)]
            )
        for bit in steps[:-1]:
            got = exchange(other, 1 << bit)
            half = got.shape[0] // 2
            other, kept = halved(got, kept[:half], kept[half:])
            if at == 0 and bit == steps[0]:
                other, first_to = lax.optimization_barrier((other, first_to))
        finished.append((kept + exchange(other, 1 << steps[-1]))[0])
    outs = ()
    for chunks, width in ((range(1, len(cuts)), feature), ((0,), cuts[0])):
        place = feature // width - 1
        outs = local(
            lambda *refs, chunks=chunks, width=width, place=place: final_kernel(
                groups,
                slot_count,
                share_rows,
                [starts[at] - place * width for at in chunks],
                *refs,
            ),
            [(coarse_in.shape, F32), ((share_rows, feature), F32)],
            [
                block((owner_cells, width), 0, place),
                block((share_rows, width), None, place),
                block((groups, slot_count, width), 0, 0, place),
                block((share_rows, LANES), None, 0),
                block((listed, LANES), None, 0),
            ]
            + [VMEM] * len(chunks)
            + [ANY] * len(outs),
            [block((owner_cells, width), 0, place), block((share_rows, width), 0, place)],
            [pltpu.VMEM((listed, width), F32)],
            1e9,
            "outputs",
            {6 + len(chunks) + number: number for number in range(len(outs))},
        )(
            me,
            coarse_in,
            fine_in,
            first_to,
            code_info,
            entry_info,
            *(finished[at] for at in chunks),
            *outs,
        )
    return tuple(outs)


def fits_dense(mesh_groups, listed, codewords, rows_here, feature):
    entries = mesh_groups * listed
    power = mesh_groups & (mesh_groups - 1) == 0 and mesh_groups >= 4
    digits = codewords % (2 * LOW) == 0 and (codewords // LOW) * listed <= LOW
    shapes = rows_here % (2 * LANES) == 0 and feature % (6 * LANES) == 0
    return power and digits and shapes and entries * codewords <= 2**20


def per_device(vectors, row_slot, fine_codes, cell_list, coarse_in, fine_in):
    groups = lax.axis_size("cell")
    dense = fits_dense(groups, cell_list.shape[1], *fine_in.shape[:1], *vectors.shape)
    plan = dense_plan if dense else routed_plan
    return plan(vectors, row_slot, fine_codes, cell_list, coarse_in, fine_in)


def solution(mesh):
    return jax.shard_map(
        per_device,
        mesh=mesh,
        in_specs=(
            P(("parts", "cell"), None),
            P(None, ("parts", "cell")),
            P(None, ("parts", "cell")),
            P(None, ("parts", "cell")),
            P("cell", None),
            P(),
        ),
        out_specs=(P(("parts", "cell"), None), P(("parts", "cell"), None)),
        check_vma=False,
    )
```
